32 devices in a mesh: dp: 8 (over z, y), mp: 4 (over x, core).
Axes of the slice: x: 2, y: 2, z: 4, core: 2. Of those that a mesh axis runs over, the one named last changes fastest.
Arguments:
- tokens: bfloat16 [8192, 768], P(('dp', 'mp')), may hold values from -6 to 6
- memory: bfloat16 [6272, 768], P(('dp', 'mp')), may hold values from -6 to 6
- split_point: int32 [32], P('dp'), may hold values from 0 to 32
- text_length: int32 [32], P('dp'), may hold values from 128 to 256
- patch_mask: int32 [32, 196], P('dp'), may hold values 0 or 1
- query_weight: bfloat16 [768, 768], P('dp', 'mp'), may hold values from -0.21875 to 0.21875
- query_bias: bfloat16 [768], P('mp'), may hold values from -3 to 3
- key_weight: bfloat16 [768, 768], P('dp', 'mp'), may hold values from -0.21875 to 0.21875
- value_weight: bfloat16 [768, 768], P('dp', 'mp'), may hold values from -0.21875 to 0.21875
- value_bias: bfloat16 [768], P('mp'), may hold values from -3 to 3
- out_weight: bfloat16 [768, 768], P('mp', 'dp'), may hold values from -1.75 to 1.75
- out_bias: bfloat16 [768], replicated, may hold values from -2 to 2
- attn_gain: bfloat16 [768], replicated, may hold values from 0.099609375 to 1.8984375
- attn_shift: bfloat16 [768], replicated, may hold values from -2 to 2
- mlp_gain: bfloat16 [768], replicated, may hold values from 0.099609375 to 1.8984375
- mlp_shift: bfloat16 [768], replicated, may hold values from -2 to 2
- up_weight: bfloat16 [768, 3072], P('dp', 'mp'), may hold values from -0.21875 to 0.21875
- up_bias: bfloat16 [3072], P('mp'), may hold values from -3 to 3
- down_weight: bfloat16 [3072, 768], P('mp', 'dp'), may hold values from -0.109375 to 0.109375
- down_bias: bfloat16 [768], replicated, may hold values from -2 to 2
- cotangent: bfloat16 [8192, 768], P(('dp', 'mp')), may hold values from -6 to 6
Outputs:
- layer_out: bfloat16 [8192, 768], P(('dp', 'mp'))
- input_grad: float32 [8192, 768], P(('dp', 'mp'))
- memory_grad: float32 [6272, 768], P(('dp', 'mp'))
- query_weight_grad: float32 [768, 768], P('dp', 'mp')
- key_weight_grad: float32 [768, 768], P('dp', 'mp')
- value_weight_grad: float32 [768, 768], P('dp', 'mp')
- out_weight_grad: float32 [768, 768], P('mp', 'dp')
- up_weight_grad: float32 [768, 3072], P('dp', 'mp')
- down_weight_grad: float32 [3072, 768], P('mp', 'dp')
- query_bias_grad: float32 [768], P(('dp', 'mp'))
- value_bias_grad: float32 [768], P(('dp', 'mp'))
- up_bias_grad: float32 [3072], P(('dp', 'mp'))
- out_bias_grad: float32 [768], P(('dp', 'mp'))
- down_bias_grad: float32 [768], P(('dp', 'mp'))
- attn_gain_grad: float32 [768], P(('dp', 'mp'))
- attn_shift_grad: float32 [768], P(('dp', 'mp'))
- mlp_gain_grad: float32 [768], P(('dp', 'mp'))
- mlp_shift_grad: float32 [768], P(('dp', 'mp'))
The draws below stay inside these ranges and needn't reach their ends.
Inputs may be any that keep to these rules, and one draw needn't show every extreme that they name: `split_point`: never exceeds the same example's text_length.
All inputs are finite; a program needn't handle non-finite values. No bound on the sum of `patch_mask` on one device may be relied on, other than what follows from the above.
Results may differ from the reference program's by a relative error of at most 0.02.
Values may be sent and summed in bfloat16 or wider, within the bound.
No kernel may reach another device: no remote copies, remote signals or barrier semaphores. Data moves between devices by JAX's collectives and lax.ppermute only.
A program may use at most 128 MiB of HBM per device.

```python
import jax
import jax.numpy as jnp
from jax import lax

D = 768
FF = 3072
HEADS = 12
HEAD = 64
TEXT = 256
PATCHES = 196
SEQ_DEV = 4
HD = 768
SEQS = 32
TOKENS = 8192
MEMROWS = 6272
N_DP = 8


def touch_ends(entries, own_key, smallest, largest):
    place = [jax.random.randint(jax.random.fold_in(own_key, axis), (), 0, length) for axis, length in enumerate(entries.shape)]
    widest = entries.shape.index(max(entries.shape))
    next_to = place[:widest] + [(place[widest] + 1) % entries.shape[widest]] + place[widest + 1:]
    return entries.at[tuple(place)].set(smallest).at[tuple(next_to)].set(largest)


def steps_of(rng, shape, pieces, low, high):
    def one(axis_at, shards_of):
        heights = jax.random.uniform(jax.random.fold_in(jax.random.fold_in(rng, 6), axis_at), (shards_of,), jnp.float32, low / len(pieces), high / len(pieces))
        return jnp.repeat(jnp.exp(heights), shape[axis_at] // shards_of).reshape((-1,) + (1,) * (len(shape) - axis_at - 1))

    loudness = one(*pieces[0])
    for cut in pieces[1:]:
        loudness = loudness * one(*cut)
    return loudness


def scatter_about(own_key, shape, scale, most, shards=(), held_as=jnp.bfloat16):
    factor_of = steps_of(own_key, shape, shards, -0.22, 0.18) if shards else 1.0
    drawn = jax.random.normal(own_key, shape, jnp.float32) * scale * factor_of
    return jnp.minimum(jnp.maximum(drawn, -most), most).astype(held_as)


def setup_inputs(seed: int = 0) -> dict:
    streams_of = jax.random.split(jax.random.key(seed), 22)
    return {
        "tokens": scatter_about(streams_of[0], (TOKENS, D), 1.0, 6.0, ((0, 32),)),
        "memory": scatter_about(streams_of[1], (MEMROWS, D), 1.0, 6.0, ((0, 32),)),
        "split_point": touch_ends(jax.random.randint(streams_of[2], (SEQS,), 0, 33), jax.random.fold_in(streams_of[2], 1), 0, 32).astype(jnp.int32),
        "text_length": touch_ends(jax.random.randint(streams_of[3], (SEQS,), TEXT // 2, TEXT + 1), jax.random.fold_in(streams_of[3], 1), TEXT // 2, TEXT).astype(jnp.int32),
        "patch_mask": touch_ends((jax.random.randint(streams_of[4], (SEQS, PATCHES), 0, 8) < 7).astype(jnp.int32), jax.random.fold_in(streams_of[4], 1), 0, 1),
        "query_weight": scatter_about(streams_of[5], (D, HD), D ** -0.5, 0.21875, ((0, 8), (1, 4))),
        "query_bias": scatter_about(streams_of[6], (HD,), 0.5, 3.0, ((0, 4),)),
        "key_weight": scatter_about(streams_of[7], (D, HD), D ** -0.5, 0.21875, ((0, 8), (1, 4))),
        "value_weight": scatter_about(streams_of[8], (D, HD), D ** -0.5, 0.21875, ((0, 8), (1, 4))),
        "value_bias": scatter_about(streams_of[9], (HD,), 0.5, 3.0, ((0, 4),)),
        "out_weight": scatter_about(streams_of[10], (HD, D), (HD // 64) ** -0.5, 1.75, ((0, 4), (1, 8))),
        "out_bias": scatter_about(streams_of[11], (D,), 0.3, 2.0),
        "attn_gain": jnp.clip(1.0 + 0.18 * jax.random.normal(streams_of[12], (D,), jnp.float32), 0.099609375, 1.8984375).astype(jnp.bfloat16),
        "attn_shift": scatter_about(streams_of[13], (D,), 0.3, 2.0),
        "mlp_gain": jnp.clip(1.0 + 0.18 * jax.random.normal(streams_of[14], (D,), jnp.float32), 0.099609375, 1.8984375).astype(jnp.bfloat16),
        "mlp_shift": scatter_about(streams_of[15], (D,), 0.3, 2.0),
        "up_weight": scatter_about(streams_of[16], (D, FF), D ** -0.5, 0.21875, ((0, 8), (1, 4))),
        "up_bias": scatter_about(streams_of[17], (FF,), 0.5, 3.0, ((0, 4),)),
        "down_weight": scatter_about(streams_of[18], (FF, D), FF ** -0.5, 0.109375, ((0, 4), (1, 8))),
        "down_bias": scatter_about(streams_of[19], (D,), 0.3, 2.0),
        "cotangent": scatter_about(streams_of[20], (TOKENS, D), 1.0, 6.0, ((0, 32),)),
    }


@jax.custom_vjp
def low(v):
    return lax.optimization_barrier(v.astype(jnp.bfloat16)).astype(jnp.float32)

@jax.custom_vjp
def low_back(v):
    return v

def low_keep(v):
    return (low(v), None)

def low_pass(kept, grad):
    return (grad,)

def back_keep(v):
    return (v, None)

def back_low(kept, grad):
    return (low(grad),)
low.defvjp(low_keep, low_pass)
low_back.defvjp(back_keep, back_low)
epsilon = 1e-06
neg_fill = -1000000000.0
highest = lax.Precision.HIGHEST

def rounded_both(value):
    return low_back(low(value))

def layer_norm(matrix, gain, shift):
    average = lax.optimization_barrier(jnp.mean(matrix, axis=-1, keepdims=True))
    centered = matrix - average
    return centered * lax.rsqrt(lax.optimization_barrier(jnp.mean(centered * centered, axis=-1, keepdims=True)) + epsilon) * gain + shift

def build_mask(split_block, length_block, patch_block, text_len):
    places = jnp.arange(text_len, dtype=jnp.int32)
    key_place = places[None, None, :]
    query_place = places[None, :, None]
    text_ok = ((key_place < split_block[:, None, None]) | (key_place <= query_place)) & (key_place < length_block[:, None, None])
    patch_ok = jnp.broadcast_to(patch_block[:, None, :] > 0, (patch_block.shape[0], text_len, patch_block.shape[1]))
    return jnp.concatenate([patch_ok, text_ok], axis=2)

def block_layer(text_in, memory_in, params, split_block, length_block, patch_block):
    query_weight, query_bias, key_weight, value_weight, value_bias, out_weight, out_bias, attn_gain, attn_shift, mlp_gain, mlp_shift, up_weight, up_bias, down_weight, down_bias = params
    examples = split_block.shape[0]
    key_span = PATCHES + TEXT
    text_normed = low(layer_norm(text_in, attn_gain, attn_shift))
    memory_normed = low(layer_norm(memory_in, attn_gain, attn_shift))
    queries = rounded_both(jnp.dot(text_normed, query_weight, precision=highest) + query_bias)
    joined = jnp.concatenate([memory_normed.reshape(examples, PATCHES, D), text_normed.reshape(examples, TEXT, D)], axis=1)
    key_rows = rounded_both(jnp.einsum('gsd,df->gsf', joined, key_weight, precision=highest))
    value_rows = rounded_both(jnp.einsum('gsd,df->gsf', joined, value_weight, precision=highest) + value_bias)
    query_heads = queries.reshape(examples, TEXT, HEADS, HEAD)
    key_heads = key_rows.reshape(examples, key_span, HEADS, HEAD)
    value_heads = value_rows.reshape(examples, key_span, HEADS, HEAD)
    scores = low_back(jnp.einsum('glhe,gshe->ghls', query_heads, key_heads, precision=highest) * HEAD ** (-0.5))
    allowed = build_mask(split_block, length_block, patch_block, TEXT)
    scores = jnp.where(allowed[:, None], scores, neg_fill)
    probs = jax.nn.softmax(scores, axis=-1)
    context = rounded_both(jnp.einsum('ghls,gshe->glhe', low(probs), value_heads, precision=highest))
    context = context.reshape(examples * TEXT, HEADS * HEAD)
    attn_out = low_back(jnp.dot(context, out_weight, precision=highest) + out_bias)
    residual = text_in + attn_out
    mid_normed = low(layer_norm(residual, mlp_gain, mlp_shift))
    pre_act = low_back(jnp.dot(mid_normed, up_weight, precision=highest) + up_bias)
    hidden = low(jax.nn.gelu(pre_act))
    mlp_out = low_back(jnp.dot(hidden, down_weight, precision=highest) + down_bias)
    return residual + mlp_out

def reference(tokens, memory, split_point, text_length, patch_mask, query_weight, query_bias, key_weight, value_weight, value_bias, out_weight, out_bias, attn_gain, attn_shift, mlp_gain, mlp_shift, up_weight, up_bias, down_weight, down_bias, cotangent):
    params = tuple((entry.astype(jnp.float32) for entry in (query_weight, query_bias, key_weight, value_weight, value_bias, out_weight, out_bias, attn_gain, attn_shift, mlp_gain, mlp_shift, up_weight, up_bias, down_weight, down_bias)))
    groups = N_DP
    text_all = tokens.astype(jnp.float32).reshape(groups, SEQ_DEV * TEXT, D)
    memory_all = memory.astype(jnp.float32).reshape(groups, SEQ_DEV * PATCHES, D)
    cot_all = cotangent.astype(jnp.float32).reshape(groups, SEQ_DEV * TEXT, D)
    split_all = split_point.astype(jnp.int32).reshape(groups, SEQ_DEV)
    length_all = text_length.astype(jnp.int32).reshape(groups, SEQ_DEV)
    patch_all = patch_mask.astype(jnp.int32).reshape(groups, SEQ_DEV, PATCHES)

    def per_group(totals, bundle):
        text_in, memory_in, cot_in, split_block, length_block, patch_block = bundle

        def forward(text_arg, memory_arg, param_arg):
            return block_layer(text_arg, memory_arg, param_arg, split_block, length_block, patch_block)
        result, pullback = jax.vjp(forward, text_in, memory_in, params)
        text_grad, memory_grad, param_grads = pullback(cot_in)
        totals = jax.tree.map(lambda earlier, current: earlier + current, totals, param_grads)
        return (totals, (result.astype(jnp.bfloat16), text_grad, memory_grad))
    zeros = jax.tree.map(jnp.zeros_like, params)
    totals, (outputs, input_grads, memory_grads) = lax.scan(per_group, zeros, (text_all, memory_all, cot_all, split_all, length_all, patch_all))
    layer_out = outputs.reshape(TOKENS, D)
    input_grad = input_grads.reshape(TOKENS, D)
    memory_grad = memory_grads.reshape(MEMROWS, D)
    return (layer_out, input_grad, memory_grad, totals[0], totals[2], totals[3], totals[5], totals[11], totals[13], totals[1], totals[4], totals[12], totals[6], totals[14], totals[7], totals[8], totals[9], totals[10])
```

```python
import functools

import jax
import jax.numpy as jnp
from jax import lax
from jax.experimental import pallas as pl
from jax.experimental.pallas import tpu as pltpu
from jax.sharding import PartitionSpec as P

HEAD = 64
TEXT = 256
PATCHES = 196
SLOTS = 256
KEYS = SLOTS + TEXT
EPS = 1e-06
NEG = -1000000000.0
SCALE = HEAD ** (-0.5)
F32 = jnp.float32
BF16 = jnp.bfloat16
AXES = ("dp", "mp")

LEFT = 512
RIGHT = 256


def nn(a, b):
    return lax.dot_general(a, b, (((1,), (0,)), ((), ())), preferred_element_type=F32)


def nt(a, b):
    return lax.dot_general(a, b, (((1,), (1,)), ((), ())), preferred_element_type=F32)


def eye(n):
    rows = lax.broadcasted_iota(jnp.int32, (n, n), 0)
    cols = lax.broadcasted_iota(jnp.int32, (n, n), 1)
    return (rows == cols).astype(F32).astype(BF16)


def standard(matrix):
    average = jnp.mean(matrix, axis=-1, keepdims=True)
    centered = matrix - average
    inverse = lax.rsqrt(jnp.mean(centered * centered, axis=-1, keepdims=True) + EPS)
    return centered * inverse, inverse


def standard_back(normed, inverse, grad_out, gain):
    scaled = grad_out * gain
    return inverse * (
        scaled
        - jnp.mean(scaled, axis=-1, keepdims=True)
        - normed * jnp.mean(scaled * normed, axis=-1, keepdims=True)
    )


def call(kernel, out_shapes, *args, scratch=(), smem=0, flops=0):
    nbytes = sum(a.size * a.dtype.itemsize for a in args) + sum(
        int(functools.reduce(lambda p, q: p * q, s, 1)) * jnp.dtype(d).itemsize for s, d in out_shapes
    )
    return pl.pallas_call(
        kernel,
        out_shape=[jax.ShapeDtypeStruct(s, d) for s, d in out_shapes],
        in_specs=[pl.BlockSpec(memory_space=pltpu.SMEM)] * smem
        + [pl.BlockSpec(memory_space=pltpu.VMEM)] * (len(args) - smem),
        out_specs=[pl.BlockSpec(memory_space=pltpu.VMEM)] * len(out_shapes),
        scratch_shapes=list(scratch),
        compiler_params=pltpu.CompilerParams(vmem_limit_bytes=56 * 1024 * 1024),
        cost_estimate=pl.CostEstimate(flops=flops, bytes_accessed=nbytes, transcendentals=0),
    )(*args)


def prep_kernel(
    place, tok_o, tok_p, mem_o, mem_p, cot_o, cot_p, vec,
    x_ref, xt_ref, tok_r, cot_r, cot_t, mem_r, vec_r, hot_ref,
):
    features = tok_o.shape[1]
    lane = lax.broadcasted_iota(jnp.int32, (features, features), 1)
    hot_ref[...] = (lane == place[...]).astype(F32).astype(BF16)
    gain = vec[0:1, :].astype(F32)
    shift = vec[1:2, :].astype(F32)
    vec_r[...] = nt(vec[...], hot_ref[...])

    for at, (mem, tok) in enumerate(((mem_o, tok_o), (mem_p, tok_p))):
        for first, src in ((0, mem), (SLOTS, tok)):
            normed, _ = standard(src[...].astype(F32))
            low = (normed * gain + shift).astype(BF16)
            x_ref[at, first : first + 256, :] = nt(low, hot_ref[...]).astype(BF16)
            xt_ref[:, at * KEYS + first : at * KEYS + first + 256] = nt(hot_ref[...], low).astype(BF16)
    mem_r[...] = nt(mem_o[...], hot_ref[...]).astype(BF16)
    for at, (tok, cot) in enumerate(((tok_o, cot_o), (tok_p, cot_p))):
        rows = slice(at * TEXT, (at + 1) * TEXT)
        tok_r[rows, :] = nt(tok[...], hot_ref[...]).astype(BF16)
        cot_r[rows, :] = nt(cot[...], hot_ref[...]).astype(BF16)
        cot_t[:, rows] = nt(hot_ref[...], cot[...]).astype(BF16)


def masked(raw, cond):
    return jnp.where(cond, raw * SCALE, NEG)


def attend_kernel(
    split, length,
    own, own_y, peer, peer_d0, peer_d1, z0, z1, z2, z3, x_ref, bias, patch,
    w_ref, y_ref, p_ref, ctx_ref, out_ref,
):
    half = own.shape[0]
    block = half // 4
    w_ref[0, 0:half, 0:LEFT] = own[...]
    w_ref[0, half : 2 * half, 0:LEFT] = own_y[...]
    w_ref[1, 0:half, 0:LEFT] = peer[...]
    w_ref[1, half : half + half // 2, 0:LEFT] = peer_d0[...]
    w_ref[1, half + half // 2 : 2 * half, 0:LEFT] = peer_d1[...]
    for k, piece in enumerate((z0, z1, z2, z3)):
        for m in range(2):
            for ry in range(2):
                first = ry * half + k * block
                src = (m * 2 + ry) * block
                w_ref[m, first : first + block, LEFT : LEFT + RIGHT] = piece[src : src + block, :]

    lane = lax.broadcasted_iota(jnp.int32, (TEXT, 128), 1)
    lane_k = lax.broadcasted_iota(jnp.int32, (KEYS, 128), 1)
    zero = jnp.zeros((TEXT, 128), BF16)
    unit = eye(128)
    unit_t = eye(TEXT)
    key_place = lax.broadcasted_iota(jnp.int32, (TEXT, TEXT), 0)
    query_place = lax.broadcasted_iota(jnp.int32, (TEXT, TEXT), 1)
    out_ref[...] = jnp.zeros_like(out_ref)

    def step(at, carry):
        e, m = at // 2, at % 2
        x = x_ref[e]
        w = w_ref[m]
        b = bias[m]
        y1 = nn(x, w[:, 0:384]) + b[:, 0:384]
        y_ref[m, e, :, 0:384] = y1.astype(BF16)
        y2 = nn(x, w[:, LEFT : LEFT + RIGHT]) + b[:, 384:640]
        y_ref[m, e, :, 384:512] = y2[:, 0:128].astype(BF16)
        y_ref[m, e, :, 512:640] = jnp.where(lane_k < HEAD, y2[:, 128:256], 0.0).astype(BF16)

        patch_ok = jnp.broadcast_to(patch[e], (SLOTS, TEXT)) > 0.0
        text_ok = ((key_place < split[e]) | (key_place <= query_place)) & (key_place < length[e])

        q01 = y_ref[m, e, SLOTS:KEYS, 0:128]
        q2 = y_ref[m, e, SLOTS:KEYS, 384:512]
        v01t = nt(unit, y_ref[m, e, :, 256:384]).astype(BF16)
        v2t = nt(unit, y_ref[m, e, :, 384:512]).astype(BF16)
        ctx01 = []
        for head in range(3):
            if head == 0:
                q, first, vt = jnp.where(lane < HEAD, q01, zero), 128, v01t[0:HEAD]
            elif head == 1:
                q, first, vt = jnp.where(lane >= HEAD, q01, zero), 128, v01t[HEAD:128]
            else:
                q, first, vt = jnp.where(lane < HEAD, q2, zero), 512, v2t[HEAD:128]
            s_mem = masked(nt(y_ref[m, e, 0:SLOTS, first : first + 128], q), patch_ok)
            s_text = masked(nt(y_ref[m, e, SLOTS:KEYS, first : first + 128], q), text_ok)
            largest = jnp.maximum(
                jnp.max(s_mem, axis=0, keepdims=True), jnp.max(s_text, axis=0, keepdims=True)
            )
            e_mem = jnp.exp(s_mem - largest)
            e_text = jnp.exp(s_text - largest)
            total = jnp.sum(e_mem, axis=0, keepdims=True) + jnp.sum(e_text, axis=0, keepdims=True)
            inverse = 1.0 / total
            p_mem = (e_mem * inverse).astype(BF16)
            p_text = (e_text * inverse).astype(BF16)
            p_ref[m, e, head, 0:SLOTS, :] = p_mem
            p_ref[m, e, head, SLOTS:KEYS, :] = p_text
            ctx01.append(nn(vt[:, 0:SLOTS], p_mem) + nn(vt[:, SLOTS:KEYS], p_text))
        c01t = jnp.concatenate([ctx01[0], ctx01[1]], axis=0).astype(BF16)
        c2t = jnp.concatenate([jnp.zeros((HEAD, TEXT), F32), ctx01[2]], axis=0).astype(BF16)
        c01 = nt(unit_t, c01t).astype(BF16)
        c2 = nt(unit_t, c2t).astype(BF16)
        ctx_ref[m, e, :, 0:128] = c01
        ctx_ref[m, e, :, 128:256] = c2
        out_ref[e] += nt(c01, w[:, 384:512]) + nt(c2, w[:, 640:768])
        return carry

    lax.fori_loop(0, 4, step, 0)


def gelu_pair(v):
    c = 0.7978845608028654
    square = v * v
    t = jnp.tanh(c * v * (1.0 + 0.044715 * square))
    gelu = 0.5 * v * (1.0 + t)
    slope = 0.5 * (1.0 + t) + 0.5 * v * (1.0 - t * t) * (c * (1.0 + 3 * 0.044715 * square))
    return gelu, slope


def assemble(own, own_y, peer, peer_d0, peer_d1, w_ref):
    half = own.shape[0]
    w_ref[0, 0:half, :] = own[...]
    w_ref[0, half : 2 * half, :] = own_y[...]
    w_ref[1, 0:half, :] = peer[...]
    w_ref[1, half : half + half // 2, :] = peer_d0[...]
    w_ref[1, half + half // 2 : 2 * half, :] = peer_d1[...]


def up_kernel(
    part, part_in, tok_r, vec_r, cot_t, bias, own, own_y, peer, peer_d0, peer_d1,
    res_ref, mid_ref, mid_t, u_ref, hid_ref, slope_ref, g00, g01, g10, g11,
):
    assemble(own, own_y, peer, peer_d0, peer_d1, u_ref)
    half = own.shape[0]
    for e in range(2):
        rows = slice(e * TEXT, (e + 1) * TEXT)
        res = (
            tok_r[rows, :].astype(F32)
            + (part[e].astype(F32) + part_in[1 - e].astype(F32))
            + vec_r[4:5, :]
        )
        res_ref[rows, :] = res
        normed, _ = standard(res)
        mid_ref[rows, :] = (normed * vec_r[2:3, :] + vec_r[3:4, :]).astype(BF16)
    mid_t[...] = nt(eye(mid_ref.shape[1]), mid_ref[...]).astype(BF16)
    for m, (top, bottom) in enumerate(((g00, g01), (g10, g11))):
        for e in range(2):
            rows = slice(e * TEXT, (e + 1) * TEXT)
            pre = nn(mid_ref[rows, :], u_ref[m]) + bias[m]
            gelu, slope = gelu_pair(pre)
            hid_ref[m, rows, :] = gelu.astype(BF16)
            slope_ref[m, rows, :] = slope.astype(BF16)
        top[...] = nn(cot_t[0:half, :], hid_ref[m]).astype(BF16)
        bottom[...] = nn(cot_t[half : 2 * half, :], hid_ref[m]).astype(BF16)


def down_kernel(
    u_ref, hid_ref, slope_ref, mid_t, cot_r, own, own_y, peer, peer_d0, peer_d1,
    out_ref, grad_ref, bias_ref, g00, g01, g10, g11, d_ref, pre_ref,
):
    assemble(own, own_y, peer, peer_d0, peer_d1, d_ref)
    half = own.shape[0]
    bias_ref[...] = jnp.zeros_like(bias_ref)
    for m in range(2):
        for e in range(2):
            rows = slice(e * TEXT, (e + 1) * TEXT)
            pre = (nn(cot_r[rows, :], d_ref[m]) * slope_ref[m, rows, :].astype(F32)).astype(BF16)
            pre_ref[m, rows, :] = pre
            bias_ref[m : m + 1, :] += jnp.sum(pre.astype(F32), axis=0, keepdims=True)
    for e in range(2):
        rows = slice(e * TEXT, (e + 1) * TEXT)
        grad_ref[e] = (nt(pre_ref[0, rows, :], u_ref[0]) + nt(pre_ref[1, rows, :], u_ref[1])).astype(BF16)
    for e in range(2):
        rows = slice(e * TEXT, (e + 1) * TEXT)
        out_ref[e] = (nt(hid_ref[0, rows, :], d_ref[0]) + nt(hid_ref[1, rows, :], d_ref[1])).astype(BF16)
    for m, (top, bottom) in enumerate(((g00, g01), (g10, g11))):
        top[...] = nn(mid_t[0:half, :], pre_ref[m]).astype(BF16)
        bottom[...] = nn(mid_t[half : 2 * half, :], pre_ref[m]).astype(BF16)


def attend_back_kernel(
    grad, grad_in, res_ref, cot_r, vec_r, w_ref, y_ref, p_ref,
    rg_ref, agt_ref, dy_ref, back_o, back_p, sums, bias_ref, ag_ref, back_ref,
):
    lane = lax.broadcasted_iota(jnp.int32, (TEXT, 128), 1)
    row = lax.broadcasted_iota(jnp.int32, (128, TEXT), 0)
    zero = jnp.zeros((TEXT, 128), BF16)
    unit = eye(128)
    unit_t = eye(TEXT)
    for e in range(2):
        rows = slice(e * TEXT, (e + 1) * TEXT)
        mid_grad = grad[e].astype(F32) + grad_in[1 - e].astype(F32)
        normed, inverse = standard(res_ref[rows, :])
        cot = cot_r[rows, :].astype(F32)
        resid = cot + standard_back(normed, inverse, mid_grad, vec_r[2:3, :])
        low = resid.astype(BF16)
        ag_ref[rows, :] = low
        if e == 0:
            rg_ref[...] = resid
            sums[0:1, :] = jnp.sum(mid_grad * normed, axis=0, keepdims=True)
            sums[1:2, :] = jnp.sum(mid_grad, axis=0, keepdims=True)
            sums[2:3, :] = jnp.sum(low.astype(F32), axis=0, keepdims=True)
            sums[3:4, :] = jnp.sum(cot, axis=0, keepdims=True)
            sums[4:8, :] = jnp.zeros_like(sums[4:8, :])
    agt_ref[...] = nt(eye(ag_ref.shape[1]), ag_ref[...]).astype(BF16)
    bias_ref[...] = jnp.zeros_like(bias_ref)
    back_ref[...] = jnp.zeros_like(back_ref)

    def step(at, carry):
        e, m = at // 2, at % 2
        w = w_ref[m]
        ag = ag_ref[pl.ds(pl.multiple_of(e * TEXT, TEXT), TEXT), :]
        dc01 = nn(ag, w[:, 384:512]).astype(BF16)
        dc2 = nn(ag, w[:, 640:768]).astype(BF16)
        q01 = y_ref[m, e, SLOTS:KEYS, 0:128]
        q2 = y_ref[m, e, SLOTS:KEYS, 384:512]
        k01 = y_ref[m, e, :, 128:256]
        k2 = y_ref[m, e, :, 512:640]
        k01t = nt(unit, k01).astype(BF16)
        k2t = nt(unit, k2).astype(BF16)
        dk, dv, dqt = [], [], []
        for head in range(3):
            keep = (lane < HEAD) if head == 0 else (lane >= HEAD)
            if head < 2:
                dc = jnp.where(keep, dc01, zero)
                q = jnp.where(keep, q01, zero)
                v = y_ref[m, e, :, 256:384]
                kt = k01t[0:HEAD] if head == 0 else k01t[HEAD:128]
            else:
                dc = jnp.where(lane >= HEAD, dc2, zero)
                q = jnp.where(lane < HEAD, q2, zero)
                v = y_ref[m, e, :, 384:512]
                kt = k2t[0:HEAD]
            prob = p_ref[m, e, head]
            probs = prob.astype(F32)
            grad_p = nt(v, dc)
            dot = jnp.sum(probs * grad_p, axis=0, keepdims=True)
            score = (probs * (grad_p - dot)).astype(BF16)
            dk.append(nn(score, q))
            dv.append(nn(prob, dc))
            dqt.append(nn(kt, score))
        dk01 = ((dk[0] + dk[1]) * SCALE).astype(BF16)
        dk2 = (dk[2] * SCALE).astype(BF16)
        dv01 = (dv[0] + dv[1]).astype(BF16)
        dv2 = dv[2].astype(BF16)
        dq01 = nt(unit_t, (jnp.concatenate([dqt[0], dqt[1]], axis=0) * SCALE).astype(BF16))
        dq2 = nt(
            unit_t,
            (jnp.concatenate([dqt[2], jnp.zeros((HEAD, TEXT), F32)], axis=0) * SCALE).astype(BF16),
        )
        dy_ref[m, e, 0:SLOTS, 0:128] = zero
        dy_ref[m, e, SLOTS:KEYS, 0:128] = dq01.astype(BF16)
        dy_ref[m, e, :, 128:256] = dk01
        dy_ref[m, e, :, 256:384] = dv01
        dy_ref[m, e, 0:SLOTS, 384:512] = dv2[0:SLOTS]
        dy_ref[m, e, SLOTS:KEYS, 384:512] = (dq2 + dv2[SLOTS:KEYS].astype(F32)).astype(BF16)
        dy_ref[m, e, :, 512:640] = dk2
        dy = dy_ref[m, e]
        bias_ref[m] += jnp.sum(dy.astype(F32), axis=0, keepdims=True)
        back_ref[e] += nt(dy[:, 0:384], w[:, 0:384]) + nt(dy[:, 384:640], w[:, LEFT : LEFT + RIGHT])
        return carry

    lax.fori_loop(0, 4, step, 0)
    back_o[...] = back_ref[0]
    back_p[...] = back_ref[1].astype(BF16)


def weight_kernel(
    xt_ref, agt_ref, dy_ref, ctx_ref,
    a00, a01, a10, a11, c0, c1, c2, c3,
):
    half = a00.shape[0]
    block = half // 4
    for m, tops in enumerate(((a00, a01), (a10, a11))):
        dy = dy_ref[m].reshape(2 * KEYS, 640)
        ctx = ctx_ref[m].reshape(2 * TEXT, 256)
        for ry in range(2):
            rows = slice(ry * half, (ry + 1) * half)
            tops[ry][:, 0:384] = nn(xt_ref[rows, :], dy[:, 0:384]).astype(BF16)
            tops[ry][:, 384:512] = nn(agt_ref[rows, :], ctx[:, 0:128]).astype(BF16)
            right = nn(xt_ref[rows, :], dy[:, 384:640])
            out2 = nn(agt_ref[rows, :], ctx[:, 128:256])
            for k, piece in enumerate((c0, c1, c2, c3)):
                src = slice(k * block, (k + 1) * block)
                first = (m * 2 + ry) * block
                piece[first : first + block, 0:128] = right[src, 0:128].astype(BF16)
                piece[first : first + block, 128:256] = (right[src, 128:256] + out2[src, :]).astype(BF16)


def last_kernel(
    back_o, back_in, tok_r, mem_r, rg_ref, res_ref, out_o, out_in, vec_r, hot_ref, sums,
    layer_ref, in_ref, mem_ref, vec_out,
):
    hot = hot_ref[...]

    def restore(v):
        high = v.astype(BF16)
        low = (v - high.astype(F32)).astype(BF16)
        return nn(high, hot) + nn(low, hot)

    gain = vec_r[0:1, :]
    layer = (
        res_ref[...] + (out_o[0].astype(F32) + out_in[...].astype(F32)) + vec_r[5:6, :]
    ).astype(BF16)
    layer_ref[...] = nn(layer, hot).astype(BF16)
    mem_back = back_o[0:SLOTS, :] + back_in[0:SLOTS, :].astype(F32)
    text_back = back_o[SLOTS:KEYS, :] + back_in[SLOTS:KEYS, :].astype(F32)
    normed, inverse = standard(tok_r[...].astype(F32))
    in_ref[...] = restore(rg_ref[...] + standard_back(normed, inverse, text_back, gain))
    normed_m, inverse_m = standard(mem_r[...].astype(F32))
    grad_m = standard_back(normed_m, inverse_m, mem_back, gain)
    mem_ref[...] = restore(grad_m)[0:PATCHES, :]
    gain_sum = jnp.sum(text_back * normed, axis=0, keepdims=True) + jnp.sum(
        mem_back * normed_m, axis=0, keepdims=True
    )
    shift_sum = jnp.sum(text_back, axis=0, keepdims=True) + jnp.sum(mem_back, axis=0, keepdims=True)
    stack = jnp.concatenate([sums[0:4, :], gain_sum, shift_sum, sums[4:6, :]], axis=0)
    vec_out[...] = restore(stack)


class Links:
    def __init__(self, dp, mp):
        self.dp, self.mp, self.depth = dp, mp, dp // 2
        self.x = self.pairs(lambda d, m: (d, m ^ 2))
        self.c = self.pairs(lambda d, m: (d, m ^ 1))
        self.y = self.pairs(lambda d, m: (d ^ 1, m))

    def pairs(self, to):
        out = []
        for d in range(self.dp):
            for m in range(self.mp):
                d2, m2 = to(d, m)
                out.append((d * self.mp + m, d2 * self.mp + m2))
        return out

    def z(self, k):
        return self.pairs(lambda d, m: ((((d // 2 + k) % self.depth) * 2 + d % 2), m))

    def send(self, a, pairs):
        return lax.ppermute(a, AXES, pairs)

    def z_gather(self, shard):
        if self.depth <= 4:
            return [shard] + [self.send(shard, self.z(k)) for k in range(1, self.depth)]
        held = shard[None]
        step = 1
        while step < self.depth:
            held = jnp.concatenate([held, self.send(held, self.z(step))], axis=0)
            step *= 2
        return [held[k] for k in range(self.depth)]

    def z_scatter(self, parts):
        if self.depth <= 4:
            got = [self.send(parts[k], self.z(-k)) for k in range(1, self.depth)]
            total = parts[0].astype(F32)
            for g in got:
                total = total + g.astype(F32)
            return total
        held = jnp.stack(parts).astype(F32)
        step = self.depth // 2
        while step >= 1:
            held = held[:step] + self.send(held[step:].astype(BF16), self.z(-step)).astype(F32)
            step //= 2
        return held[0]

    def gather_rows(self, shard):
        own = jnp.concatenate(self.z_gather(shard), axis=0)
        cut = own.shape[0] // 2
        peer = self.send(own, self.x)
        own_y = self.send(own, self.y)
        d0 = self.send(own_y[:cut], self.x)
        d1 = self.send(peer[cut:], self.y)
        return own, own_y, peer, d0, d1

    def gather_quads(self, shard):
        y1 = self.send(shard, self.y)
        x1 = self.send(shard, self.x)
        d1 = self.send(y1, self.x)
        pieces = self.z_gather(jnp.concatenate([shard, y1, x1, d1], axis=0))
        if self.depth == 4:
            return pieces
        r, lanes = shard.shape
        whole = jnp.stack(pieces).reshape(self.depth, 4, r, lanes).transpose(1, 0, 2, 3)
        whole = whole.reshape(4, 4, self.depth * r // 4, lanes)
        return [whole[:, k].reshape(-1, lanes) for k in range(4)]

    def scatter_rows(self, g00, g01, g10, g11):
        cut = g00.shape[0] // 2
        rows = g00.shape[0]
        d0 = self.send(g11[:cut], self.x)
        d1 = self.send(g11[cut:], self.y)
        send_y = jnp.concatenate([(g01[:cut].astype(F32) + d0.astype(F32)).astype(BF16), g01[cut:]], axis=0)
        send_x = jnp.concatenate([g10[:cut], (g10[cut:].astype(F32) + d1.astype(F32)).astype(BF16)], axis=0)
        from_y = self.send(send_y, self.y)
        from_x = self.send(send_x, self.x)
        total = (g00.astype(F32) + from_y.astype(F32) + from_x.astype(F32)).astype(BF16)
        r = rows // self.depth
        return self.z_scatter([total[k * r : (k + 1) * r] for k in range(self.depth)])

    def scatter_quads(self, pieces):
        if self.depth != 4:
            lanes = pieces[0].shape[1]
            whole = jnp.stack([p.reshape(4, -1, lanes) for p in pieces], axis=1)
            whole = whole.reshape(4, self.depth, -1, lanes).transpose(1, 0, 2, 3)
            pieces = [whole[k].reshape(-1, lanes) for k in range(self.depth)]
        total = self.z_scatter(pieces)
        r = total.shape[0] // 4
        t00, t01, t10, t11 = (total[i * r : (i + 1) * r] for i in range(4))
        d = self.send(t11.astype(BF16), self.x)
        from_y = self.send((t01 + d.astype(F32)).astype(BF16), self.y)
        from_x = self.send(t10.astype(BF16), self.x)
        return t00 + from_y.astype(F32) + from_x.astype(F32)

    def add_all(self, a):
        a = a + self.send(a, self.c)
        a = a + self.send(a, self.x)
        a = a + self.send(a, self.y)
        if self.depth <= 4:
            got = [self.send(a, self.z(k)) for k in range(1, self.depth)]
            for g in got:
                a = a + g
            return a
        step = 1
        while step < self.depth:
            a = a + self.send(a, self.z(step))
            step *= 2
        return a


def per_device(
    tokens, memory, split_point, text_length, patch_mask,
    query_weight, query_bias, key_weight, value_weight, value_bias,
    out_weight, out_bias, attn_gain, attn_shift, mlp_gain, mlp_shift,
    up_weight, up_bias, down_weight, down_bias, cotangent,
):
    features = tokens.shape[1]
    width = query_weight.shape[1]
    hidden = up_weight.shape[1]
    dp, mp = lax.axis_size("dp"), lax.axis_size("mp")
    links = Links(dp, mp)
    dp_at, mp_at = lax.axis_index("dp"), lax.axis_index("mp")
    z_at, y_at, x_at, c_at = dp_at // 2, dp_at % 2, mp_at // 2, mp_at % 2
    depth = dp // 2
    r = features // dp
    half = features // 2

    out_t = out_weight.T
    left = jnp.concatenate(
        [query_weight[:, :128], key_weight[:, :128], value_weight[:, :128], out_t[:, :128]], axis=1
    )
    right = jnp.concatenate(
        [query_weight[:, 128:], value_weight[:, 128:], key_weight[:, 128:], out_t[:, 128:]], axis=1
    )
    down_t = down_weight.T
    biases = jnp.concatenate([query_bias, value_bias, up_bias]).astype(BF16).reshape(1, -1)
    biases_x = links.send(biases, links.x)
    tok_p = links.send(tokens, links.c)
    mem = jnp.pad(memory, ((0, SLOTS - PATCHES), (0, 0)))
    mem_p = links.send(mem, links.c)
    cot_p = links.send(cotangent, links.c)
    attn_rows = links.gather_rows(left)
    attn_quads = links.gather_quads(right)
    up_rows = links.gather_rows(up_weight)
    down_rows = links.gather_rows(down_t)

    rel = jnp.arange(features, dtype=jnp.int32)
    rest = rel % half
    place = ((z_at - rest // r) % depth) * (2 * r) + (y_at ^ (rel // half)) * r + rest % r
    place = place.astype(jnp.int32).reshape(features, 1)

    blank = jnp.zeros_like(attn_gain)
    vec = jnp.stack(
        [attn_gain, attn_shift, mlp_gain, mlp_shift, out_bias, down_bias] + [blank] * 10
    )
    x, xt, tok_r, cot_r, cot_t, mem_r, vec_r, hot = call(
        prep_kernel,
        [
            ((2, KEYS, features), BF16), ((features, 2 * KEYS), BF16),
            ((2 * TEXT, features), BF16), ((2 * TEXT, features), BF16), ((features, 2 * TEXT), BF16),
            ((SLOTS, features), BF16), ((16, features), F32), ((features, features), BF16),
        ],
        place, tokens, tok_p, mem, mem_p, cotangent, cot_p, vec,
    )

    both = jnp.stack([biases[0], biases_x[0]]).astype(F32)
    qb, vb, ub = both[:, :width], both[:, width : 2 * width], both[:, 2 * width :]
    none = jnp.zeros((2, 128), F32)
    bias = jnp.concatenate([qb[:, :128], none, vb[:, :128], qb[:, 128:], vb[:, 128:], none], axis=1)
    at_own = x_at * 2 + c_at
    at_peer = x_at * 2 + 1 - c_at
    split = jnp.stack([split_point[at_own], split_point[at_peer]])
    length = jnp.stack([text_length[at_own], text_length[at_peer]])
    patch = jnp.stack([patch_mask[at_own], patch_mask[at_peer]]).astype(F32)
    patch = jnp.pad(patch, ((0, 0), (0, SLOTS - PATCHES)))[:, :, None]

    w, y, p, ctx, part = call(
        attend_kernel,
        [
            ((2, features, features), BF16), ((2, 2, KEYS, 640), BF16), ((2, 2, 3, KEYS, TEXT), BF16),
            ((2, 2, TEXT, 256), BF16), ((2, TEXT, features), F32),
        ],
        split, length, *attn_rows, *attn_quads, x, bias.reshape(2, 1, 640), patch,
        smem=2,
    )
    part = part.astype(BF16)
    part_in = links.send(part, links.c)

    quarter = ((half, hidden), BF16)
    res, _, mid_t, u, hid, slope, d00, d01, d10, d11 = call(
        up_kernel,
        [
            ((2 * TEXT, features), F32), ((2 * TEXT, features), BF16), ((features, 2 * TEXT), BF16),
            ((2, features, hidden), BF16), ((2, 2 * TEXT, hidden), BF16), ((2, 2 * TEXT, hidden), BF16),
        ]
        + [quarter] * 4,
        part, part_in, tok_r, vec_r, cot_t, ub.reshape(2, 1, hidden), *up_rows,
    )
    down_sum = links.scatter_rows(d00, d01, d10, d11)

    layer, mid_grad, up_bias_part, u00, u01, u10, u11 = call(
        down_kernel,
        [((2, TEXT, features), BF16), ((2, TEXT, features), BF16), ((2, hidden), F32)] + [quarter] * 4,
        u, hid, slope, mid_t, cot_r, *down_rows,
        scratch=[pltpu.VMEM((2, features, hidden), BF16), pltpu.VMEM((2, 2 * TEXT, hidden), BF16)],
    )
    grad_in = links.send(mid_grad, links.c)
    layer_in = links.send(layer[1], links.c)
    up_sum = links.scatter_rows(u00, u01, u10, u11)

    rg, ag_t, dy, back_o, back_p, sums, bias_part = call(
        attend_back_kernel,
        [
            ((TEXT, features), F32), ((features, 2 * TEXT), BF16), ((2, 2, KEYS, 640), BF16),
            ((KEYS, features), F32), ((KEYS, features), BF16), ((8, features), F32), ((2, 1, 640), F32),
        ],
        mid_grad, grad_in, res, cot_r, vec_r, w, y, p,
        scratch=[pltpu.VMEM((2 * TEXT, features), BF16), pltpu.VMEM((2, KEYS, features), F32)],
    )
    back_in = links.send(back_p, links.c)
    a00, a01, a10, a11, c0, c1, c2, c3 = call(
        weight_kernel,
        [((half, LEFT), BF16)] * 4 + [((features // 2, RIGHT), BF16)] * 4,
        xt, ag_t, dy, ctx,
    )
    left_sum = links.scatter_rows(a00, a01, a10, a11)
    right_sum = links.scatter_quads([c0, c1, c2, c3])

    layer_out, input_grad, memory_grad, vec_sum = call(
        last_kernel,
        [((TEXT, features), BF16), ((TEXT, features), F32), ((PATCHES, features), F32), ((8, features), F32)],
        back_o, back_in, tok_r[:TEXT], mem_r, rg, res[:TEXT], layer, layer_in, vec_r, hot, sums,
    )

    bias_part = bias_part.reshape(2, 640)
    q_part = jnp.concatenate([bias_part[:, 0:128], bias_part[:, 384:448]], axis=1)
    v_part = jnp.concatenate([bias_part[:, 256:384], bias_part[:, 448:512]], axis=1)
    m_own, m_peer = mp_at, mp_at ^ 2
    slots = jnp.arange(mp, dtype=jnp.int32)[:, None]

    def spread(pair):
        return (
            jnp.where(slots == m_own, pair[0:1], 0.0) + jnp.where(slots == m_peer, pair[1:2], 0.0)
        ).reshape(-1, features)

    stack = jnp.concatenate([vec_sum[0:6], spread(q_part), spread(v_part), spread(up_bias_part)], axis=0)
    stack = links.add_all(stack)
    at = dp_at * mp + mp_at
    few = features // (dp * mp)
    vectors = lax.dynamic_slice(stack[:8], (0, at * few), (8, few))
    many = up_bias.shape[0] // dp
    up_bias_sum = lax.dynamic_slice(stack[8:].reshape(-1), (at * many,), (many,))

    query_sum = jnp.concatenate([left_sum[:, 0:128], right_sum[:, 0:64]], axis=1)
    key_sum = jnp.concatenate([left_sum[:, 128:256], right_sum[:, 128:192]], axis=1)
    value_sum = jnp.concatenate([left_sum[:, 256:384], right_sum[:, 64:128]], axis=1)
    out_sum = jnp.concatenate([left_sum[:, 384:512], right_sum[:, 192:256]], axis=1).T
    return (
        layer_out, input_grad, memory_grad,
        query_sum, key_sum, value_sum, out_sum, up_sum, down_sum.T,
        vectors[6], vectors[7], up_bias_sum,
        vectors[2], vectors[3], vectors[4], vectors[5], vectors[0], vectors[1],
    )


def solution(mesh):
    rows = P(AXES, None)
    flat = P(AXES)
    in_specs = (
        rows, rows, P("dp"), P("dp"), P("dp", None),
        P("dp", "mp"), P("mp"), P("dp", "mp"), P("dp", "mp"), P("mp"),
        P("mp", "dp"), P(), P(), P(), P(), P(),
        P("dp", "mp"), P("mp"), P("mp", "dp"), P(), rows,
    )
    out_specs = (
        rows, rows, rows,
        P("dp", "mp"), P("dp", "mp"), P("dp", "mp"), P("mp", "dp"), P("dp", "mp"), P("mp", "dp"),
    ) + (flat,) * 9
    return jax.shard_map(
        per_device, mesh=mesh, in_specs=in_specs, out_specs=out_specs, check_vma=False
    )
```

```python
import functools

import jax
import jax.numpy as jnp
from jax import lax
from jax.experimental import pallas as pl
from jax.experimental.pallas import tpu as pltpu
from jax.sharding import PartitionSpec as P

HEAD = 64
TEXT = 256
PATCHES = 196
SLOTS = 256
KEYS = SLOTS + TEXT
EPS = 1e-06
NEG = -1000000000.0
SCALE = HEAD ** (-0.5)
F32 = jnp.float32
BF16 = jnp.bfloat16
AXES = ("dp", "mp")

CUT = 384


def nn(a, b):
    return lax.dot_general(a, b, (((1,), (0,)), ((), ())), preferred_element_type=F32)


def nt(a, b):
    return lax.dot_general(a, b, (((1,), (1,)), ((), ())), preferred_element_type=F32)


def eye(n):
    rows = lax.broadcasted_iota(jnp.int32, (n, n), 0)
    cols = lax.broadcasted_iota(jnp.int32, (n, n), 1)
    return (rows == cols).astype(F32).astype(BF16)


def standard(matrix):
    average = jnp.mean(matrix, axis=-1, keepdims=True)
    centered = matrix - average
    inverse = lax.rsqrt(jnp.mean(centered * centered, axis=-1, keepdims=True) + EPS)
    return centered * inverse, inverse


def standard_back(normed, inverse, grad_out, gain):
    scaled = grad_out * gain
    return inverse * (
        scaled
        - jnp.mean(scaled, axis=-1, keepdims=True)
        - normed * jnp.mean(scaled * normed, axis=-1, keepdims=True)
    )


UNIT = 1e9
COST = {
    "prep_kernel": 8.0, "attend_kernel": 17.0, "up_kernel": 9.0, "down_kernel": 9.0,
    "gate_kernel": 12.0, "add_kernel": 30.0, "attend_back_kernel": 19.0, "weight_kernel": 6.0, "last_kernel": 6.0,
}


def call(kernel, out_shapes, *args, scratch=(), smem=0, after=(), anywhere=False):
    name = getattr(kernel, "func", kernel).__name__
    waits = len(after)

    def body(*refs):
        return kernel(*refs[waits:])

    place = pl.BlockSpec(memory_space=pl.ANY if anywhere else pltpu.VMEM)
    return pl.pallas_call(
        body,
        out_shape=[jax.ShapeDtypeStruct(s, d) for s, d in out_shapes],
        in_specs=[pl.BlockSpec(memory_space=pl.ANY)] * waits
        + [pl.BlockSpec(memory_space=pltpu.SMEM)] * smem
        + [place] * (len(args) - smem),
        out_specs=[place] * len(out_shapes),
        scratch_shapes=list(scratch),
        compiler_params=pltpu.CompilerParams(vmem_limit_bytes=56 * 1024 * 1024),
        cost_estimate=pl.CostEstimate(
            flops=int(COST.get(name, 2.0) * UNIT), bytes_accessed=0, transcendentals=0
        ),
        name=name,
    )(*after, *args)


def pack_kernel(q, k, v, o, a_ref):
    ot = nt(eye(q.shape[0]), o[...]).astype(BF16)
    a_ref[:, 0:128] = q[:, 0:128]
    a_ref[:, 128:256] = k[:, 0:128]
    a_ref[:, 256:384] = v[:, 0:128]
    a_ref[:, 384:512] = jnp.concatenate([q[:, 128:192], v[:, 128:192]], axis=1)
    a_ref[:, 512:640] = jnp.concatenate([k[:, 128:192], ot[:, 128:192]], axis=1)
    a_ref[:, 640:768] = ot[:, 0:128]


def stack_kernel(count, *refs):
    extra = (len(refs) - count - 1) // 2
    pieces, others, out, copies = refs[:count], refs[count : count + extra], refs[count + extra], refs[count + extra + 1 :]
    rows = pieces[0].shape[0]
    for k, piece in enumerate(pieces):
        out[k * rows : (k + 1) * rows, :] = piece[...]
    for src, dst in zip(others, copies):
        dst[...] = src[...]


def cut_kernel(a, b, out_a, out_b):
    cut = out_a.shape[0]
    out_a[...] = a[0:cut, :]
    out_b[...] = b[cut : 2 * cut, :]


def gate_kernel(token):
    token[...] = jnp.zeros_like(token)


def add_kernel(top, far_top, bottom, far_bottom, out_top, out_bottom):
    cut = far_top.shape[0]
    out_top[0:cut, :] = (top[0:cut, :].astype(F32) + far_top[...].astype(F32)).astype(BF16)
    out_top[cut:, :] = top[cut:, :]
    out_bottom[0:cut, :] = bottom[0:cut, :]
    out_bottom[cut:, :] = (bottom[cut:, :].astype(F32) + far_bottom[...].astype(F32)).astype(BF16)


def total_kernel(count, *refs):
    rows = refs[count].shape[0]
    for k, dst in enumerate(refs[count:]):
        at = slice(k * rows, (k + 1) * rows)
        value = refs[0][at, :].astype(F32)
        for other in refs[1:count]:
            value += other[at, :].astype(F32)
        dst[...] = value.astype(dst.dtype)


def total_vec_kernel(count, vec, *refs):
    vec_out, dsts = refs[count], refs[count + 1 :]
    rows, more = dsts[0].shape[0], vec.shape[0]
    total_kernel(count, *refs[:count], *(d.at[0:rows, :] for d in dsts))
    first = 4 * rows
    sums = vec[...]
    for other in refs[1:count]:
        sums += other[first : first + more, :].astype(F32) + other[first + more : first + 2 * more, :].astype(F32)
    vec_out[...] = sums
    high = sums.astype(BF16)
    low = (sums - high.astype(F32)).astype(BF16)
    for dst in dsts[1:]:
        dst[rows : rows + more, :] = high
        dst[rows + more : rows + 2 * more, :] = low


def finish_kernel(*refs):
    vec, (parts, (q, k, v, o, vec_out)) = refs[0], (refs[1:-5], refs[-5:])
    rows, more = parts[0].shape[0], vec.shape[0]
    total = parts[0][...]
    sums = vec[...]
    for part in parts[1:]:
        total += part[0:rows, :].astype(F32)
        sums += part[rows : rows + more, :].astype(F32) + part[rows + more : rows + 2 * more, :].astype(F32)
    vec_out[...] = sums
    q[...] = jnp.concatenate([total[:, 0:128], total[:, 384:448]], axis=1)
    k[...] = jnp.concatenate([total[:, 128:256], total[:, 512:576]], axis=1)
    v[...] = jnp.concatenate([total[:, 256:384], total[:, 448:512]], axis=1)
    out = jnp.concatenate([total[:, 640:768], total[:, 576:640]], axis=1)
    high = out.astype(BF16)
    low = (out - high.astype(F32)).astype(BF16)
    unit = eye(out.shape[1])
    o[...] = nt(unit, high) + nt(unit, low)


def place_of(depth, r, z, y, count):
    rel = lax.broadcasted_iota(jnp.int32, (count, 1), 0)
    half = count // 2
    ry = (rel >= half).astype(jnp.int32)
    rest = rel - ry * half
    rz = jnp.zeros_like(rel)
    for k in range(1, depth):
        rz += (rest >= k * r).astype(jnp.int32)
    az = z - rz
    az += depth * (az < 0).astype(jnp.int32)
    ay = y + ry - 2 * y * ry
    return az * (2 * r) + ay * r + rest - rz * r


def prep_kernel(
    depth, where, tok_o, tok_p, mem_o, mem_p, cot_o, cot_p, vec, patch, bias_o, bias_p,
    x_ref, xt_ref, tok_r, cot_r, cot_t, mem_r, vec_r, hot_ref, ok_ref, bias_ref, up_ref, unscaled,
):
    features = tok_o.shape[1]
    lane = lax.broadcasted_iota(jnp.int32, (features, features), 1)
    place = place_of(depth, features // (2 * depth), where[0], where[1], features)
    hot_ref[...] = (lane == place).astype(F32).astype(BF16)
    gain = vec[0:1, :].astype(F32)
    shift = vec[1:2, :].astype(F32)
    vec_r[...] = nt(vec[...], hot_ref[...])
    for m, bias in enumerate((bias_o, bias_p)):
        row = bias[...].astype(F32)
        bias_ref[m] = jnp.zeros_like(bias_ref[m])
        bias_ref[m, :, 0:128] = row[:, 0:128]
        bias_ref[m, :, 256:512] = row[:, 128:384]
        up_ref[m] = row[:, 384:]

    rows = lax.broadcasted_iota(jnp.int32, (SLOTS, PATCHES), 0)
    cols = lax.broadcasted_iota(jnp.int32, (SLOTS, PATCHES), 1)
    columns = nt((rows == cols).astype(F32), (patch[...] > 0).astype(F32))
    which = lax.broadcasted_iota(jnp.int32, columns.shape, 1)
    for at in range(2):
        one = jnp.sum(jnp.where(which == where[2 + at], columns, 0.0), axis=1, keepdims=True)
        ok_ref[at] = jnp.broadcast_to(one, (SLOTS, 128))

    for at, (mem, tok) in enumerate(((mem_o, tok_o), (mem_p, tok_p))):
        normed, _ = standard(tok[...].astype(F32))
        low = (normed * gain + shift).astype(BF16)
        x_ref[at, SLOTS:KEYS, :] = nt(low, hot_ref[...]).astype(BF16)
        unscaled[at, SLOTS:KEYS, :] = nt(normed.astype(BF16), hot_ref[...]).astype(BF16)
        xt_ref[:, at * KEYS + SLOTS : (at + 1) * KEYS] = nt(hot_ref[...], low).astype(BF16)
        normed, _ = standard(mem[...].astype(F32))
        normed = jnp.concatenate([normed, jnp.zeros((SLOTS - PATCHES, features), F32)], axis=0)
        unscaled[at, 0:SLOTS, :] = nt(normed.astype(BF16), hot_ref[...]).astype(BF16)
        low = (normed * gain + shift).astype(BF16)
        x_ref[at, 0:SLOTS, :] = nt(low, hot_ref[...]).astype(BF16)
        xt_ref[:, at * KEYS : at * KEYS + SLOTS] = nt(hot_ref[...], low).astype(BF16)
    raw = jnp.concatenate([mem_o[...].astype(F32), jnp.zeros((SLOTS - PATCHES, features), F32)], axis=0)
    mem_r[...] = nt(raw.astype(BF16), hot_ref[...]).astype(BF16)
    for at, (tok, cot) in enumerate(((tok_o, cot_o), (tok_p, cot_p))):
        rows = slice(at * TEXT, (at + 1) * TEXT)
        tok_r[rows, :] = nt(tok[...], hot_ref[...]).astype(BF16)
        cot_r[rows, :] = nt(cot[...], hot_ref[...]).astype(BF16)
        cot_t[:, rows] = nt(hot_ref[...], cot[...]).astype(BF16)


def masked(raw, cond):
    return jnp.where(cond, raw * SCALE, NEG)


def assemble(quads, w_ref):
    half = quads[0].shape[0]
    for k, quad in enumerate(quads):
        w_ref[k // 2, (k % 2) * half : (k % 2 + 1) * half, :] = quad[...]


def arrange(depth, where, whole, w_ref):
    rows = whole.shape[1]
    half = depth * rows
    x = where[4] // 2
    for m in range(2):
        for ry in range(2):
            for rz in range(depth):
                az = lax.rem(where[0] - rz + depth, depth)
                ay = where[1] if ry == 0 else 1 - where[1]
                ax = x if m == 0 else 1 - x
                first = ry * half + rz * rows
                w_ref[m, first : first + rows, :] = whole[(az * 2 + ay) * 2 + ax]


def attend_kernel(
    where, split, length,
    own, own_y, peer, far_top, far_bottom, x_ref, bias, ok_ref,
    w_ref, y_ref, p_ref, ctx_ref, part_ref, out_ref,
):
    assemble((own, own_y, peer), w_ref)
    half, cut = own.shape[0], far_top.shape[0]
    w_ref[1, half : half + cut, :] = far_top[...]
    w_ref[1, half + cut : 2 * half, :] = far_bottom[...]
    lane = lax.broadcasted_iota(jnp.int32, (TEXT, 128), 1)
    lane_k = lax.broadcasted_iota(jnp.int32, (KEYS, 128), 1)
    zero = jnp.zeros((TEXT, 128), BF16)
    unit = eye(128)
    unit_t = eye(TEXT)
    key_place = lax.broadcasted_iota(jnp.int32, (TEXT, TEXT), 0)
    query_place = lax.broadcasted_iota(jnp.int32, (TEXT, TEXT), 1)
    out_ref[...] = jnp.zeros_like(out_ref)

    def step(at, carry):
        e, m = at // 2, at % 2
        x = x_ref[e]
        w = w_ref[m]
        b = bias[m]
        y1 = nn(x, w[:, 0:384]) + b[:, 0:384]
        y_ref[m, e, :, 0:384] = y1.astype(BF16)
        y2 = nn(x, w[:, 384:640]) + b[:, 384:640]
        y_ref[m, e, :, 384:512] = y2[:, 0:128].astype(BF16)
        y_ref[m, e, :, 512:640] = jnp.where(lane_k < HEAD, y2[:, 128:256], 0.0).astype(BF16)

        patch_ok = jnp.concatenate([ok_ref[e], ok_ref[e]], axis=1) > 0.0
        prefix, valid = split[where[2 + e]], length[where[2 + e]]
        text_ok = ((key_place < prefix) | (key_place <= query_place)) & (key_place < valid)

        q01 = y_ref[m, e, SLOTS:KEYS, 0:128]
        q2 = y_ref[m, e, SLOTS:KEYS, 384:512]
        v01t = nt(unit, y_ref[m, e, :, 256:384]).astype(BF16)
        v2t = nt(unit, y_ref[m, e, :, 384:512]).astype(BF16)
        ctx01 = []
        for head in range(3):
            if head == 0:
                q, first, vt = jnp.where(lane < HEAD, q01, zero), 128, v01t[0:HEAD]
            elif head == 1:
                q, first, vt = jnp.where(lane >= HEAD, q01, zero), 128, v01t[HEAD:128]
            else:
                q, first, vt = jnp.where(lane < HEAD, q2, zero), 512, v2t[HEAD:128]
            s_mem = masked(nt(y_ref[m, e, 0:SLOTS, first : first + 128], q), patch_ok)
            s_text = masked(nt(y_ref[m, e, SLOTS:KEYS, first : first + 128], q), text_ok)
            largest = jnp.maximum(
                jnp.max(s_mem, axis=0, keepdims=True), jnp.max(s_text, axis=0, keepdims=True)
            )
            e_mem = jnp.exp(s_mem - largest)
            e_text = jnp.exp(s_text - largest)
            total = jnp.sum(e_mem, axis=0, keepdims=True) + jnp.sum(e_text, axis=0, keepdims=True)
            inverse = 1.0 / total
            p_mem = (e_mem * inverse).astype(BF16)
            p_text = (e_text * inverse).astype(BF16)
            p_ref[m, e, head, 0:SLOTS, :] = p_mem
            p_ref[m, e, head, SLOTS:KEYS, :] = p_text
            ctx01.append(nn(vt[:, 0:SLOTS], p_mem) + nn(vt[:, SLOTS:KEYS], p_text))
        c01t = jnp.concatenate([ctx01[0], ctx01[1]], axis=0).astype(BF16)
        c2t = jnp.concatenate([jnp.zeros((HEAD, TEXT), F32), ctx01[2]], axis=0).astype(BF16)
        c01 = nt(unit_t, c01t).astype(BF16)
        c2 = nt(unit_t, c2t).astype(BF16)
        ctx_ref[m, e, :, 0:128] = c01
        ctx_ref[m, e, :, 128:256] = c2
        out_ref[e] += nt(c01, w[:, 640:768]) + nt(c2, w[:, 512:640])
        return carry

    lax.fori_loop(0, 4, step, 0)
    part_ref[...] = out_ref[...].astype(BF16)


def gelu_pair(v):
    c = 0.7978845608028654
    square = v * v
    t = jnp.tanh(c * v * (1.0 + 0.044715 * square))
    gelu = 0.5 * v * (1.0 + t)
    slope = 0.5 * (1.0 + t) + 0.5 * v * (1.0 - t * t) * (c * (1.0 + 3 * 0.044715 * square))
    return gelu, slope


def up_kernel(
    depth, where, part, part_in, tok_r, vec_r, cot_t, bias, whole,
    res_ref, mid_t, hid_ref, slope_ref, g00, g01, g10, g11_top, g11_bottom, mid_ref, u_ref,
):
    half = g00.shape[0]
    arrange(depth, where, whole, u_ref)
    for e in range(2):
        rows = slice(e * TEXT, (e + 1) * TEXT)
        res = (
            tok_r[rows, :].astype(F32)
            + (part[e].astype(F32) + part_in[1 - e].astype(F32))
            + vec_r[4:5, :]
        )
        res_ref[rows, :] = res
        normed, _ = standard(res)
        mid_ref[rows, :] = (normed * vec_r[2:3, :] + vec_r[3:4, :]).astype(BF16)
    mid_t[...] = nt(eye(mid_ref.shape[1]), mid_ref[...]).astype(BF16)
    for m in range(2):
        for e in range(2):
            rows = slice(e * TEXT, (e + 1) * TEXT)
            pre = nn(mid_ref[rows, :], u_ref[m]) + bias[m]
            gelu, slope = gelu_pair(pre)
            hid_ref[m, rows, :] = gelu.astype(BF16)
            slope_ref[m, rows, :] = slope.astype(BF16)
    for dst, m, first in (
        (g11_top, 1, half), (g11_bottom, 1, half + half // 2), (g01, 0, half), (g10, 1, 0), (g00, 0, 0)
    ):
        dst[...] = nn(cot_t[first : first + dst.shape[0], :], hid_ref[m]).astype(BF16)


def down_kernel(
    depth, where, whole, hid_ref, slope_ref, mid_t, cot_r, w0, w1, w2, w3,
    out_o, grad_ref, bias_ref, g00, g01, g10, g11_top, g11_bottom, d_ref, pre_ref, u_ref,
):
    half = g00.shape[0]
    arrange(depth, where, whole, u_ref)
    assemble((w0, w1, w2, w3), d_ref)
    bias_ref[...] = jnp.zeros_like(bias_ref)
    for m in range(2):
        for e in range(2):
            rows = slice(e * TEXT, (e + 1) * TEXT)
            pre = (nn(cot_r[rows, :], d_ref[m]) * slope_ref[m, rows, :].astype(F32)).astype(BF16)
            pre_ref[m, rows, :] = pre
            bias_ref[m : m + 1, :] += jnp.sum(pre.astype(F32), axis=0, keepdims=True)
    for e in range(2):
        rows = slice(e * TEXT, (e + 1) * TEXT)
        grad_ref[e] = (nt(pre_ref[0, rows, :], u_ref[0]) + nt(pre_ref[1, rows, :], u_ref[1])).astype(BF16)
    for e, out in enumerate((out_o, grad_ref.at[2])):
        rows = slice(e * TEXT, (e + 1) * TEXT)
        out[...] = (nt(hid_ref[0, rows, :], d_ref[0]) + nt(hid_ref[1, rows, :], d_ref[1])).astype(BF16)
    for dst, m, first in (
        (g11_top, 1, half), (g11_bottom, 1, half + half // 2), (g01, 0, half), (g10, 1, 0), (g00, 0, 0)
    ):
        dst[...] = nn(mid_t[first : first + dst.shape[0], :], pre_ref[m]).astype(BF16)


def attend_back_kernel(
    where, grad, grad_in, res_ref, cot_r, vec_r, w_ref, y_ref, p_ref, unscaled, up_bias,
    rg_ref, agt_ref, dy_ref, back_o, back_p, sums, bias_ref, ag_ref, back_ref,
):
    lane = lax.broadcasted_iota(jnp.int32, (TEXT, 128), 1)
    row = lax.broadcasted_iota(jnp.int32, (128, TEXT), 0)
    zero = jnp.zeros((TEXT, 128), BF16)
    unit = eye(128)
    unit_t = eye(TEXT)
    for e in range(2):
        rows = slice(e * TEXT, (e + 1) * TEXT)
        mid_grad = grad[e].astype(F32) + grad_in[1 - e].astype(F32)
        normed, inverse = standard(res_ref[rows, :])
        cot = cot_r[rows, :].astype(F32)
        resid = cot + standard_back(normed, inverse, mid_grad, vec_r[2:3, :])
        low = resid.astype(BF16)
        ag_ref[rows, :] = low
        if e == 0:
            rg_ref[...] = resid
            sums[0:1, :] = jnp.sum(mid_grad * normed, axis=0, keepdims=True)
            sums[1:2, :] = jnp.sum(mid_grad, axis=0, keepdims=True)
            sums[2:3, :] = jnp.sum(low.astype(F32), axis=0, keepdims=True)
            sums[3:4, :] = jnp.sum(cot, axis=0, keepdims=True)
            sums[4:8, :] = jnp.zeros_like(sums[4:8, :])
    agt_ref[...] = nt(eye(ag_ref.shape[1]), ag_ref[...]).astype(BF16)
    bias_ref[...] = jnp.zeros_like(bias_ref)
    back_ref[...] = jnp.zeros_like(back_ref)

    def step(at, carry):
        e, m = at // 2, at % 2
        w = w_ref[m]
        ag = ag_ref[pl.ds(pl.multiple_of(e * TEXT, TEXT), TEXT), :]
        dc01 = nn(ag, w[:, 640:768]).astype(BF16)
        dc2 = nn(ag, w[:, 512:640]).astype(BF16)
        q01 = y_ref[m, e, SLOTS:KEYS, 0:128]
        q2 = y_ref[m, e, SLOTS:KEYS, 384:512]
        k01 = y_ref[m, e, :, 128:256]
        k2 = y_ref[m, e, :, 512:640]
        k01t = nt(unit, k01).astype(BF16)
        k2t = nt(unit, k2).astype(BF16)
        dk, dv, dqt = [], [], []
        for head in range(3):
            keep = (lane < HEAD) if head == 0 else (lane >= HEAD)
            if head < 2:
                dc = jnp.where(keep, dc01, zero)
                q = jnp.where(keep, q01, zero)
                v = y_ref[m, e, :, 256:384]
                kt = k01t[0:HEAD] if head == 0 else k01t[HEAD:128]
            else:
                dc = jnp.where(lane >= HEAD, dc2, zero)
                q = jnp.where(lane < HEAD, q2, zero)
                v = y_ref[m, e, :, 384:512]
                kt = k2t[0:HEAD]
            prob = p_ref[m, e, head]
            probs = prob.astype(F32)
            grad_p = nt(v, dc)
            dot = jnp.sum(probs * grad_p, axis=0, keepdims=True)
            score = (probs * (grad_p - dot)).astype(BF16)
            dk.append(nn(score, q))
            dv.append(nn(prob, dc))
            dqt.append(nn(kt, score))
        dk01 = ((dk[0] + dk[1]) * SCALE).astype(BF16)
        dk2 = (dk[2] * SCALE).astype(BF16)
        dv01 = (dv[0] + dv[1]).astype(BF16)
        dv2 = dv[2].astype(BF16)
        dq01 = nt(unit_t, (jnp.concatenate([dqt[0], dqt[1]], axis=0) * SCALE).astype(BF16))
        dq2 = nt(
            unit_t,
            (jnp.concatenate([dqt[2], jnp.zeros((HEAD, TEXT), F32)], axis=0) * SCALE).astype(BF16),
        )
        dy_ref[m, e, 0:SLOTS, 0:128] = zero
        dy_ref[m, e, SLOTS:KEYS, 0:128] = dq01.astype(BF16)
        dy_ref[m, e, :, 128:256] = dk01
        dy_ref[m, e, :, 256:384] = dv01
        dy_ref[m, e, 0:SLOTS, 384:512] = dv2[0:SLOTS]
        dy_ref[m, e, SLOTS:KEYS, 384:512] = (dq2 + dv2[SLOTS:KEYS].astype(F32)).astype(BF16)
        dy_ref[m, e, :, 512:640] = dk2
        dy = dy_ref[m, e]
        bias_ref[m] += jnp.sum(dy.astype(F32), axis=0, keepdims=True)
        back_ref[e] += nt(dy, w[:, 0:640])
        return carry

    lax.fori_loop(0, 4, step, 0)
    back_o[...] = back_ref[0]
    back_p[0:KEYS, :] = back_ref[1].astype(BF16)
    for e in range(2):
        sums[4:5, :] += jnp.sum(back_ref[e] * unscaled[e].astype(F32), axis=0, keepdims=True)
        sums[5:6, :] += jnp.sum(back_ref[e], axis=0, keepdims=True)
    index = lax.broadcasted_iota(jnp.int32, (4, 1), 0)
    own, peer = index == where[4], index == where[5]
    sums[8:12, 0:640] = jnp.where(own, bias_ref[0], 0.0) + jnp.where(peer, bias_ref[1], 0.0)
    sums[8:12, 640:768] = jnp.zeros((4, 128), F32)
    sums[12:16, :] = jnp.where(own, up_bias[0:1, :], 0.0) + jnp.where(peer, up_bias[1:2, :], 0.0)
    high = sums[...].astype(BF16)
    back_p[KEYS : KEYS + 16, :] = high
    back_p[KEYS + 16 : KEYS + 32, :] = (sums[...] - high.astype(F32)).astype(BF16)


def weight_kernel(
    xt_ref, agt_ref, dy_ref, ctx_ref, sums, back_in, hot_ref, g00, g01, g10, g11, vec_ref,
):
    half = g00.shape[0]
    more = vec_ref.shape[0]
    vec = sums[...] + back_in[KEYS : KEYS + more, :].astype(F32) + back_in[KEYS + more :, :].astype(F32)
    vec_ref[...] = vec
    vec_ref[0:8, :] = restore(vec[0:8, :], hot_ref[...])
    high = vec_ref[...].astype(BF16)
    low = (vec_ref[...] - high.astype(F32)).astype(BF16)
    for dst in (g01, g10, g11):
        dst[half : half + more, :] = high
        dst[half + more : half + 2 * more, :] = low
    for dst, m, first in ((g11, 1, half), (g01, 0, half), (g10, 1, 0), (g00, 0, 0)):
        rows = slice(first, first + half)
        dy = dy_ref[m].reshape(2 * KEYS, 640)
        ctx = ctx_ref[m].reshape(2 * TEXT, 256)
        grad = nn(xt_ref[rows, :], dy)
        out = nn(agt_ref[rows, :], ctx)
        dst[0:half, 0:512] = grad[:, 0:512].astype(BF16)
        dst[0:half, 512:640] = (grad[:, 512:640] + out[:, 128:256]).astype(BF16)
        dst[0:half, 640:768] = out[:, 0:128].astype(BF16)


def restore(v, hot):
    high = v.astype(BF16)
    low = (v - high.astype(F32)).astype(BF16)
    return nn(high, hot) + nn(low, hot)


def last_kernel(
    back_o, back_in, tok_r, mem_r, rg_ref, res_ref, out_o, out_in, vec_r, hot_ref,
    layer_ref, in_ref, mem_ref,
):
    hot = hot_ref[...]
    gain = vec_r[0:1, :]
    layer = (
        res_ref[0:TEXT, :] + (out_o[...].astype(F32) + out_in[2].astype(F32)) + vec_r[5:6, :]
    ).astype(BF16)
    layer_ref[...] = nn(layer, hot).astype(BF16)
    mem_back = back_o[0:SLOTS, :] + back_in[0:SLOTS, :].astype(F32)
    text_back = back_o[SLOTS:KEYS, :] + back_in[SLOTS:KEYS, :].astype(F32)
    normed, inverse = standard(tok_r[0:TEXT, :].astype(F32))
    in_ref[...] = restore(rg_ref[...] + standard_back(normed, inverse, text_back, gain), hot)
    normed, inverse = standard(mem_r[...].astype(F32))
    mem_ref[...] = restore(standard_back(normed, inverse, mem_back, gain), hot)[0:PATCHES, :]


class Links:
    def __init__(self, dp, mp):
        self.dp, self.mp, self.depth = dp, mp, dp // 2
        self.x = self.pairs(lambda d, m: (d, m ^ 2))
        self.c = self.pairs(lambda d, m: (d, m ^ 1))
        self.y = self.pairs(lambda d, m: (d ^ 1, m))
        self.xy = self.pairs(lambda d, m: (d ^ 1, m ^ 2))

    def pairs(self, to):
        out = []
        for d in range(self.dp):
            for m in range(self.mp):
                d2, m2 = to(d, m)
                out.append((d * self.mp + m, d2 * self.mp + m2))
        return out

    def z(self, k):
        return self.pairs(lambda d, m: ((((d // 2 + k) % self.depth) * 2 + d % 2), m))

    def send(self, a, pairs):
        return lax.ppermute(a, AXES, pairs)

    def line(self, shard, *others, after=()):
        if self.depth == 4:
            pieces = [shard] + [self.send(shard, self.z(k)) for k in range(1, 4)]
            rows, lanes = shard.shape
            return call(
                functools.partial(stack_kernel, 4),
                [((4 * rows, lanes), BF16)] + [(o.shape, BF16) for o in others],
                *pieces, *others, after=after,
            )
        held = shard[None]
        step = 1
        while step < self.depth:
            held = jnp.concatenate([held, self.send(held, self.z(step))], axis=0)
            step *= 2
        return (held.reshape(-1, shard.shape[1]),) + others

    def home(self, after, *parts):
        rows, lanes = parts[0].shape
        if self.depth == 4:
            r = rows // 4
            own, *rest = call(
                functools.partial(total_kernel, len(parts)),
                [((r, lanes), F32)] + [((r, lanes), BF16)] * 3, *parts, after=after,
            )
            return [own] + [self.send(rest[k], self.z(-k - 1)) for k in range(3)]
        held = sum(p.astype(F32) for p in parts).reshape(self.depth, -1, lanes)
        step = self.depth // 2
        while step >= 1:
            held = held[:step] + self.send(held[step:].astype(BF16), self.z(-step)).astype(F32)
            step //= 2
        return [held[0]]

    def meet(self, after, g01, g10, far_top, far_bottom):
        to_y, to_x = call(
            add_kernel, [(g01.shape, BF16), (g10.shape, BF16)], g01, far_top, g10, far_bottom, after=after
        )
        return self.send(to_y, self.y), self.send(to_x, self.x), to_x

    def direct(self, g01, g10, g11):
        return self.send(g11, self.xy), self.send(g01, self.y), self.send(g10, self.x)

    def fold(self, after, *parts):
        if self.depth != 4:
            return self.home(after, *parts)[0], None
        rows, lanes = parts[0].shape
        near, far = call(
            functools.partial(total_kernel, len(parts)),
            [((rows // 2, lanes), F32), ((rows // 2, lanes), BF16)], *parts, after=after,
        )
        return near, self.send(far, self.z(-2))

    def fold_more(self, after, near, far):
        if self.depth != 4:
            return [near]
        rows, lanes = near.shape
        own, other = call(
            functools.partial(total_kernel, 2),
            [((rows // 2, lanes), F32), ((rows // 2, lanes), BF16)], near, far, after=after,
        )
        return [own, self.send(other, self.z(-1))]

    def home_with(self, after, vec, own, *got):
        rows, lanes = own.shape
        more = vec.shape[0]
        if self.depth == 4:
            r = rows // 4
            vec, own, *rest = call(
                functools.partial(total_vec_kernel, 1 + len(got)),
                [(vec.shape, F32), ((r, lanes), F32)] + [((r + 2 * more, lanes), BF16)] * 3,
                vec, own, *got, after=after,
            )
            return [vec, own] + [self.send(rest[k], self.z(-k - 1)) for k in range(3)]
        for g in got:
            vec = vec + g[rows : rows + more].astype(F32) + g[rows + more :].astype(F32)
        step = 1
        while step < self.depth:
            vec = vec + self.send(vec, self.z(step))
            step *= 2
        return [vec] + self.home((), own, *(g[:rows] for g in got))


def add_up(parts):
    total = parts[0]
    for part in parts[1:]:
        total = total + part.astype(F32)
    return total


def per_device(
    tokens, memory, split_point, text_length, patch_mask,
    query_weight, query_bias, key_weight, value_weight, value_bias,
    out_weight, out_bias, attn_gain, attn_shift, mlp_gain, mlp_shift,
    up_weight, up_bias, down_weight, down_bias, cotangent,
):
    features = tokens.shape[1]
    width = query_weight.shape[1]
    hidden = up_weight.shape[1]
    dp, mp = lax.axis_size("dp"), lax.axis_size("mp")
    links = Links(dp, mp)
    dp_at, mp_at = lax.axis_index("dp"), lax.axis_index("mp")
    r = features // dp
    half = features // 2

    sides = [[d * mp + 2 * i + c for d in range(dp) for i in range(mp // 2)] for c in range(2)]
    up_all = lax.all_gather(up_weight, AXES, axis=0, axis_index_groups=sides)

    biases = jnp.concatenate(
        [query_bias[:128], value_bias[:128], query_bias[128:], value_bias[128:], up_bias]
    ).reshape(1, -1)
    biases_x = links.send(biases, links.x)
    tok_p = links.send(tokens, links.c)
    mem_p = links.send(memory, links.c)
    cot_p = links.send(cotangent, links.c)
    (attn_own,) = call(
        pack_kernel, [((r, features), BF16)], query_weight, key_weight, value_weight, out_weight
    )

    where = jnp.stack([dp_at // 2, dp_at % 2, mp_at, mp_at ^ 1, mp_at, mp_at ^ 2]).astype(jnp.int32)
    blank = jnp.zeros_like(attn_gain)
    vec = jnp.stack(
        [attn_gain, attn_shift, mlp_gain, mlp_shift, out_bias, down_bias] + [blank] * 10
    )
    x, xt, tok_r, cot_r, cot_t, mem_r, vec_r, hot, ok, bias, ub, unscaled = call(
        functools.partial(prep_kernel, dp // 2),
        [
            ((2, KEYS, features), BF16), ((features, 2 * KEYS), BF16),
            ((2 * TEXT, features), BF16), ((2 * TEXT, features), BF16), ((features, 2 * TEXT), BF16),
            ((SLOTS, features), BF16), ((16, features), F32), ((features, features), BF16),
            ((2, SLOTS, 128), F32), ((2, 1, 640), F32), ((2, 1, hidden), F32),
            ((2, KEYS, features), BF16),
        ],
        where, tokens, tok_p, memory, mem_p, cotangent, cot_p, vec, patch_mask, biases, biases_x,
        smem=1, after=(attn_own,),
    )
    own, down_own = links.line(attn_own, down_weight.T, after=(ok,))
    own_y, peer = links.send(own, links.y), links.send(own, links.x)
    cut_y, cut_x = call(cut_kernel, [((half // 2, features), BF16)] * 2, own_y, peer)
    far_top, far_bottom = links.send(cut_y, links.x), links.send(cut_x, links.y)
    (down_rows,) = links.line(down_own, after=(cut_x,))
    quads_d = [
        down_rows, links.send(down_rows, links.y), links.send(down_rows, links.x), links.send(down_rows, links.xy)
    ]

    w, y, p, ctx, part = call(
        attend_kernel,
        [
            ((2, features, features), BF16), ((2, 2, KEYS, 640), BF16), ((2, 2, 3, KEYS, TEXT), BF16),
            ((2, 2, TEXT, 256), BF16), ((2, TEXT, features), BF16),
        ],
        where, split_point, text_length, own, own_y, peer, far_top, far_bottom,
        x, bias, ok,
        smem=3, scratch=[pltpu.VMEM((2, TEXT, features), F32)], after=(down_rows,),
    )
    part_in = links.send(part, links.c)
    (token,) = call(gate_kernel, [((8, 128), F32)], after=(part, *quads_d[1:]))

    quarter = ((half, hidden), BF16)
    eighth = ((half // 2, hidden), BF16)
    res, mid_t, hid, slope, d00, d01, d10, d11t, d11b = call(
        functools.partial(up_kernel, dp // 2),
        [
            ((2 * TEXT, features), F32), ((features, 2 * TEXT), BF16),
            ((2, 2 * TEXT, hidden), BF16), ((2, 2 * TEXT, hidden), BF16),
        ]
        + [quarter] * 3 + [eighth] * 2,
        where, part, part_in, tok_r, vec_r, cot_t, ub, up_all, smem=1, after=(token,),
        scratch=[pltpu.VMEM((2 * TEXT, features), BF16), pltpu.VMEM((2, features, hidden), BF16)],
    )
    d_far = links.send(d11t, links.x), links.send(d11b, links.y)

    layer_o, mid_grad, up_bias_part, u00, u01, u10, u11t, u11b = call(
        functools.partial(down_kernel, dp // 2),
        [((TEXT, features), BF16), ((3, TEXT, features), BF16), ((2, hidden), F32)]
        + [quarter] * 3 + [eighth] * 2,
        where, up_all, hid, slope, mid_t, cot_r, *quads_d, smem=1,
        scratch=[
            pltpu.VMEM((2, features, hidden), BF16), pltpu.VMEM((2, 2 * TEXT, hidden), BF16),
            pltpu.VMEM((2, features, hidden), BF16),
        ],
    )
    grad_in = links.send(mid_grad, links.c)
    d_y, d_x, token = links.meet((mid_grad,), d01, d10, *d_far)
    u_far = links.send(u11t, links.x), links.send(u11b, links.y)

    rg, ag_t, dy, back_o, back_p, sums = call(
        attend_back_kernel,
        [
            ((TEXT, features), F32), ((features, 2 * TEXT), BF16), ((2, 2, KEYS, 640), BF16),
            ((KEYS, features), F32), ((KEYS + 32, features), BF16), ((16, features), F32),
        ],
        where, mid_grad, grad_in, res, cot_r, vec_r, w, y, p, unscaled, up_bias_part, smem=1, after=(token,),
        scratch=[
            pltpu.VMEM((2, 1, 640), F32), pltpu.VMEM((2 * TEXT, features), BF16), pltpu.VMEM((2, KEYS, features), F32)
        ],
    )
    back_in = links.send(back_p, links.c)
    u_y, u_x, token = links.meet((dy, d_y, d_x), u01, u10, *u_far)
    a00, a01, a10, a11, stack = call(
        weight_kernel,
        [((half, features), BF16)] + [((half + 32, features), BF16)] * 3 + [((16, features), F32)],
        xt, ag_t, dy, ctx, sums, back_in, hot, after=(token,),
    )
    a_got = links.direct(a01, a10, a11)
    down_total, down_more = links.fold((a00,), d00, d_y, d_x)
    layer_out, input_grad, memory_grad = call(
        last_kernel,
        [((TEXT, features), BF16), ((TEXT, features), F32), ((PATCHES, features), F32)],
        back_o, back_in, tok_r, mem_r, rg, res, layer_o, grad_in, vec_r, hot, after=(down_total,),
    )
    down_parts = links.fold_more((input_grad,), down_total, down_more)
    up_total, up_more = links.fold((down_parts[0],), u00, u_y, u_x)
    up_parts = links.fold_more((), up_total, up_more)
    attn_parts = links.home_with((up_parts[0],), stack, a00, *a_got)
    query_sum, key_sum, value_sum, out_sum, stack = call(
        finish_kernel,
        [((r, width), F32)] * 3 + [((width, r), F32), (stack.shape, F32)], *attn_parts,
    )

    at = dp_at * mp + mp_at
    few = features // (dp * mp)
    q_bias = jnp.concatenate([stack[8:12, 0:128], stack[8:12, 384:448]], axis=1).reshape(1, features)
    v_bias = jnp.concatenate([stack[8:12, 256:384], stack[8:12, 448:512]], axis=1).reshape(1, features)
    vectors = lax.dynamic_slice(jnp.concatenate([stack[0:6], q_bias, v_bias]), (0, at * few), (8, few))
    many = up_bias.shape[0] // dp
    up_bias_sum = lax.dynamic_slice(stack[12:16].reshape(-1), (at * many,), (many,))

    return (
        layer_out, input_grad, memory_grad,
        query_sum, key_sum, value_sum, out_sum, add_up(up_parts), add_up(down_parts).T,
        vectors[6], vectors[7], up_bias_sum,
        vectors[2], vectors[3], vectors[4], vectors[5], vectors[0], vectors[1],
    )


def solution(mesh):
    rows = P(AXES, None)
    flat = P(AXES)
    in_specs = (
        rows, rows, P("dp"), P("dp"), P("dp", None),
        P("dp", "mp"), P("mp"), P("dp", "mp"), P("dp", "mp"), P("mp"),
        P("mp", "dp"), P(), P(), P(), P(), P(),
        P("dp", "mp"), P("mp"), P("mp", "dp"), P(), rows,
    )
    out_specs = (
        rows, rows, rows,
        P("dp", "mp"), P("dp", "mp"), P("dp", "mp"), P("mp", "dp"), P("dp", "mp"), P("mp", "dp"),
    ) + (flat,) * 9
    return jax.shard_map(
        per_device, mesh=mesh, in_specs=in_specs, out_specs=out_specs, check_vma=False
    )
```

```python
import functools

import jax
import jax.numpy as jnp
from jax import lax
from jax.experimental import pallas as pl
from jax.experimental.pallas import tpu as pltpu
from jax.sharding import PartitionSpec as P

HEAD = 64
TEXT = 256
PATCHES = 196
SLOTS = 256
KEYS = SLOTS + TEXT
EPS = 1e-06
NEG = -1000000000.0
SCALE = HEAD ** (-0.5)
F32 = jnp.float32
BF16 = jnp.bfloat16
AXES = ("dp", "mp")

CUT = 384


def nn(a, b):
    return lax.dot_general(a, b, (((1,), (0,)), ((), ())), preferred_element_type=F32)


def nt(a, b):
    return lax.dot_general(a, b, (((1,), (1,)), ((), ())), preferred_element_type=F32)


def eye(n):
    rows = lax.broadcasted_iota(jnp.int32, (n, n), 0)
    cols = lax.broadcasted_iota(jnp.int32, (n, n), 1)
    return (rows == cols).astype(F32).astype(BF16)


def standard(matrix):
    average = jnp.mean(matrix, axis=-1, keepdims=True)
    centered = matrix - average
    inverse = lax.rsqrt(jnp.mean(centered * centered, axis=-1, keepdims=True) + EPS)
    return centered * inverse, inverse


def standard_back(normed, inverse, grad_out, gain):
    scaled = grad_out * gain
    return inverse * (
        scaled
        - jnp.mean(scaled, axis=-1, keepdims=True)
        - normed * jnp.mean(scaled * normed, axis=-1, keepdims=True)
    )


UNIT = 1e9
COST = {
    "prep_kernel": 8.0, "attend_kernel": 17.0, "up_kernel": 9.0, "down_kernel": 9.0,
    "gate_kernel": 12.0, "add_kernel": 30.0, "turn_kernel": 30.0, "attend_back_kernel": 19.0, "weight_kernel": 6.0, "last_kernel": 6.0,
}


ROOM = {
    "prep_kernel": 24, "attend_kernel": 26, "up_kernel": 26, "down_kernel": 26,
    "attend_back_kernel": 26, "weight_kernel": 20, "last_kernel": 16,
}


def call(kernel, out_shapes, *args, scratch=(), smem=0, after=(), anywhere=False):
    name = getattr(kernel, "func", kernel).__name__
    waits = len(after)

    def body(*refs):
        return kernel(*refs[waits:])

    place = pl.BlockSpec(memory_space=pl.ANY if anywhere else pltpu.VMEM)
    return pl.pallas_call(
        body,
        out_shape=[jax.ShapeDtypeStruct(s, d) for s, d in out_shapes],
        in_specs=[pl.BlockSpec(memory_space=pl.ANY)] * waits
        + [pl.BlockSpec(memory_space=pltpu.SMEM)] * smem
        + [place] * (len(args) - smem),
        out_specs=[place] * len(out_shapes),
        scratch_shapes=list(scratch),
        compiler_params=pltpu.CompilerParams(vmem_limit_bytes=ROOM.get(name, 8) * 1024 * 1024),
        cost_estimate=pl.CostEstimate(
            flops=int(COST.get(name, 2.0) * UNIT), bytes_accessed=0, transcendentals=0
        ),
        name=name,
    )(*after, *args)


def pack_kernel(q, k, v, o, a_ref):
    ot = nt(eye(q.shape[0]), o[...]).astype(BF16)
    a_ref[:, 0:128] = q[:, 0:128]
    a_ref[:, 128:256] = k[:, 0:128]
    a_ref[:, 256:384] = v[:, 0:128]
    a_ref[:, 384:512] = jnp.concatenate([q[:, 128:192], v[:, 128:192]], axis=1)
    a_ref[:, 512:640] = jnp.concatenate([k[:, 128:192], ot[:, 128:192]], axis=1)
    a_ref[:, 640:768] = ot[:, 0:128]


def bias_kernel(qb, vb, ub, bias_ref):
    blank = jnp.zeros((1, 128), F32)
    qf, vf = qb[...].astype(F32), vb[...].astype(F32)
    row = jnp.concatenate(
        [qf[:, 0:128], blank, vf[:, 0:128], qf[:, 128:192], vf[:, 128:192], blank, blank], axis=1
    )
    rest = jnp.zeros((14, row.shape[1]), F32)
    bias_ref[...] = jnp.concatenate([row, ub[...].astype(F32), rest], axis=0).astype(BF16)


def stack_kernel(count, *refs):
    pieces, other, out, copy = refs[:count], refs[count], refs[count + 1], refs[count + 2]
    first = 0
    for piece in pieces:
        out[first : first + piece.shape[0], :] = piece[...]
        first += piece.shape[0]
    copy[...] = other[...]


def gate_kernel(token):
    token[...] = jnp.zeros_like(token)


def add_kernel(top, far_top, bottom, far_bottom, out_top, out_bottom):
    cut = far_top.shape[0]
    out_top[0:cut, :] = (top[0:cut, :].astype(F32) + far_top[...].astype(F32)).astype(BF16)
    out_top[cut:, :] = top[cut:, :]
    out_bottom[0:cut, :] = bottom[0:cut, :]
    out_bottom[cut:, :] = (bottom[cut:, :].astype(F32) + far_bottom[...].astype(F32)).astype(BF16)


def turn_kernel(top, far_top, bottom, far_bottom, a, b, c, out_top, out_bottom, near, far):
    add_kernel(top, far_top, bottom, far_bottom, out_top, out_bottom)
    total_kernel(3, a, b, c, near, far)


def total_kernel(count, *refs):
    rows = refs[count].shape[0]
    for k, dst in enumerate(refs[count:]):
        at = slice(k * rows, (k + 1) * rows)
        value = refs[0][at, :].astype(F32)
        for other in refs[1:count]:
            value += other[at, :].astype(F32)
        dst[...] = value.astype(dst.dtype)


def total_vec_kernel(count, vec, *refs):
    vec_out, dsts = refs[count], refs[count + 1 :]
    rows, more = dsts[0].shape[0], vec.shape[0]
    total_kernel(count, *refs[:count], *(d.at[0:rows, :] for d in dsts))
    first = 4 * rows
    sums = vec[...]
    for other in refs[1:count]:
        sums += other[first : first + more, :].astype(F32) + other[first + more : first + 2 * more, :].astype(F32)
    vec_out[...] = sums
    high = sums.astype(BF16)
    low = (sums - high.astype(F32)).astype(BF16)
    for dst in dsts[1:]:
        dst[rows : rows + more, :] = high
        dst[rows + more : rows + 2 * more, :] = low


def finish_kernel(*refs):
    vec, (parts, (q, k, v, o, vec_out)) = refs[0], (refs[1:-5], refs[-5:])
    rows, more = parts[0].shape[0], vec.shape[0]
    total = parts[0][...]
    sums = vec[...]
    for part in parts[1:]:
        total += part[0:rows, :].astype(F32)
        sums += part[rows : rows + more, :].astype(F32) + part[rows + more : rows + 2 * more, :].astype(F32)
    vec_out[...] = sums
    q[...] = jnp.concatenate([total[:, 0:128], total[:, 384:448]], axis=1)
    k[...] = jnp.concatenate([total[:, 128:256], total[:, 512:576]], axis=1)
    v[...] = jnp.concatenate([total[:, 256:384], total[:, 448:512]], axis=1)
    out = jnp.concatenate([total[:, 640:768], total[:, 576:640]], axis=1)
    high = out.astype(BF16)
    low = (out - high.astype(F32)).astype(BF16)
    unit = eye(out.shape[1])
    o[...] = nt(unit, high) + nt(unit, low)


def place_of(depth, r, z, y, count):
    rel = lax.broadcasted_iota(jnp.int32, (count, 1), 0)
    half = count // 2
    ry = (rel >= half).astype(jnp.int32)
    rest = rel - ry * half
    rz = jnp.zeros_like(rel)
    for k in range(1, depth):
        rz += (rest >= k * r).astype(jnp.int32)
    az = z - rz
    az += depth * (az < 0).astype(jnp.int32)
    ay = y + ry - 2 * y * ry
    return az * (2 * r) + ay * r + rest - rz * r


def prep_kernel(
    depth, where, tok_o, tok_p, mem_o, mem_p, cot_o, cot_p, vec, patch,
    x_ref, xt_ref, tok_r, cot_r, cot_t, mem_r, vec_r, hot_ref, ok_ref, unscaled,
):
    features = tok_o.shape[1]
    lane = lax.broadcasted_iota(jnp.int32, (features, features), 1)
    place = place_of(depth, features // (2 * depth), where[0], where[1], features)
    hot_ref[...] = (lane == place).astype(F32).astype(BF16)
    gain = vec[0:1, :].astype(F32)
    shift = vec[1:2, :].astype(F32)
    vec_r[...] = nt(vec[...], hot_ref[...])
    rows = lax.broadcasted_iota(jnp.int32, (SLOTS, PATCHES), 0)
    cols = lax.broadcasted_iota(jnp.int32, (SLOTS, PATCHES), 1)
    columns = nt((rows == cols).astype(F32), (patch[...] > 0).astype(F32))
    which = lax.broadcasted_iota(jnp.int32, columns.shape, 1)
    for at in range(2):
        one = jnp.sum(jnp.where(which == where[2 + at], columns, 0.0), axis=1, keepdims=True)
        ok_ref[at] = jnp.broadcast_to(one, (SLOTS, 128))

    for at, (mem, tok) in enumerate(((mem_o, tok_o), (mem_p, tok_p))):
        normed, _ = standard(tok[...].astype(F32))
        low = (normed * gain + shift).astype(BF16)
        x_ref[at, SLOTS:KEYS, :] = nt(low, hot_ref[...]).astype(BF16)
        unscaled[at, SLOTS:KEYS, :] = nt(normed.astype(BF16), hot_ref[...]).astype(BF16)
        xt_ref[:, at * KEYS + SLOTS : (at + 1) * KEYS] = nt(hot_ref[...], low).astype(BF16)
        normed, _ = standard(mem[...].astype(F32))
        normed = jnp.concatenate([normed, jnp.zeros((SLOTS - PATCHES, features), F32)], axis=0)
        unscaled[at, 0:SLOTS, :] = nt(normed.astype(BF16), hot_ref[...]).astype(BF16)
        low = (normed * gain + shift).astype(BF16)
        x_ref[at, 0:SLOTS, :] = nt(low, hot_ref[...]).astype(BF16)
        xt_ref[:, at * KEYS : at * KEYS + SLOTS] = nt(hot_ref[...], low).astype(BF16)
    raw = jnp.concatenate([mem_o[...].astype(F32), jnp.zeros((SLOTS - PATCHES, features), F32)], axis=0)
    mem_r[...] = nt(raw.astype(BF16), hot_ref[...]).astype(BF16)
    for at, (tok, cot) in enumerate(((tok_o, cot_o), (tok_p, cot_p))):
        rows = slice(at * TEXT, (at + 1) * TEXT)
        tok_r[rows, :] = nt(tok[...], hot_ref[...]).astype(BF16)
        cot_r[rows, :] = nt(cot[...], hot_ref[...]).astype(BF16)
        cot_t[:, rows] = nt(hot_ref[...], cot[...]).astype(BF16)


def masked(raw, cond):
    return jnp.where(cond, raw * SCALE, NEG)


def assemble(quads, w_ref):
    half = w_ref.shape[1] // 2
    for k, quad in enumerate(quads):
        w_ref[k // 2, (k % 2) * half : (k % 2 + 1) * half, :] = quad[0:half, :]


def attend_kernel(
    where, split, length,
    own, own_y, peer, far, x_ref, ok_ref,
    w_ref, y_ref, p_ref, ctx_ref, part_ref, up_ref, out_ref, bias,
):
    assemble((own, own_y, peer, far), w_ref)
    half = w_ref.shape[1] // 2
    for m, src in enumerate((own, peer)):
        tail = src[half : half + 16, :].astype(F32)
        bias[m] = tail[0:1, 0:640]
        up_ref[m] = tail[1:2, :]
    lane = lax.broadcasted_iota(jnp.int32, (TEXT, 128), 1)
    lane_k = lax.broadcasted_iota(jnp.int32, (KEYS, 128), 1)
    zero = jnp.zeros((TEXT, 128), BF16)
    unit = eye(128)
    unit_t = eye(TEXT)
    key_place = lax.broadcasted_iota(jnp.int32, (TEXT, TEXT), 0)
    query_place = lax.broadcasted_iota(jnp.int32, (TEXT, TEXT), 1)
    out_ref[...] = jnp.zeros_like(out_ref)

    def step(at, carry):
        e, m = at // 2, at % 2
        x = x_ref[e]
        w = w_ref[m]
        b = bias[m]
        y1 = nn(x, w[:, 0:384]) + b[:, 0:384]
        y_ref[m, e, :, 0:384] = y1.astype(BF16)
        y2 = nn(x, w[:, 384:640]) + b[:, 384:640]
        y_ref[m, e, :, 384:512] = y2[:, 0:128].astype(BF16)
        y_ref[m, e, :, 512:640] = jnp.where(lane_k < HEAD, y2[:, 128:256], 0.0).astype(BF16)

        patch_ok = jnp.concatenate([ok_ref[e], ok_ref[e]], axis=1) > 0.0
        prefix, valid = split[where[2 + e]], length[where[2 + e]]
        text_ok = ((key_place < prefix) | (key_place <= query_place)) & (key_place < valid)

        q01 = y_ref[m, e, SLOTS:KEYS, 0:128]
        q2 = y_ref[m, e, SLOTS:KEYS, 384:512]
        v01t = nt(unit, y_ref[m, e, :, 256:384]).astype(BF16)
        v2t = nt(unit, y_ref[m, e, :, 384:512]).astype(BF16)
        ctx01 = []
        for head in range(3):
            if head == 0:
                q, first, vt = jnp.where(lane < HEAD, q01, zero), 128, v01t[0:HEAD]
            elif head == 1:
                q, first, vt = jnp.where(lane >= HEAD, q01, zero), 128, v01t[HEAD:128]
            else:
                q, first, vt = jnp.where(lane < HEAD, q2, zero), 512, v2t[HEAD:128]
            s_mem = masked(nt(y_ref[m, e, 0:SLOTS, first : first + 128], q), patch_ok)
            s_text = masked(nt(y_ref[m, e, SLOTS:KEYS, first : first + 128], q), text_ok)
            largest = jnp.maximum(
                jnp.max(s_mem, axis=0, keepdims=True), jnp.max(s_text, axis=0, keepdims=True)
            )
            e_mem = jnp.exp(s_mem - largest)
            e_text = jnp.exp(s_text - largest)
            total = jnp.sum(e_mem, axis=0, keepdims=True) + jnp.sum(e_text, axis=0, keepdims=True)
            inverse = 1.0 / total
            p_mem = (e_mem * inverse).astype(BF16)
            p_text = (e_text * inverse).astype(BF16)
            p_ref[m, e, head, 0:SLOTS, :] = p_mem
            p_ref[m, e, head, SLOTS:KEYS, :] = p_text
            ctx01.append(nn(vt[:, 0:SLOTS], p_mem) + nn(vt[:, SLOTS:KEYS], p_text))
        c01t = jnp.concatenate([ctx01[0], ctx01[1]], axis=0).astype(BF16)
        c2t = jnp.concatenate([jnp.zeros((HEAD, TEXT), F32), ctx01[2]], axis=0).astype(BF16)
        c01 = nt(unit_t, c01t).astype(BF16)
        c2 = nt(unit_t, c2t).astype(BF16)
        ctx_ref[m, e, :, 0:128] = c01
        ctx_ref[m, e, :, 128:256] = c2
        out_ref[e] += nt(c01, w[:, 640:768]) + nt(c2, w[:, 512:640])
        return carry

    lax.fori_loop(0, 4, step, 0)
    part_ref[...] = out_ref[...].astype(BF16)


def gelu_pair(v):
    c = 0.7978845608028654
    square = v * v
    t = jnp.tanh(c * v * (1.0 + 0.044715 * square))
    gelu = 0.5 * v * (1.0 + t)
    slope = 0.5 * (1.0 + t) + 0.5 * v * (1.0 - t * t) * (c * (1.0 + 3 * 0.044715 * square))
    return gelu, slope


def up_kernel(
    part, part_in, tok_r, vec_r, cot_t, bias, w0, w1, w2, w3,
    res_ref, mid_t, hid_ref, slope_ref, g00, g01, g10, g11_top, g11_bottom, mid_ref, u_ref,
):
    half = g00.shape[0]
    assemble((w0, w1, w2, w3), u_ref)
    for e in range(2):
        rows = slice(e * TEXT, (e + 1) * TEXT)
        res = (
            tok_r[rows, :].astype(F32)
            + (part[e].astype(F32) + part_in[1 - e].astype(F32))
            + vec_r[4:5, :]
        )
        res_ref[rows, :] = res
        normed, _ = standard(res)
        mid_ref[rows, :] = (normed * vec_r[2:3, :] + vec_r[3:4, :]).astype(BF16)
    mid_t[...] = nt(eye(mid_ref.shape[1]), mid_ref[...]).astype(BF16)
    for m in range(2):
        for e in range(2):
            rows = slice(e * TEXT, (e + 1) * TEXT)
            pre = nn(mid_ref[rows, :], u_ref[m]) + bias[m]
            gelu, slope = gelu_pair(pre)
            hid_ref[m, rows, :] = gelu.astype(BF16)
            slope_ref[m, rows, :] = slope.astype(BF16)
    for dst, m, first in (
        (g11_top, 1, half), (g11_bottom, 1, half + half // 2), (g01, 0, half), (g10, 1, 0), (g00, 0, 0)
    ):
        dst[...] = nn(cot_t[first : first + dst.shape[0], :], hid_ref[m]).astype(BF16)


def down_kernel(
    v0, v1, v2, v3, hid_ref, slope_ref, mid_t, cot_r, w0, w1, w2, w3,
    out_o, grad_ref, bias_ref, g00, g01, g10, g11_top, g11_bottom, d_ref, pre_ref, u_ref,
):
    half = g00.shape[0]
    assemble((v0, v1, v2, v3), u_ref)
    assemble((w0, w1, w2, w3), d_ref)
    bias_ref[...] = jnp.zeros_like(bias_ref)
    for m in range(2):
        for e in range(2):
            rows = slice(e * TEXT, (e + 1) * TEXT)
            pre = (nn(cot_r[rows, :], d_ref[m]) * slope_ref[m, rows, :].astype(F32)).astype(BF16)
            pre_ref[m, rows, :] = pre
            bias_ref[m : m + 1, :] += jnp.sum(pre.astype(F32), axis=0, keepdims=True)
    for e in range(2):
        rows = slice(e * TEXT, (e + 1) * TEXT)
        grad_ref[e] = (nt(pre_ref[0, rows, :], u_ref[0]) + nt(pre_ref[1, rows, :], u_ref[1])).astype(BF16)
    for e, out in enumerate((out_o, grad_ref.at[2])):
        rows = slice(e * TEXT, (e + 1) * TEXT)
        out[...] = (nt(hid_ref[0, rows, :], d_ref[0]) + nt(hid_ref[1, rows, :], d_ref[1])).astype(BF16)
    for dst, m, first in (
        (g11_top, 1, half), (g11_bottom, 1, half + half // 2), (g01, 0, half), (g10, 1, 0), (g00, 0, 0)
    ):
        dst[...] = nn(mid_t[first : first + dst.shape[0], :], pre_ref[m]).astype(BF16)


def attend_back_kernel(
    where, grad, grad_in, res_ref, cot_r, vec_r, w_ref, y_ref, p_ref, unscaled, up_bias,
    rg_ref, agt_ref, dy_ref, back_o, back_p, sums, bias_ref, ag_ref, back_ref,
):
    lane = lax.broadcasted_iota(jnp.int32, (TEXT, 128), 1)
    row = lax.broadcasted_iota(jnp.int32, (128, TEXT), 0)
    zero = jnp.zeros((TEXT, 128), BF16)
    unit = eye(128)
    unit_t = eye(TEXT)
    for e in range(2):
        rows = slice(e * TEXT, (e + 1) * TEXT)
        mid_grad = grad[e].astype(F32) + grad_in[1 - e].astype(F32)
        normed, inverse = standard(res_ref[rows, :])
        cot = cot_r[rows, :].astype(F32)
        resid = cot + standard_back(normed, inverse, mid_grad, vec_r[2:3, :])
        low = resid.astype(BF16)
        ag_ref[rows, :] = low
        if e == 0:
            rg_ref[...] = resid
            sums[0:1, :] = jnp.sum(mid_grad * normed, axis=0, keepdims=True)
            sums[1:2, :] = jnp.sum(mid_grad, axis=0, keepdims=True)
            sums[2:3, :] = jnp.sum(low.astype(F32), axis=0, keepdims=True)
            sums[3:4, :] = jnp.sum(cot, axis=0, keepdims=True)
            sums[4:8, :] = jnp.zeros_like(sums[4:8, :])
    agt_ref[...] = nt(eye(ag_ref.shape[1]), ag_ref[...]).astype(BF16)
    bias_ref[...] = jnp.zeros_like(bias_ref)
    back_ref[...] = jnp.zeros_like(back_ref)

    def step(at, carry):
        e, m = at // 2, at % 2
        w = w_ref[m]
        ag = ag_ref[pl.ds(pl.multiple_of(e * TEXT, TEXT), TEXT), :]
        dc01 = nn(ag, w[:, 640:768]).astype(BF16)
        dc2 = nn(ag, w[:, 512:640]).astype(BF16)
        q01 = y_ref[m, e, SLOTS:KEYS, 0:128]
        q2 = y_ref[m, e, SLOTS:KEYS, 384:512]
        k01 = y_ref[m, e, :, 128:256]
        k2 = y_ref[m, e, :, 512:640]
        k01t = nt(unit, k01).astype(BF16)
        k2t = nt(unit, k2).astype(BF16)
        dk, dv, dqt = [], [], []
        for head in range(3):
            keep = (lane < HEAD) if head == 0 else (lane >= HEAD)
            if head < 2:
                dc = jnp.where(keep, dc01, zero)
                q = jnp.where(keep, q01, zero)
                v = y_ref[m, e, :, 256:384]
                kt = k01t[0:HEAD] if head == 0 else k01t[HEAD:128]
            else:
                dc = jnp.where(lane >= HEAD, dc2, zero)
                q = jnp.where(lane < HEAD, q2, zero)
                v = y_ref[m, e, :, 384:512]
                kt = k2t[0:HEAD]
            prob = p_ref[m, e, head]
            probs = prob.astype(F32)
            grad_p = nt(v, dc)
            dot = jnp.sum(probs * grad_p, axis=0, keepdims=True)
            score = (probs * (grad_p - dot)).astype(BF16)
            dk.append(nn(score, q))
            dv.append(nn(prob, dc))
            dqt.append(nn(kt, score))
        dk01 = ((dk[0] + dk[1]) * SCALE).astype(BF16)
        dk2 = (dk[2] * SCALE).astype(BF16)
        dv01 = (dv[0] + dv[1]).astype(BF16)
        dv2 = dv[2].astype(BF16)
        dq01 = nt(unit_t, (jnp.concatenate([dqt[0], dqt[1]], axis=0) * SCALE).astype(BF16))
        dq2 = nt(
            unit_t,
            (jnp.concatenate([dqt[2], jnp.zeros((HEAD, TEXT), F32)], axis=0) * SCALE).astype(BF16),
        )
        dy_ref[m, e, 0:SLOTS, 0:128] = zero
        dy_ref[m, e, SLOTS:KEYS, 0:128] = dq01.astype(BF16)
        dy_ref[m, e, :, 128:256] = dk01
        dy_ref[m, e, :, 256:384] = dv01
        dy_ref[m, e, 0:SLOTS, 384:512] = dv2[0:SLOTS]
        dy_ref[m, e, SLOTS:KEYS, 384:512] = (dq2 + dv2[SLOTS:KEYS].astype(F32)).astype(BF16)
        dy_ref[m, e, :, 512:640] = dk2
        dy = dy_ref[m, e]
        bias_ref[m] += jnp.sum(dy.astype(F32), axis=0, keepdims=True)
        back_ref[e] += nt(dy, w[:, 0:640])
        return carry

    lax.fori_loop(0, 4, step, 0)
    back_o[...] = back_ref[0]
    back_p[0:KEYS, :] = back_ref[1].astype(BF16)
    for e in range(2):
        sums[4:5, :] += jnp.sum(back_ref[e] * unscaled[e].astype(F32), axis=0, keepdims=True)
        sums[5:6, :] += jnp.sum(back_ref[e], axis=0, keepdims=True)
    index = lax.broadcasted_iota(jnp.int32, (4, 1), 0)
    own, peer = index == where[4], index == where[5]
    sums[8:12, 0:640] = jnp.where(own, bias_ref[0], 0.0) + jnp.where(peer, bias_ref[1], 0.0)
    sums[8:12, 640:768] = jnp.zeros((4, 128), F32)
    sums[12:16, :] = jnp.where(own, up_bias[0:1, :], 0.0) + jnp.where(peer, up_bias[1:2, :], 0.0)
    high = sums[...].astype(BF16)
    back_p[KEYS : KEYS + 16, :] = high
    back_p[KEYS + 16 : KEYS + 32, :] = (sums[...] - high.astype(F32)).astype(BF16)


def weight_kernel(
    xt_ref, agt_ref, dy_ref, ctx_ref, sums, back_in, hot_ref, g00, g01, g10, g11, vec_ref,
):
    half = g00.shape[0]
    more = vec_ref.shape[0]
    vec = sums[...] + back_in[KEYS : KEYS + more, :].astype(F32) + back_in[KEYS + more :, :].astype(F32)
    vec_ref[...] = vec
    vec_ref[0:8, :] = restore(vec[0:8, :], hot_ref[...])
    high = vec_ref[...].astype(BF16)
    low = (vec_ref[...] - high.astype(F32)).astype(BF16)
    for dst in (g01, g10, g11):
        dst[half : half + more, :] = high
        dst[half + more : half + 2 * more, :] = low
    for dst, m, first in ((g11, 1, half), (g01, 0, half), (g10, 1, 0), (g00, 0, 0)):
        rows = slice(first, first + half)
        dy = dy_ref[m].reshape(2 * KEYS, 640)
        ctx = ctx_ref[m].reshape(2 * TEXT, 256)
        grad = nn(xt_ref[rows, :], dy)
        out = nn(agt_ref[rows, :], ctx)
        dst[0:half, 0:512] = grad[:, 0:512].astype(BF16)
        dst[0:half, 512:640] = (grad[:, 512:640] + out[:, 128:256]).astype(BF16)
        dst[0:half, 640:768] = out[:, 0:128].astype(BF16)


def restore(v, hot):
    high = v.astype(BF16)
    low = (v - high.astype(F32)).astype(BF16)
    return nn(high, hot) + nn(low, hot)


def last_kernel(
    back_o, back_in, tok_r, mem_r, rg_ref, res_ref, out_o, out_in, vec_r, hot_ref,
    layer_ref, in_ref, mem_ref,
):
    hot = hot_ref[...]
    gain = vec_r[0:1, :]
    layer = (
        res_ref[0:TEXT, :] + (out_o[...].astype(F32) + out_in[2].astype(F32)) + vec_r[5:6, :]
    ).astype(BF16)
    layer_ref[...] = nn(layer, hot).astype(BF16)
    mem_back = back_o[0:SLOTS, :] + back_in[0:SLOTS, :].astype(F32)
    text_back = back_o[SLOTS:KEYS, :] + back_in[SLOTS:KEYS, :].astype(F32)
    normed, inverse = standard(tok_r[0:TEXT, :].astype(F32))
    in_ref[...] = restore(rg_ref[...] + standard_back(normed, inverse, text_back, gain), hot)
    normed, inverse = standard(mem_r[...].astype(F32))
    mem_ref[...] = restore(standard_back(normed, inverse, mem_back, gain), hot)[0:PATCHES, :]


class Links:
    def __init__(self, dp, mp):
        self.dp, self.mp, self.depth = dp, mp, dp // 2
        self.x = self.pairs(lambda d, m: (d, m ^ 2))
        self.c = self.pairs(lambda d, m: (d, m ^ 1))
        self.y = self.pairs(lambda d, m: (d ^ 1, m))
        self.xy = self.pairs(lambda d, m: (d ^ 1, m ^ 2))

    def pairs(self, to):
        out = []
        for d in range(self.dp):
            for m in range(self.mp):
                d2, m2 = to(d, m)
                out.append((d * self.mp + m, d2 * self.mp + m2))
        return out

    def z(self, k):
        return self.pairs(lambda d, m: ((((d // 2 + k) % self.depth) * 2 + d % 2), m))

    def send(self, a, pairs):
        return lax.ppermute(a, AXES, pairs)

    def line(self, shard, other, tail=None, after=()):
        more = [] if tail is None else [tail]
        if self.depth == 4:
            pieces = [shard] + [self.send(shard, self.z(k)) for k in range(1, 4)] + more
            return call(
                functools.partial(stack_kernel, len(pieces)),
                [((sum(p.shape[0] for p in pieces), shard.shape[1]), BF16), (other.shape, other.dtype)],
                *pieces, other, after=after,
            )
        held = shard[None]
        step = 1
        while step < self.depth:
            held = jnp.concatenate([held, self.send(held, self.z(step))], axis=0)
            step *= 2
        return jnp.concatenate([held.reshape(-1, shard.shape[1])] + more, axis=0), other

    def plane(self, rows):
        return [rows, self.send(rows, self.y), self.send(rows, self.x), self.send(rows, self.xy)]

    def turn(self, after, g01, g10, far_top, far_bottom, *parts):
        if self.depth != 4:
            return self.meet(after, g01, g10, far_top, far_bottom) + self.fold((), *parts)
        rows, lanes = parts[0].shape
        to_y, to_x, near, far = call(
            turn_kernel,
            [(g01.shape, BF16), (g10.shape, BF16), ((rows // 2, lanes), F32), ((rows // 2, lanes), BF16)],
            g01, far_top, g10, far_bottom, *parts, after=after,
        )
        return self.send(to_y, self.y), self.send(to_x, self.x), to_x, near, self.send(far, self.z(-2))

    def home(self, after, *parts):
        rows, lanes = parts[0].shape
        if self.depth == 4:
            r = rows // 4
            own, *rest = call(
                functools.partial(total_kernel, len(parts)),
                [((r, lanes), F32)] + [((r, lanes), BF16)] * 3, *parts, after=after,
            )
            return [own] + [self.send(rest[k], self.z(-k - 1)) for k in range(3)]
        held = sum(p.astype(F32) for p in parts).reshape(self.depth, -1, lanes)
        step = self.depth // 2
        while step >= 1:
            held = held[:step] + self.send(held[step:].astype(BF16), self.z(-step)).astype(F32)
            step //= 2
        return [held[0]]

    def meet(self, after, g01, g10, far_top, far_bottom):
        to_y, to_x = call(
            add_kernel, [(g01.shape, BF16), (g10.shape, BF16)], g01, far_top, g10, far_bottom, after=after
        )
        return self.send(to_y, self.y), self.send(to_x, self.x), to_x

    def direct(self, g01, g10, g11):
        return self.send(g11, self.xy), self.send(g01, self.y), self.send(g10, self.x)

    def fold(self, after, *parts):
        if self.depth != 4:
            return self.home(after, *parts)[0], None
        rows, lanes = parts[0].shape
        near, far = call(
            functools.partial(total_kernel, len(parts)),
            [((rows // 2, lanes), F32), ((rows // 2, lanes), BF16)], *parts, after=after,
        )
        return near, self.send(far, self.z(-2))

    def fold_more(self, after, near, far):
        if self.depth != 4:
            return [near]
        rows, lanes = near.shape
        own, other = call(
            functools.partial(total_kernel, 2),
            [((rows // 2, lanes), F32), ((rows // 2, lanes), BF16)], near, far, after=after,
        )
        return [own, self.send(other, self.z(-1))]

    def home_with(self, after, vec, own, *got):
        rows, lanes = own.shape
        more = vec.shape[0]
        if self.depth == 4:
            r = rows // 4
            vec, own, *rest = call(
                functools.partial(total_vec_kernel, 1 + len(got)),
                [(vec.shape, F32), ((r, lanes), F32)] + [((r + 2 * more, lanes), BF16)] * 3,
                vec, own, *got, after=after,
            )
            return [vec, own] + [self.send(rest[k], self.z(-k - 1)) for k in range(3)]
        for g in got:
            vec = vec + g[rows : rows + more].astype(F32) + g[rows + more :].astype(F32)
        step = 1
        while step < self.depth:
            vec = vec + self.send(vec, self.z(step))
            step *= 2
        return [vec] + self.home((), own, *(g[:rows] for g in got))


def add_up(parts):
    total = parts[0]
    for part in parts[1:]:
        total = total + part.astype(F32)
    return total


def per_device(
    tokens, memory, split_point, text_length, patch_mask,
    query_weight, query_bias, key_weight, value_weight, value_bias,
    out_weight, out_bias, attn_gain, attn_shift, mlp_gain, mlp_shift,
    up_weight, up_bias, down_weight, down_bias, cotangent,
):
    features = tokens.shape[1]
    width = query_weight.shape[1]
    hidden = up_weight.shape[1]
    dp, mp = lax.axis_size("dp"), lax.axis_size("mp")
    links = Links(dp, mp)
    dp_at, mp_at = lax.axis_index("dp"), lax.axis_index("mp")
    r = features // dp
    half = features // 2

    tok_p = links.send(tokens, links.c)
    mem_p = links.send(memory, links.c)
    cot_p = links.send(cotangent, links.c)
    (attn_own,) = call(
        pack_kernel, [((r, features), BF16)], query_weight, key_weight, value_weight, out_weight
    )
    (biases,) = call(
        bias_kernel, [((16, features), BF16)],
        query_bias.reshape(1, -1), value_bias.reshape(1, -1), up_bias.reshape(1, -1),
        after=(attn_own, tok_p, mem_p, cot_p),
    )

    where = jnp.stack([dp_at // 2, dp_at % 2, mp_at, mp_at ^ 1, mp_at, mp_at ^ 2]).astype(jnp.int32)
    blank = jnp.zeros_like(attn_gain)
    vec = jnp.stack(
        [attn_gain, attn_shift, mlp_gain, mlp_shift, out_bias, down_bias] + [blank] * 10
    )
    x, xt, tok_r, cot_r, cot_t, mem_r, vec_r, hot, ok, unscaled = call(
        functools.partial(prep_kernel, dp // 2),
        [
            ((2, KEYS, features), BF16), ((features, 2 * KEYS), BF16),
            ((2 * TEXT, features), BF16), ((2 * TEXT, features), BF16), ((features, 2 * TEXT), BF16),
            ((SLOTS, features), BF16), ((16, features), F32), ((features, features), BF16),
            ((2, SLOTS, 128), F32), ((2, KEYS, features), BF16),
        ],
        where, tokens, tok_p, memory, mem_p, cotangent, cot_p, vec, patch_mask,
        smem=1, after=(biases,),
    )
    rows_a, up_own = links.line(attn_own, up_weight, biases, after=(ok,))
    quads_a = links.plane(rows_a)
    rows_u, down_own = links.line(up_own, down_weight.T, after=(rows_a,))
    quads_u = links.plane(rows_u)

    w, y, p, ctx, part, ub = call(
        attend_kernel,
        [
            ((2, features, features), BF16), ((2, 2, KEYS, 640), BF16), ((2, 2, 3, KEYS, TEXT), BF16),
            ((2, 2, TEXT, 256), BF16), ((2, TEXT, features), BF16), ((2, 1, hidden), F32),
        ],
        where, split_point, text_length, *quads_a, x, ok,
        smem=3, scratch=[pltpu.VMEM((2, TEXT, features), F32), pltpu.VMEM((2, 1, 640), F32)], after=(rows_u,),
    )
    part_in = links.send(part, links.c)
    (token,) = call(gate_kernel, [((8, 128), F32)], after=(part, *quads_u[1:]))
    rows_d, _ = links.line(down_own, where, after=(part,))
    quads_d = links.plane(rows_d)

    quarter = ((half, hidden), BF16)
    eighth = ((half // 2, hidden), BF16)
    res, mid_t, hid, slope, d00, d01, d10, d11t, d11b = call(
        up_kernel,
        [
            ((2 * TEXT, features), F32), ((features, 2 * TEXT), BF16),
            ((2, 2 * TEXT, hidden), BF16), ((2, 2 * TEXT, hidden), BF16),
        ]
        + [quarter] * 3 + [eighth] * 2,
        part, part_in, tok_r, vec_r, cot_t, ub, *quads_u, after=(token, rows_d),
        scratch=[pltpu.VMEM((2 * TEXT, features), BF16), pltpu.VMEM((2, features, hidden), BF16)],
    )
    d_far = links.send(d11t, links.x), links.send(d11b, links.y)

    layer_o, mid_grad, up_bias_part, u00, u01, u10, u11t, u11b = call(
        down_kernel,
        [((TEXT, features), BF16), ((3, TEXT, features), BF16), ((2, hidden), F32)]
        + [quarter] * 3 + [eighth] * 2,
        *quads_u, hid, slope, mid_t, cot_r, *quads_d,
        scratch=[
            pltpu.VMEM((2, features, hidden), BF16), pltpu.VMEM((2, 2 * TEXT, hidden), BF16),
            pltpu.VMEM((2, features, hidden), BF16),
        ],
    )
    grad_in = links.send(mid_grad, links.c)
    d_y, d_x, token = links.meet((mid_grad,), d01, d10, *d_far)
    u_far = links.send(u11t, links.x), links.send(u11b, links.y)

    rg, ag_t, dy, back_o, back_p, sums = call(
        attend_back_kernel,
        [
            ((TEXT, features), F32), ((features, 2 * TEXT), BF16), ((2, 2, KEYS, 640), BF16),
            ((KEYS, features), F32), ((KEYS + 32, features), BF16), ((16, features), F32),
        ],
        where, mid_grad, grad_in, res, cot_r, vec_r, w, y, p, unscaled, up_bias_part, smem=1, after=(token,),
        scratch=[
            pltpu.VMEM((2, 1, 640), F32), pltpu.VMEM((2 * TEXT, features), BF16), pltpu.VMEM((2, KEYS, features), F32)
        ],
    )
    back_in = links.send(back_p, links.c)
    u_y, u_x, token, down_total, down_more = links.turn((dy,), u01, u10, *u_far, d00, d_y, d_x)
    a00, a01, a10, a11, stack = call(
        weight_kernel,
        [((half, features), BF16)] + [((half + 32, features), BF16)] * 3 + [((16, features), F32)],
        xt, ag_t, dy, ctx, sums, back_in, hot, after=(token,),
    )
    a_got = links.direct(a01, a10, a11)
    layer_out, input_grad, memory_grad = call(
        last_kernel,
        [((TEXT, features), BF16), ((TEXT, features), F32), ((PATCHES, features), F32)],
        back_o, back_in, tok_r, mem_r, rg, res, layer_o, grad_in, vec_r, hot, after=(a00,),
    )
    down_parts = links.fold_more((input_grad,), down_total, down_more)
    up_total, up_more = links.fold((down_parts[0],), u00, u_y, u_x)
    up_parts = links.fold_more((), up_total, up_more)
    attn_parts = links.home_with((up_parts[0],), stack, a00, *a_got)
    query_sum, key_sum, value_sum, out_sum, stack = call(
        finish_kernel,
        [((r, width), F32)] * 3 + [((width, r), F32), (stack.shape, F32)], *attn_parts,
    )

    at = dp_at * mp + mp_at
    few = features // (dp * mp)
    q_bias = jnp.concatenate([stack[8:12, 0:128], stack[8:12, 384:448]], axis=1).reshape(1, features)
    v_bias = jnp.concatenate([stack[8:12, 256:384], stack[8:12, 448:512]], axis=1).reshape(1, features)
    vectors = lax.dynamic_slice(jnp.concatenate([stack[0:6], q_bias, v_bias]), (0, at * few), (8, few))
    many = up_bias.shape[0] // dp
    up_bias_sum = lax.dynamic_slice(stack[12:16].reshape(-1), (at * many,), (many,))

    return (
        layer_out, input_grad, memory_grad,
        query_sum, key_sum, value_sum, out_sum, add_up(up_parts), add_up(down_parts).T,
        vectors[6], vectors[7], up_bias_sum,
        vectors[2], vectors[3], vectors[4], vectors[5], vectors[0], vectors[1],
    )


def solution(mesh):
    rows = P(AXES, None)
    flat = P(AXES)
    in_specs = (
        rows, rows, P("dp"), P("dp"), P("dp", None),
        P("dp", "mp"), P("mp"), P("dp", "mp"), P("dp", "mp"), P("mp"),
        P("mp", "dp"), P(), P(), P(), P(), P(),
        P("dp", "mp"), P("mp"), P("mp", "dp"), P(), rows,
    )
    out_specs = (
        rows, rows, rows,
        P("dp", "mp"), P("dp", "mp"), P("dp", "mp"), P("mp", "dp"), P("dp", "mp"), P("mp", "dp"),
    ) + (flat,) * 9
    return jax.shard_map(
        per_device, mesh=mesh, in_specs=in_specs, out_specs=out_specs, check_vma=False
    )
```

```python
import functools

import jax
import jax.numpy as jnp
from jax import lax
from jax.experimental import pallas as pl
from jax.experimental.pallas import tpu as pltpu
from jax.sharding import PartitionSpec as P

HEAD = 64
TEXT = 256
PATCHES = 196
SLOTS = 256
KEYS = SLOTS + TEXT
EPS = 1e-06
NEG = -1000000000.0
SCALE = HEAD ** (-0.5)
F32 = jnp.float32
BF16 = jnp.bfloat16
AXES = ("dp", "mp")

CUT = 384


def nn(a, b):
    return lax.dot_general(a, b, (((1,), (0,)), ((), ())), preferred_element_type=F32)


def nt(a, b):
    return lax.dot_general(a, b, (((1,), (1,)), ((), ())), preferred_element_type=F32)


def eye(n):
    rows = lax.broadcasted_iota(jnp.int32, (n, n), 0)
    cols = lax.broadcasted_iota(jnp.int32, (n, n), 1)
    return (rows == cols).astype(F32).astype(BF16)


def standard(matrix):
    average = jnp.mean(matrix, axis=-1, keepdims=True)
    centered = matrix - average
    inverse = lax.rsqrt(jnp.mean(centered * centered, axis=-1, keepdims=True) + EPS)
    return centered * inverse, inverse


def standard_back(normed, inverse, grad_out, gain):
    scaled = grad_out * gain
    return inverse * (
        scaled
        - jnp.mean(scaled, axis=-1, keepdims=True)
        - normed * jnp.mean(scaled * normed, axis=-1, keepdims=True)
    )


UNIT = 1e9
COST = {
    "prep_kernel": 8.0, "attend_kernel": 17.0, "up_kernel": 9.0, "down_kernel": 9.0,
    "gate_kernel": 12.0, "add_kernel": 30.0, "add_vec_kernel": 30.0, "turn_kernel": 30.0, "cut_kernel": 30.0, "attend_back_kernel": 19.0, "weight_kernel": 6.0, "last_kernel": 6.0,
}


ROOM = {
    "pack_kernel": 56,    "prep_kernel": 24, "attend_kernel": 26, "up_kernel": 26, "down_kernel": 26,
    "attend_back_kernel": 26, "weight_kernel": 20, "last_kernel": 16,
}


def call(kernel, out_shapes, *args, scratch=(), smem=0, after=(), anywhere=False):
    name = getattr(kernel, "func", kernel).__name__
    waits = len(after)

    def body(*refs):
        return kernel(*refs[waits:])

    place = pl.BlockSpec(memory_space=pl.ANY if anywhere else pltpu.VMEM)
    return pl.pallas_call(
        body,
        out_shape=[jax.ShapeDtypeStruct(s, d) for s, d in out_shapes],
        in_specs=[pl.BlockSpec(memory_space=pl.ANY)] * waits
        + [pl.BlockSpec(memory_space=pltpu.SMEM)] * smem
        + [place] * (len(args) - smem),
        out_specs=[place] * len(out_shapes),
        scratch_shapes=list(scratch),
        compiler_params=pltpu.CompilerParams(vmem_limit_bytes=ROOM.get(name, 8) * 1024 * 1024),
        cost_estimate=pl.CostEstimate(
            flops=int(COST.get(name, 2.0) * UNIT), bytes_accessed=0, transcendentals=0
        ),
        name=name,
    )(*after, *args)


def pack_kernel(q, k, v, o, a_ref):
    ot = nt(eye(q.shape[0]), o[...]).astype(BF16)
    a_ref[:, 0:128] = q[:, 0:128]
    a_ref[:, 128:256] = k[:, 0:128]
    a_ref[:, 256:384] = v[:, 0:128]
    a_ref[:, 384:512] = jnp.concatenate([q[:, 128:192], v[:, 128:192]], axis=1)
    a_ref[:, 512:640] = jnp.concatenate([k[:, 128:192], ot[:, 128:192]], axis=1)
    a_ref[:, 640:768] = ot[:, 0:128]


def bias_kernel(qb, vb, ub, bias_ref):
    blank = jnp.zeros((1, 128), F32)
    qf, vf = qb[...].astype(F32), vb[...].astype(F32)
    row = jnp.concatenate(
        [qf[:, 0:128], blank, vf[:, 0:128], qf[:, 128:192], vf[:, 128:192], blank, blank], axis=1
    )
    rest = jnp.zeros((14, row.shape[1]), F32)
    bias_ref[...] = jnp.concatenate([row, ub[...].astype(F32), rest], axis=0).astype(BF16)


def join_kernel(count, *refs):
    extra = (len(refs) - count - 1) // 2
    out, first = refs[count + extra], 0
    for piece in refs[:count]:
        out[first : first + piece.shape[0], :] = piece[...]
        first += piece.shape[0]
    for src, dst in zip(refs[count : count + extra], refs[count + extra + 1 :]):
        dst[...] = src[...]


def cut_kernel(a, b, out_a, out_b):
    cut = out_a.shape[0]
    out_a[...] = a[0:cut, :]
    out_b[...] = b[cut : 2 * cut, :]


def gate_kernel(token):
    token[...] = jnp.zeros_like(token)


def add_kernel(top, far_top, bottom, far_bottom, out_top, out_bottom):
    cut = far_top.shape[0]
    out_top[0:cut, :] = (top[0:cut, :].astype(F32) + far_top[...].astype(F32)).astype(BF16)
    out_top[cut:, :] = top[cut:, :]
    out_bottom[0:cut, :] = bottom[0:cut, :]
    out_bottom[cut:, :] = (bottom[cut:, :].astype(F32) + far_bottom[...].astype(F32)).astype(BF16)


def add_vec_kernel(vec, top, far_top, bottom, far_bottom, out_top, out_bottom, vec_out):
    half, cut, more = bottom.shape[0], far_bottom.shape[0], vec.shape[0]
    add_kernel(
        top, far_top.at[0:cut, :], bottom, far_bottom, out_top.at[0:half, :], out_bottom
    )
    sums = vec[...] + far_top[cut : cut + more, :].astype(F32) + far_top[cut + more :, :].astype(F32)
    vec_out[...] = sums
    high = sums.astype(BF16)
    out_top[half : half + more, :] = high
    out_top[half + more :, :] = (sums - high.astype(F32)).astype(BF16)


def turn_kernel(own, got, a, b, c, out, near, far):
    out[...] = (own[...].astype(F32) + got[...].astype(F32)).astype(BF16)
    total_kernel(3, a, b, c, near, far)


def corner_kernel(low, one, two, t00, t01, t10, t11):
    rows = t00.shape[0]
    for k, dst in enumerate((t00, t01, t10, t11)):
        at = slice(k * rows, (k + 1) * rows)
        dst[...] = (low[at, :].astype(F32) + one[at, :].astype(F32) + two[at, :].astype(F32)).astype(dst.dtype)


def total_kernel(count, *refs):
    rows = refs[count].shape[0]
    for k, dst in enumerate(refs[count:]):
        at = slice(k * rows, (k + 1) * rows)
        value = refs[0][at, :].astype(F32)
        for other in refs[1:count]:
            value += other[at, :].astype(F32)
        dst[...] = value.astype(dst.dtype)


def total_vec_kernel(count, vec, *refs):
    vec_out, dsts = refs[count], refs[count + 1 :]
    rows, more = dsts[0].shape[0], vec.shape[0]
    total_kernel(count, *refs[:count], *(d.at[0:rows, :] for d in dsts))
    first = 4 * rows
    sums = vec[...]
    for other in refs[1:count]:
        if other.shape[0] > first:
            sums += other[first : first + more, :].astype(F32) + other[first + more :, :].astype(F32)
    vec_out[...] = sums
    high = sums.astype(BF16)
    low = (sums - high.astype(F32)).astype(BF16)
    for dst in dsts[1:]:
        dst[rows : rows + more, :] = high
        dst[rows + more : rows + 2 * more, :] = low


def finish_kernel(*refs):
    vec, (parts, (q, k, v, o, vec_out)) = refs[0], (refs[1:-5], refs[-5:])
    rows, more = parts[0].shape[0], vec.shape[0]
    total = parts[0][...]
    sums = vec[...]
    for part in parts[1:]:
        total += part[0:rows, :].astype(F32)
        sums += part[rows : rows + more, :].astype(F32) + part[rows + more : rows + 2 * more, :].astype(F32)
    vec_out[...] = sums
    q[...] = jnp.concatenate([total[:, 0:128], total[:, 384:448]], axis=1)
    k[...] = jnp.concatenate([total[:, 128:256], total[:, 512:576]], axis=1)
    v[...] = jnp.concatenate([total[:, 256:384], total[:, 448:512]], axis=1)
    out = jnp.concatenate([total[:, 640:768], total[:, 576:640]], axis=1)
    high = out.astype(BF16)
    low = (out - high.astype(F32)).astype(BF16)
    unit = eye(out.shape[1])
    o[...] = nt(unit, high) + nt(unit, low)


def place_of(depth, r, z, y, count):
    rel = lax.broadcasted_iota(jnp.int32, (count, 1), 0)
    half = count // 2
    ry = (rel >= half).astype(jnp.int32)
    rest = rel - ry * half
    rz = jnp.zeros_like(rel)
    for k in range(1, depth):
        rz += (rest >= k * r).astype(jnp.int32)
    az = z - rz
    az += depth * (az < 0).astype(jnp.int32)
    ay = y + ry - 2 * y * ry
    return az * (2 * r) + ay * r + rest - rz * r


def prep_kernel(
    depth, where, tok_o, tok_p, mem_o, mem_p, cot_o, cot_p, vec, patch,
    x_ref, xt_ref, tok_r, cot_r, cot_t, mem_r, vec_r, hot_ref, ok_ref, unscaled,
):
    features = tok_o.shape[1]
    lane = lax.broadcasted_iota(jnp.int32, (features, features), 1)
    place = place_of(depth, features // (2 * depth), where[0], where[1], features)
    hot_ref[...] = (lane == place).astype(F32).astype(BF16)
    gain = vec[0:1, :].astype(F32)
    shift = vec[1:2, :].astype(F32)
    vec_r[...] = nt(vec[...], hot_ref[...])
    rows = lax.broadcasted_iota(jnp.int32, (SLOTS, PATCHES), 0)
    cols = lax.broadcasted_iota(jnp.int32, (SLOTS, PATCHES), 1)
    columns = nt((rows == cols).astype(F32), (patch[...] > 0).astype(F32))
    which = lax.broadcasted_iota(jnp.int32, columns.shape, 1)
    for at in range(2):
        one = jnp.sum(jnp.where(which == where[2 + at], columns, 0.0), axis=1, keepdims=True)
        ok_ref[at] = jnp.broadcast_to(one, (SLOTS, 128))

    for at, (mem, tok) in enumerate(((mem_o, tok_o), (mem_p, tok_p))):
        normed, _ = standard(tok[...].astype(F32))
        low = (normed * gain + shift).astype(BF16)
        x_ref[at, SLOTS:KEYS, :] = nt(low, hot_ref[...]).astype(BF16)
        unscaled[at, SLOTS:KEYS, :] = nt(normed.astype(BF16), hot_ref[...]).astype(BF16)
        xt_ref[:, at * KEYS + SLOTS : (at + 1) * KEYS] = nt(hot_ref[...], low).astype(BF16)
        normed, _ = standard(mem[...].astype(F32))
        normed = jnp.concatenate([normed, jnp.zeros((SLOTS - PATCHES, features), F32)], axis=0)
        unscaled[at, 0:SLOTS, :] = nt(normed.astype(BF16), hot_ref[...]).astype(BF16)
        low = (normed * gain + shift).astype(BF16)
        x_ref[at, 0:SLOTS, :] = nt(low, hot_ref[...]).astype(BF16)
        xt_ref[:, at * KEYS : at * KEYS + SLOTS] = nt(hot_ref[...], low).astype(BF16)
    raw = jnp.concatenate([mem_o[...].astype(F32), jnp.zeros((SLOTS - PATCHES, features), F32)], axis=0)
    mem_r[...] = nt(raw.astype(BF16), hot_ref[...]).astype(BF16)
    for at, (tok, cot) in enumerate(((tok_o, cot_o), (tok_p, cot_p))):
        rows = slice(at * TEXT, (at + 1) * TEXT)
        tok_r[rows, :] = nt(tok[...], hot_ref[...]).astype(BF16)
        cot_r[rows, :] = nt(cot[...], hot_ref[...]).astype(BF16)
        cot_t[:, rows] = nt(hot_ref[...], cot[...]).astype(BF16)


def assemble(parts, w_ref):
    own, own_y, peer, far_top, far_bottom = parts
    half, cut = w_ref.shape[1] // 2, far_top.shape[0]
    w_ref[0, 0:half, :] = own[0:half, :]
    w_ref[0, half : 2 * half, :] = own_y[0:half, :]
    w_ref[1, 0:half, :] = peer[0:half, :]
    w_ref[1, half : half + cut, :] = far_top[...]
    w_ref[1, half + cut : 2 * half, :] = far_bottom[...]


def assemble_quads(pieces, w_ref):
    block = pieces[0].shape[0] // 4
    for k, piece in enumerate(pieces):
        for quarter in range(4):
            first = (quarter % 2) * 4 * block + k * block
            w_ref[quarter // 2, first : first + block, :] = piece[quarter * block : (quarter + 1) * block, :]


def head_lanes(m, head):
    first = m * 640
    if head < 2:
        return first, first + 128, first + 256
    return first + 384, first + 512, first + 384


def attend_kernel(
    where, split, length,
    own, own_y, peer, far_top, far_bottom, x_ref, ok_ref,
    wq_ref, wo_ref, y_ref, p_ref, ctx_ref, part_ref, up_ref, bias, factor,
):
    half, cut = wq_ref.shape[0] // 2, far_top.shape[0]
    for m, first, src, size in (
        (0, 0, own, half), (0, half, own_y, half), (1, 0, peer, half),
        (1, half, far_top, cut), (1, half + cut, far_bottom, cut),
    ):
        rows = slice(first, first + size)
        wq_ref[rows, m * 640 : (m + 1) * 640] = src[0:size, 0:640]
        wo_ref[rows, m * 128 : (m + 1) * 128] = src[0:size, 640:768]
        wo_ref[rows, 256 + m * 128 : 384 + m * 128] = src[0:size, 512:640]
    lane = lax.broadcasted_iota(jnp.int32, (1, 128), 1)
    one = jnp.ones((1, 128), F32)
    for m, src in enumerate((own, peer)):
        tail = src[half : half + 16, :].astype(F32)
        bias[0:1, m * 640 : (m + 1) * 640] = tail[0:1, 0:640]
        up_ref[m] = tail[1:2, :]
        for group, value in enumerate(
            (one * SCALE, one, one, jnp.where(lane < HEAD, SCALE, 1.0), jnp.where(lane < HEAD, 1.0, 0.0))
        ):
            first = m * 640 + group * 128
            factor[0:1, first : first + 128] = value
    for e in range(2):
        for first in range(0, 1280, 256):
            at = slice(first, first + 256)
            y = (nn(x_ref[e], wq_ref[:, at]) + bias[0:1, at]) * factor[0:1, at]
            y_ref[e, :, at] = y.astype(BF16)

    lane = lax.broadcasted_iota(jnp.int32, (TEXT, 128), 1)
    zero = jnp.zeros((TEXT, 128), BF16)
    unit = eye(128)
    unit_t = eye(TEXT)
    key_place = lax.broadcasted_iota(jnp.int32, (TEXT, TEXT), 0)
    query_place = lax.broadcasted_iota(jnp.int32, (TEXT, TEXT), 1)

    def step(e, carry):
        patch_ok = jnp.concatenate([ok_ref[e], ok_ref[e]], axis=1) > 0.0
        prefix, valid = split[where[2 + e]], length[where[2 + e]]
        text_ok = ((key_place < prefix) | (key_place <= query_place)) & (key_place < valid)
        for m in range(2):
            parts = []
            for head in range(3):
                qa, ka, va = head_lanes(m, head)
                low = head != 1
                q = jnp.where((lane < HEAD) if low else (lane >= HEAD), y_ref[e, SLOTS:KEYS, qa : qa + 128], zero)
                if head != 1:
                    vt_all = nt(unit, y_ref[e, :, va : va + 128]).astype(BF16)
                vt = vt_all[0:HEAD] if head == 0 else vt_all[HEAD:128]
                s_mem = jnp.where(patch_ok, nt(y_ref[e, 0:SLOTS, ka : ka + 128], q), NEG)
                s_text = jnp.where(text_ok, nt(y_ref[e, SLOTS:KEYS, ka : ka + 128], q), NEG)
                largest = jnp.maximum(
                    jnp.max(s_mem, axis=0, keepdims=True), jnp.max(s_text, axis=0, keepdims=True)
                )
                e_mem = jnp.exp(s_mem - largest)
                e_text = jnp.exp(s_text - largest)
                total = jnp.sum(e_mem, axis=0, keepdims=True) + jnp.sum(e_text, axis=0, keepdims=True)
                inverse = 1.0 / total
                p_mem = (e_mem * inverse).astype(BF16)
                p_text = (e_text * inverse).astype(BF16)
                p_ref[e, m * 3 + head, 0:SLOTS, :] = p_mem
                p_ref[e, m * 3 + head, SLOTS:KEYS, :] = p_text
                parts.append(nn(vt[:, 0:SLOTS], p_mem) + nn(vt[:, SLOTS:KEYS], p_text))
            c01t = jnp.concatenate([parts[0], parts[1]], axis=0).astype(BF16)
            c2t = jnp.concatenate([jnp.zeros((HEAD, TEXT), F32), parts[2]], axis=0).astype(BF16)
            ctx_ref[e, :, m * 128 : (m + 1) * 128] = nt(unit_t, c01t).astype(BF16)
            ctx_ref[e, :, 256 + m * 128 : 384 + m * 128] = nt(unit_t, c2t).astype(BF16)
        return carry

    lax.fori_loop(0, 2, step, 0, unroll=True)
    features = wo_ref.shape[0]
    ctx = ctx_ref[...].reshape(2 * TEXT, 512)
    for first in range(0, features, 256):
        at = slice(first, first + 256)
        part_ref[:, :, at] = nt(ctx, wo_ref[at, :]).astype(BF16).reshape(2, TEXT, 256)


def gelu_pair(v):
    c = 0.7978845608028654
    square = v * v
    t = jnp.tanh(c * v * (1.0 + 0.044715 * square))
    gelu = 0.5 * v * (1.0 + t)
    slope = 0.5 * (1.0 + t) + 0.5 * v * (1.0 - t * t) * (c * (1.0 + 3 * 0.044715 * square))
    return gelu, slope


def up_kernel(
    part, part_in, tok_r, vec_r, cot_t, bias, u0, u1, u2, u3, u4,
    res_ref, mid_t, hid_ref, slope_ref, g00, g01, g10, g11_top, g11_bottom, mid_ref, u_ref,
):
    half = g00.shape[0]
    assemble((u0, u1, u2, u3, u4), u_ref)
    for e in range(2):
        rows = slice(e * TEXT, (e + 1) * TEXT)
        res = (
            tok_r[rows, :].astype(F32)
            + (part[e].astype(F32) + part_in[1 - e].astype(F32))
            + vec_r[4:5, :]
        )
        res_ref[rows, :] = res
        normed, _ = standard(res)
        mid_ref[rows, :] = (normed * vec_r[2:3, :] + vec_r[3:4, :]).astype(BF16)
    mid_t[...] = nt(eye(mid_ref.shape[1]), mid_ref[...]).astype(BF16)
    wide = u_ref.shape[2]
    for m in range(2):
        for first in range(0, wide, 256):
            at = slice(first, first + 256)
            gelu, slope = gelu_pair(nn(mid_ref[...], u_ref[m, :, at]) + bias[m, :, at])
            hid_ref[m, :, at] = gelu.astype(BF16)
            slope_ref[m, :, at] = slope.astype(BF16)
    for dst, m, first in (
        (g11_top, 1, half), (g11_bottom, 1, half + half // 2), (g01, 0, half), (g10, 1, 0), (g00, 0, 0)
    ):
        for lanes in range(0, wide, 256):
            at = slice(lanes, lanes + 256)
            dst[:, at] = nn(cot_t[first : first + dst.shape[0], :], hid_ref[m, :, at]).astype(BF16)


def down_kernel(
    u0, u1, u2, u3, u4, hid_ref, slope_ref, mid_t, cot_r, w0, w1, w2, w3,
    out_o, grad_ref, bias_ref, g0, g1, g2, g3, d_ref, pre_ref, u_ref,
):
    half = g0.shape[0]
    block = half // 4
    assemble((u0, u1, u2, u3, u4), u_ref)
    assemble_quads((w0, w1, w2, w3), d_ref)
    wide = d_ref.shape[2]
    for m in range(2):
        for first in range(0, wide, 256):
            at = slice(first, first + 256)
            pre = (nn(cot_r[...], d_ref[m, :, at]) * slope_ref[m, :, at].astype(F32)).astype(BF16)
            pre_ref[m, :, at] = pre
            bias_ref[m : m + 1, at] = jnp.sum(pre.astype(F32), axis=0, keepdims=True)
    for first in range(0, cot_r.shape[1], 256):
        at = slice(first, first + 256)
        grad = (nt(pre_ref[0], u_ref[0, at, :]) + nt(pre_ref[1], u_ref[1, at, :])).astype(BF16)
        grad_ref[0, :, at] = grad[0:TEXT]
        grad_ref[1, :, at] = grad[TEXT:]
        out = (nt(hid_ref[0], d_ref[0, at, :]) + nt(hid_ref[1], d_ref[1, at, :])).astype(BF16)
        out_o[:, at] = out[0:TEXT]
        grad_ref[2, :, at] = out[TEXT:]
    for m in range(2):
        for ry in range(2):
            rows = slice((m * 2 + ry) * block, (m * 2 + ry + 1) * block)
            for first in range(0, wide, 256):
                at = slice(first, first + 256)
                grad = nn(mid_t[ry * half : (ry + 1) * half, :], pre_ref[m, :, at]).astype(BF16)
                for k, dst in enumerate((g0, g1, g2, g3)):
                    dst[rows, at] = grad[k * block : (k + 1) * block, :]


def attend_back_kernel(
    where, grad, grad_in, res_ref, cot_r, vec_r, wq_ref, wo_ref, y_ref, p_ref, unscaled, up_bias,
    rg_ref, agt_ref, dy_ref, back_o, back_p, sums, ag_ref, back_ref, dc_ref,
):
    lane = lax.broadcasted_iota(jnp.int32, (TEXT, 128), 1)
    row = lax.broadcasted_iota(jnp.int32, (128, TEXT), 0)
    zero = jnp.zeros((TEXT, 128), BF16)
    unit = eye(128)
    unit_t = eye(TEXT)
    for e in range(2):
        rows = slice(e * TEXT, (e + 1) * TEXT)
        mid_grad = grad[e].astype(F32) + grad_in[1 - e].astype(F32)
        normed, inverse = standard(res_ref[rows, :])
        cot = cot_r[rows, :].astype(F32)
        resid = cot + standard_back(normed, inverse, mid_grad, vec_r[2:3, :])
        low = resid.astype(BF16)
        ag_ref[rows, :] = low
        if e == 0:
            rg_ref[...] = resid
            sums[0:1, :] = jnp.sum(mid_grad * normed, axis=0, keepdims=True)
            sums[1:2, :] = jnp.sum(mid_grad, axis=0, keepdims=True)
            sums[2:3, :] = jnp.sum(low.astype(F32), axis=0, keepdims=True)
            sums[3:4, :] = jnp.sum(cot, axis=0, keepdims=True)
            sums[4:8, :] = jnp.zeros_like(sums[4:8, :])
    features = ag_ref.shape[1]
    agt_ref[...] = nt(eye(features), ag_ref[...]).astype(BF16)
    for first in range(0, 512, 256):
        at = slice(first, first + 256)
        dc_ref[:, at] = nn(ag_ref[...], wo_ref[:, at]).astype(BF16)

    def step(e, carry):
        rows = pl.ds(pl.multiple_of(e * TEXT, TEXT), TEXT)
        for m in range(2):
            dk, dv, dqt = [], [], []
            for head in range(3):
                qa, ka, va = head_lanes(m, head)
                low = lane < HEAD
                keep = low if head == 0 else ~low
                first = m * 128 if head < 2 else 256 + m * 128
                dc = jnp.where(keep, dc_ref[rows, first : first + 128], zero)
                q = jnp.where(~low if head == 1 else low, y_ref[e, SLOTS:KEYS, qa : qa + 128], zero)
                if head != 1:
                    kt_all = nt(unit, y_ref[e, :, ka : ka + 128]).astype(BF16)
                kt = kt_all[HEAD:128] if head == 1 else kt_all[0:HEAD]
                prob = p_ref[e, m * 3 + head]
                probs = prob.astype(F32)
                grad_p = nt(y_ref[e, :, va : va + 128], dc)
                dot = jnp.sum(probs * grad_p, axis=0, keepdims=True)
                score = (probs * (grad_p - dot)).astype(BF16)
                dk.append(nn(score, q))
                dv.append(nn(prob, dc))
                dqt.append(nn(kt, score))
            first = m * 640
            dv2 = dv[2].astype(BF16)
            dq01 = nt(unit_t, (jnp.concatenate([dqt[0], dqt[1]], axis=0) * SCALE).astype(BF16))
            dq2 = nt(
                unit_t,
                (jnp.concatenate([dqt[2], jnp.zeros((HEAD, TEXT), F32)], axis=0) * SCALE).astype(BF16),
            )
            dy_ref[e, 0:SLOTS, first : first + 128] = zero
            dy_ref[e, SLOTS:KEYS, first : first + 128] = dq01.astype(BF16)
            dy_ref[e, :, first + 128 : first + 256] = (dk[0] + dk[1]).astype(BF16)
            dy_ref[e, :, first + 256 : first + 384] = (dv[0] + dv[1]).astype(BF16)
            dy_ref[e, 0:SLOTS, first + 384 : first + 512] = dv2[0:SLOTS]
            dy_ref[e, SLOTS:KEYS, first + 384 : first + 512] = (dq2 + dv2[SLOTS:KEYS].astype(F32)).astype(BF16)
            dy_ref[e, :, first + 512 : first + 640] = dk[2].astype(BF16)
        return carry

    lax.fori_loop(0, 2, step, 0, unroll=True)
    for e in range(2):
        for first in range(0, features, 256):
            at = slice(first, first + 256)
            back_ref[e, :, at] = nt(dy_ref[e], wq_ref[at, :])
    bias = jnp.sum(dy_ref[0].astype(F32), axis=0, keepdims=True) + jnp.sum(
        dy_ref[1].astype(F32), axis=0, keepdims=True
    )
    back_o[...] = back_ref[0]
    back_p[0:KEYS, :] = back_ref[1].astype(BF16)
    for e in range(2):
        sums[4:5, :] += jnp.sum(back_ref[e] * unscaled[e].astype(F32), axis=0, keepdims=True)
        sums[5:6, :] += jnp.sum(back_ref[e], axis=0, keepdims=True)
    index = lax.broadcasted_iota(jnp.int32, (4, 1), 0)
    own, peer = index == where[4], index == where[5]
    sums[8:12, 0:640] = jnp.where(own, bias[:, 0:640], 0.0) + jnp.where(peer, bias[:, 640:1280], 0.0)
    sums[8:12, 640:768] = jnp.zeros((4, 128), F32)
    sums[12:16, :] = jnp.where(own, up_bias[0:1, :], 0.0) + jnp.where(peer, up_bias[1:2, :], 0.0)
    high = sums[...].astype(BF16)
    back_p[KEYS : KEYS + 16, :] = high
    back_p[KEYS + 16 : KEYS + 32, :] = (sums[...] - high.astype(F32)).astype(BF16)


def weight_kernel(
    xt_ref, agt_ref, dy_ref, ctx_ref, sums, back_in, hot_ref, g00, g01, g10, g11_top, g11_bottom, vec_ref,
):
    half = g00.shape[0]
    more = vec_ref.shape[0]
    vec = sums[...] + back_in[KEYS : KEYS + more, :].astype(F32) + back_in[KEYS + more :, :].astype(F32)
    vec_ref[...] = vec
    vec_ref[0:8, :] = restore(vec[0:8, :], hot_ref[...])
    high = vec_ref[...].astype(BF16)
    low = (vec_ref[...] - high.astype(F32)).astype(BF16)
    cut = g11_bottom.shape[0]
    g11_top[cut : cut + more, :] = high
    g11_top[cut + more :, :] = low
    dy = dy_ref[...].reshape(2 * KEYS, 1280)
    ctx = ctx_ref[...].reshape(2 * TEXT, 512)
    for ry in range(2):
        rows = slice(ry * half, (ry + 1) * half)
        out = [nn(agt_ref[rows, :], ctx[:, k * 256 : (k + 1) * 256]) for k in range(2)]

        def put(m, lanes, value):
            value = value.astype(BF16)
            if m == 0:
                (g00, g01)[ry][0:half, lanes] = value
            elif ry == 0:
                g10[0:half, lanes] = value
            else:
                g11_top[0:cut, lanes] = value[0:cut]
                g11_bottom[0:cut, lanes] = value[cut:]

        for chunk in range(5):
            grad = nn(xt_ref[rows, :], dy[:, chunk * 256 : (chunk + 1) * 256])
            for side in range(2):
                m, group = divmod(chunk * 2 + side, 5)
                value = grad[:, side * 128 : (side + 1) * 128]
                if group == 4:
                    value += out[1][:, m * 128 : (m + 1) * 128]
                put(m, slice(group * 128, (group + 1) * 128), value)
        for m in range(2):
            put(m, slice(640, 768), out[0][:, m * 128 : (m + 1) * 128])


def restore(v, hot):
    high = v.astype(BF16)
    low = (v - high.astype(F32)).astype(BF16)
    return nn(high, hot) + nn(low, hot)


def last_kernel(
    back_o, back_in, tok_r, mem_r, rg_ref, res_ref, out_o, out_in, vec_r, hot_ref,
    layer_ref, in_ref, mem_ref,
):
    hot = hot_ref[...]
    gain = vec_r[0:1, :]
    layer = (
        res_ref[0:TEXT, :] + (out_o[...].astype(F32) + out_in[2].astype(F32)) + vec_r[5:6, :]
    ).astype(BF16)
    layer_ref[...] = nn(layer, hot).astype(BF16)
    mem_back = back_o[0:SLOTS, :] + back_in[0:SLOTS, :].astype(F32)
    text_back = back_o[SLOTS:KEYS, :] + back_in[SLOTS:KEYS, :].astype(F32)
    normed, inverse = standard(tok_r[0:TEXT, :].astype(F32))
    in_ref[...] = restore(rg_ref[...] + standard_back(normed, inverse, text_back, gain), hot)
    normed, inverse = standard(mem_r[...].astype(F32))
    mem_ref[...] = restore(standard_back(normed, inverse, mem_back, gain), hot)[0:PATCHES, :]


def attend_call(where, split, length, parts, x, ok, after=()):
    features = x.shape[-1]
    return call(
        attend_kernel,
        [
            ((features, 1280), BF16), ((features, 512), BF16), ((2, KEYS, 1280), BF16), ((2, 6, KEYS, TEXT), BF16),
            ((2, TEXT, 512), BF16), ((2, TEXT, features), BF16), ((2, 1, features), F32),
        ],
        where, split, length, *parts, x, ok,
        smem=3, scratch=[pltpu.VMEM((8, 1280), F32), pltpu.VMEM((8, 1280), F32)], after=after,
    )


def back_call(where, grad, grad_in, res, cot_r, vec_r, wq, wo, y, p, unscaled, up_bias, after=()):
    features = res.shape[-1]
    return call(
        attend_back_kernel,
        [
            ((TEXT, features), F32), ((features, 2 * TEXT), BF16), ((2, KEYS, 1280), BF16),
            ((KEYS, features), F32), ((KEYS + 32, features), BF16), ((16, features), F32),
        ],
        where, grad, grad_in, res, cot_r, vec_r, wq, wo, y, p, unscaled, up_bias, smem=1, after=after,
        scratch=[
            pltpu.VMEM((2 * TEXT, features), BF16), pltpu.VMEM((2, KEYS, features), F32),
            pltpu.VMEM((2 * TEXT, 512), BF16),
        ],
    )


class Links:
    def __init__(self, dp, mp):
        self.dp, self.mp, self.depth = dp, mp, dp // 2
        self.x = self.pairs(lambda d, m: (d, m ^ 2))
        self.c = self.pairs(lambda d, m: (d, m ^ 1))
        self.y = self.pairs(lambda d, m: (d ^ 1, m))
        self.xy = self.pairs(lambda d, m: (d ^ 1, m ^ 2))

    def pairs(self, to):
        out = []
        for d in range(self.dp):
            for m in range(self.mp):
                d2, m2 = to(d, m)
                out.append((d * self.mp + m, d2 * self.mp + m2))
        return out

    def z(self, k):
        return self.pairs(lambda d, m: ((((d // 2 + k) % self.depth) * 2 + d % 2), m))

    def send(self, a, pairs):
        return lax.ppermute(a, AXES, pairs)

    def line(self, shard, *others, tail=None, ring=False, after=()):
        more = [] if tail is None else [tail]
        if self.depth == 4:
            pieces = [shard]
            for k in range(1, 4):
                pieces.append(self.send(pieces[-1], self.z(1)) if ring else self.send(shard, self.z(k)))
            pieces += more
            return call(
                functools.partial(join_kernel, len(pieces)),
                [((sum(p.shape[0] for p in pieces), shard.shape[1]), BF16)] + [(o.shape, o.dtype) for o in others],
                *pieces, *others, after=after,
            )
        held = shard[None]
        step = 1
        while step < self.depth:
            held = jnp.concatenate([held, self.send(held, self.z(step))], axis=0)
            step *= 2
        return (jnp.concatenate([held.reshape(-1, shard.shape[1])] + more, axis=0),) + tuple(others)

    def square(self, rows, half, after=()):
        own_y, peer = self.send(rows, self.y), self.send(rows, self.x)
        top, bottom = call(cut_kernel, [((half // 2, rows.shape[1]), BF16)] * 2, own_y, peer, after=after)
        return [rows, own_y, peer, self.send(top, self.x), self.send(bottom, self.y)], bottom

    def low(self, shard, after=()):
        own_y, peer = self.send(shard, self.y), self.send(shard, self.x)
        return call(
            functools.partial(join_kernel, 4), [((4 * shard.shape[0], shard.shape[1]), shard.dtype)],
            shard, own_y, peer, self.send(own_y, self.x), after=after,
        )[0]

    def quads(self, low):
        pieces = [low]
        if self.depth == 4:
            for _ in range(3):
                pieces.append(self.send(pieces[-1], self.z(1)))
            return pieces
        held = low[None]
        step = 1
        while step < self.depth:
            held = jnp.concatenate([held, self.send(held, self.z(step))], axis=0)
            step *= 2
        r, lanes = low.shape[0] // 4, low.shape[1]
        whole = held.reshape(self.depth, 4, r, lanes).transpose(1, 0, 2, 3).reshape(4, 4, -1, lanes)
        return [whole[:, k].reshape(-1, lanes) for k in range(4)]

    def turn(self, after, own, got, *parts):
        rows, lanes = parts[0].shape
        both, near, far = call(
            turn_kernel,
            [(own.shape, BF16), ((rows // 2, lanes), F32), ((rows // 2, lanes), BF16)],
            own, got, *parts, after=after,
        )
        return self.send(both, self.z(-1)), near, self.send(far, self.z(-2))

    def halve(self, pieces):
        lanes = pieces[0].shape[1]
        whole = jnp.stack([p.reshape(4, -1, lanes) for p in pieces], axis=1)
        whole = whole.reshape(4, self.depth, -1, lanes).transpose(1, 0, 2, 3).astype(F32)
        step = self.depth // 2
        while step >= 1:
            whole = whole[:step] + self.send(whole[step:].astype(BF16), self.z(-step)).astype(F32)
            step //= 2
        return whole.reshape(-1, lanes)

    def spread(self, after, low, one, two):
        r, lanes = low.shape[0] // 4, low.shape[1]
        t00, t01, t10, t11 = call(
            corner_kernel, [((r, lanes), F32)] + [((r, lanes), BF16)] * 3, low, one, two, after=after
        )
        return [t00, self.send(t11, self.xy), self.send(t01, self.y), self.send(t10, self.x)]

    def home(self, after, *parts):
        rows, lanes = parts[0].shape
        if self.depth == 4:
            r = rows // 4
            own, *rest = call(
                functools.partial(total_kernel, len(parts)),
                [((r, lanes), F32)] + [((r, lanes), BF16)] * 3, *parts, after=after,
            )
            return [own] + [self.send(rest[k], self.z(-k - 1)) for k in range(3)]
        held = sum(p.astype(F32) for p in parts).reshape(self.depth, -1, lanes)
        step = self.depth // 2
        while step >= 1:
            held = held[:step] + self.send(held[step:].astype(BF16), self.z(-step)).astype(F32)
            step //= 2
        return [held[0]]

    def meet(self, after, g01, g10, far_top, far_bottom):
        to_y, to_x = call(
            add_kernel, [(g01.shape, BF16), (g10.shape, BF16)], g01, far_top, g10, far_bottom, after=after
        )
        return self.send(to_y, self.y), self.send(to_x, self.x), to_x

    def meet_with(self, after, vec, g01, g10, far_top, far_bottom):
        to_y, to_x, vec = call(
            add_vec_kernel,
            [((g01.shape[0] + 2 * vec.shape[0], g01.shape[1]), BF16), (g10.shape, BF16), (vec.shape, F32)],
            vec, g01, far_top, g10, far_bottom, after=after,
        )
        return self.send(to_y, self.y), self.send(to_x, self.x), vec

    def fold(self, after, *parts):
        if self.depth != 4:
            return self.home(after, *parts)[0], None
        rows, lanes = parts[0].shape
        near, far = call(
            functools.partial(total_kernel, len(parts)),
            [((rows // 2, lanes), F32), ((rows // 2, lanes), BF16)], *parts, after=after,
        )
        return near, self.send(far, self.z(-2))

    def fold_more(self, after, near, far):
        if self.depth != 4:
            return [near]
        rows, lanes = near.shape
        own, other = call(
            functools.partial(total_kernel, 2),
            [((rows // 2, lanes), F32), ((rows // 2, lanes), BF16)], near, far, after=after,
        )
        return [own, self.send(other, self.z(-1))]

    def home_with(self, after, vec, own, *got):
        rows, lanes = own.shape
        more = vec.shape[0]
        if self.depth == 4:
            r = rows // 4
            vec, own, *rest = call(
                functools.partial(total_vec_kernel, 1 + len(got)),
                [(vec.shape, F32), ((r, lanes), F32)] + [((r + 2 * more, lanes), BF16)] * 3,
                vec, own, *got, after=after,
            )
            return [vec, own] + [self.send(rest[k], self.z(-k - 1)) for k in range(3)]
        for g in got:
            if g.shape[0] > rows:
                vec = vec + g[rows : rows + more].astype(F32) + g[rows + more :].astype(F32)
        step = 1
        while step < self.depth:
            vec = vec + self.send(vec, self.z(step))
            step *= 2
        return [vec] + self.home((), own, *(g[:rows] for g in got))


def add_up(parts):
    total = parts[0]
    for part in parts[1:]:
        total = total + part.astype(F32)
    return total


def per_device(
    tokens, memory, split_point, text_length, patch_mask,
    query_weight, query_bias, key_weight, value_weight, value_bias,
    out_weight, out_bias, attn_gain, attn_shift, mlp_gain, mlp_shift,
    up_weight, up_bias, down_weight, down_bias, cotangent,
):
    features = tokens.shape[1]
    width = query_weight.shape[1]
    hidden = up_weight.shape[1]
    dp, mp = lax.axis_size("dp"), lax.axis_size("mp")
    links = Links(dp, mp)
    dp_at, mp_at = lax.axis_index("dp"), lax.axis_index("mp")
    r = features // dp
    half = features // 2

    tok_p = links.send(tokens, links.c)
    mem_p = links.send(memory, links.c)
    cot_p = links.send(cotangent, links.c)
    (attn_own,) = call(
        pack_kernel, [((r, features), BF16)], query_weight, key_weight, value_weight, out_weight
    )
    (biases,) = call(
        bias_kernel, [((16, features), BF16)],
        query_bias.reshape(1, -1), value_bias.reshape(1, -1), up_bias.reshape(1, -1),
        after=(attn_own, tok_p, mem_p, cot_p),
    )

    low_d = links.low(down_weight.T, after=(biases,))
    quads_d = links.quads(low_d)
    rows_a, up_own = links.line(attn_own, up_weight, tail=biases, after=(low_d,))

    where = jnp.stack([dp_at // 2, dp_at % 2, mp_at, mp_at ^ 1, mp_at, mp_at ^ 2]).astype(jnp.int32)
    blank = jnp.zeros_like(attn_gain)
    vec = jnp.stack(
        [attn_gain, attn_shift, mlp_gain, mlp_shift, out_bias, down_bias] + [blank] * 10
    )
    x, xt, tok_r, cot_r, cot_t, mem_r, vec_r, hot, ok, unscaled = call(
        functools.partial(prep_kernel, dp // 2),
        [
            ((2, KEYS, features), BF16), ((features, 2 * KEYS), BF16),
            ((2 * TEXT, features), BF16), ((2 * TEXT, features), BF16), ((features, 2 * TEXT), BF16),
            ((SLOTS, features), BF16), ((16, features), F32), ((features, features), BF16),
            ((2, SLOTS, 128), F32), ((2, KEYS, features), BF16),
        ],
        where, tokens, tok_p, memory, mem_p, cotangent, cot_p, vec, patch_mask,
        smem=1, after=(rows_a,),
    )
    parts_a, token = links.square(rows_a, half, after=(ok,))
    (rows_u,) = links.line(up_own, ring=True, after=(token,))

    wq, wo, y, p, ctx, part, ub = attend_call(where, split_point, text_length, parts_a, x, ok, after=(rows_u,))
    part_in = links.send(part, links.c)
    parts_u, token = links.square(rows_u, half, after=(part,))
    (token,) = call(gate_kernel, [((8, 128), F32)], after=(token, *parts_u[3:]))

    quarter = ((half, hidden), BF16)
    eighth = ((half // 2, hidden), BF16)
    res, mid_t, hid, slope, d00, d01, d10, d11t, d11b = call(
        up_kernel,
        [
            ((2 * TEXT, features), F32), ((features, 2 * TEXT), BF16),
            ((2, 2 * TEXT, hidden), BF16), ((2, 2 * TEXT, hidden), BF16),
        ]
        + [quarter] * 3 + [eighth] * 2,
        part, part_in, tok_r, vec_r, cot_t, ub, *parts_u, after=(token,),
        scratch=[pltpu.VMEM((2 * TEXT, features), BF16), pltpu.VMEM((2, features, hidden), BF16)],
    )
    d_far = links.send(d11t, links.x), links.send(d11b, links.y)

    layer_o, mid_grad, up_bias_part, *u = call(
        down_kernel,
        [((TEXT, features), BF16), ((3, TEXT, features), BF16), ((2, hidden), F32)]
        + [quarter] * 4,
        *parts_u, hid, slope, mid_t, cot_r, *quads_d,
        scratch=[
            pltpu.VMEM((2, features, hidden), BF16), pltpu.VMEM((2, 2 * TEXT, hidden), BF16),
            pltpu.VMEM((2, features, hidden), BF16),
        ],
    )
    grad_in = links.send(mid_grad, links.c)
    d_y, d_x, token = links.meet((mid_grad,), d01, d10, *d_far)
    ring = links.depth == 4
    if ring:
        u_got = links.send(u[2], links.z(-1)), links.send(u[3], links.z(1))

    rg, ag_t, dy, back_o, back_p, sums = back_call(
        where, mid_grad, grad_in, res, cot_r, vec_r, wq, wo, y, p, unscaled, up_bias_part, after=(token,)
    )
    back_in = links.send(back_p, links.c)
    if ring:
        u_one, down_total, down_more = links.turn((dy,), u[1], u_got[0], d00, d_y, d_x)
        low, u_got = u[0], (u_one, u_got[1])
    else:
        down_total, down_more = links.fold((dy,), d00, d_y, d_x)
        low = links.halve(u)
        u_got = jnp.zeros_like(low), jnp.zeros_like(low)
    a00, a01, a10, a11t, a11b, stack = call(
        weight_kernel,
        [((half, features), BF16)] * 3
        + [((half // 2 + 32, features), BF16), ((half // 2, features), BF16), ((16, features), F32)],
        xt, ag_t, dy, ctx, sums, back_in, hot, after=(down_total,),
    )
    a_far = links.send(a11t, links.x), links.send(a11b, links.y)
    layer_out, input_grad, memory_grad = call(
        last_kernel,
        [((TEXT, features), BF16), ((TEXT, features), F32), ((PATCHES, features), F32)],
        back_o, back_in, tok_r, mem_r, rg, res, layer_o, grad_in, vec_r, hot, after=(a00,),
    )
    a_y, a_x, stack = links.meet_with((input_grad,), stack, a01, a10, *a_far)
    up_parts = links.spread((stack,), low, *u_got)
    down_parts = links.fold_more((up_parts[0],), down_total, down_more)
    attn_parts = links.home_with((down_parts[0],), stack, a00, a_y, a_x)
    query_sum, key_sum, value_sum, out_sum, stack = call(
        finish_kernel,
        [((r, width), F32)] * 3 + [((width, r), F32), (stack.shape, F32)], *attn_parts,
    )

    at = dp_at * mp + mp_at
    few = features // (dp * mp)
    q_bias = jnp.concatenate([stack[8:12, 0:128], stack[8:12, 384:448]], axis=1).reshape(1, features)
    v_bias = jnp.concatenate([stack[8:12, 256:384], stack[8:12, 448:512]], axis=1).reshape(1, features)
    vectors = lax.dynamic_slice(jnp.concatenate([stack[0:6], q_bias, v_bias]), (0, at * few), (8, few))
    many = up_bias.shape[0] // dp
    up_bias_sum = lax.dynamic_slice(stack[12:16].reshape(-1), (at * many,), (many,))

    return (
        layer_out, input_grad, memory_grad,
        query_sum, key_sum, value_sum, out_sum, add_up(up_parts), add_up(down_parts).T,
        vectors[6], vectors[7], up_bias_sum,
        vectors[2], vectors[3], vectors[4], vectors[5], vectors[0], vectors[1],
    )


def solution(mesh):
    rows = P(AXES, None)
    flat = P(AXES)
    in_specs = (
        rows, rows, P("dp"), P("dp"), P("dp", None),
        P("dp", "mp"), P("mp"), P("dp", "mp"), P("dp", "mp"), P("mp"),
        P("mp", "dp"), P(), P(), P(), P(), P(),
        P("dp", "mp"), P("mp"), P("mp", "dp"), P(), rows,
    )
    out_specs = (
        rows, rows, rows,
        P("dp", "mp"), P("dp", "mp"), P("dp", "mp"), P("mp", "dp"), P("dp", "mp"), P("mp", "dp"),
    ) + (flat,) * 9
    return jax.shard_map(
        per_device, mesh=mesh, in_specs=in_specs, out_specs=out_specs, check_vma=False
    )
```

```python
import functools

import jax
import jax.numpy as jnp
from jax import lax
from jax.experimental import pallas as pl
from jax.experimental.pallas import tpu as pltpu
from jax.sharding import PartitionSpec as P

HEAD = 64
TEXT = 256
PATCHES = 196
SLOTS = 256
KEYS = SLOTS + TEXT
EPS = 1e-06
NEG = -1000000000.0
SCALE = HEAD ** (-0.5)
F32 = jnp.float32
BF16 = jnp.bfloat16
AXES = ("dp", "mp")

CUT = 384


def nn(a, b):
    return lax.dot_general(a, b, (((1,), (0,)), ((), ())), preferred_element_type=F32)


def nt(a, b):
    return lax.dot_general(a, b, (((1,), (1,)), ((), ())), preferred_element_type=F32)


def eye(n):
    rows = lax.broadcasted_iota(jnp.int32, (n, n), 0)
    cols = lax.broadcasted_iota(jnp.int32, (n, n), 1)
    return (rows == cols).astype(F32).astype(BF16)


def standard(matrix):
    average = jnp.mean(matrix, axis=-1, keepdims=True)
    centered = matrix - average
    inverse = lax.rsqrt(jnp.mean(centered * centered, axis=-1, keepdims=True) + EPS)
    return centered * inverse, inverse


def standard_back(normed, inverse, grad_out, gain):
    scaled = grad_out * gain
    return inverse * (
        scaled
        - jnp.mean(scaled, axis=-1, keepdims=True)
        - normed * jnp.mean(scaled * normed, axis=-1, keepdims=True)
    )


UNIT = 1e9
COST = {
    "prep_kernel": 8.0, "attend_kernel": 17.0, "up_kernel": 9.0, "down_kernel": 9.0,
    "gate_kernel": 30.0, "add_kernel": 30.0, "pass_kernel": 30.0, "add_bottom_kernel": 30.0, "fold_kernel": 30.0, "corner_kernel": 30.0, "cut_kernel": 30.0, "attend_back_kernel": 19.0, "weight_kernel": 6.0, "last_kernel": 6.0,
}


ROOM = {
    "pack_kernel": 56,    "prep_kernel": 24, "attend_kernel": 26, "up_kernel": 26, "down_kernel": 26,
    "attend_back_kernel": 26, "weight_kernel": 20, "last_kernel": 16,
}


def call(kernel, out_shapes, *args, scratch=(), smem=0, after=(), anywhere=False):
    name = getattr(kernel, "func", kernel).__name__
    waits = len(after)

    def body(*refs):
        return kernel(*refs[waits:])

    place = pl.BlockSpec(memory_space=pl.ANY if anywhere else pltpu.VMEM)
    return pl.pallas_call(
        body,
        out_shape=[jax.ShapeDtypeStruct(s, d) for s, d in out_shapes],
        in_specs=[pl.BlockSpec(memory_space=pl.ANY)] * waits
        + [pl.BlockSpec(memory_space=pltpu.SMEM)] * smem
        + [place] * (len(args) - smem),
        out_specs=[place] * len(out_shapes),
        scratch_shapes=list(scratch),
        compiler_params=pltpu.CompilerParams(vmem_limit_bytes=ROOM.get(name, 8) * 1024 * 1024),
        cost_estimate=pl.CostEstimate(
            flops=int(COST.get(name, 2.0) * UNIT), bytes_accessed=0, transcendentals=0
        ),
        name=name,
    )(*after, *args)


def pack_kernel(q, k, v, o, a_ref):
    ot = nt(eye(q.shape[0]), o[...]).astype(BF16)
    a_ref[:, 0:128] = q[:, 0:128]
    a_ref[:, 128:256] = k[:, 0:128]
    a_ref[:, 256:384] = v[:, 0:128]
    a_ref[:, 384:512] = jnp.concatenate([q[:, 128:192], v[:, 128:192]], axis=1)
    a_ref[:, 512:640] = jnp.concatenate([k[:, 128:192], ot[:, 128:192]], axis=1)
    a_ref[:, 640:768] = ot[:, 0:128]


def bias_kernel(qb, vb, ub, bias_ref):
    blank = jnp.zeros((1, 128), F32)
    qf, vf = qb[...].astype(F32), vb[...].astype(F32)
    row = jnp.concatenate(
        [qf[:, 0:128], blank, vf[:, 0:128], qf[:, 128:192], vf[:, 128:192], blank, blank], axis=1
    )
    rest = jnp.zeros((14, row.shape[1]), F32)
    bias_ref[...] = jnp.concatenate([row, ub[...].astype(F32), rest], axis=0).astype(BF16)


def join_kernel(count, *refs):
    extra = (len(refs) - count - 1) // 2
    out, first = refs[count + extra], 0
    for piece in refs[:count]:
        out[first : first + piece.shape[0], :] = piece[...]
        first += piece.shape[0]
    for src, dst in zip(refs[count : count + extra], refs[count + extra + 1 :]):
        dst[...] = src[...]


def cut_kernel(a, b, out_a, out_b):
    cut = out_a.shape[0]
    out_a[...] = a[0:cut, :]
    out_b[...] = b[cut : 2 * cut, :]


def gate_kernel(token):
    token[...] = jnp.zeros_like(token)


def add_kernel(top, far_top, bottom, far_bottom, out_top, out_bottom):
    cut = far_top.shape[0]
    out_top[0:cut, :] = (top[0:cut, :].astype(F32) + far_top[...].astype(F32)).astype(BF16)
    out_top[cut:, :] = top[cut:, :]
    out_bottom[0:cut, :] = bottom[0:cut, :]
    out_bottom[cut:, :] = (bottom[cut:, :].astype(F32) + far_bottom[...].astype(F32)).astype(BF16)


def add_bottom_kernel(bottom, far_bottom, out):
    cut = far_bottom.shape[0]
    out[0:cut, :] = bottom[0:cut, :]
    out[cut:, :] = (bottom[cut:, :].astype(F32) + far_bottom[...].astype(F32)).astype(BF16)


def add_top_kernel(vec, top, far_top, out, vec_out):
    half, more = top.shape[0], vec.shape[0]
    cut = half // 2
    out[0:cut, :] = (top[0:cut, :].astype(F32) + far_top[0:cut, :].astype(F32)).astype(BF16)
    out[cut:half, :] = top[cut:, :]
    sums = vec[...] + far_top[cut : cut + more, :].astype(F32) + far_top[cut + more :, :].astype(F32)
    vec_out[...] = sums
    high = sums.astype(BF16)
    out[half : half + more, :] = high
    out[half + more :, :] = (sums - high.astype(F32)).astype(BF16)


def pass_kernel(one, got_one, low, got_low, out, low_out):
    out[...] = (one[...].astype(F32) + got_one[...].astype(F32)).astype(BF16)
    low_out[...] = (low[...].astype(F32) + got_low[...].astype(F32)).astype(BF16)


def fold_kernel(*refs):
    total_kernel(3, *refs)


def total_kernel(count, *refs):
    rows = refs[count].shape[0]
    for k, dst in enumerate(refs[count:]):
        at = slice(k * rows, (k + 1) * rows)
        value = refs[0][at, :].astype(F32)
        for other in refs[1:count]:
            value += other[at, :].astype(F32)
        dst[...] = value.astype(dst.dtype)


def final_kernel(
    vec, g00, from_y, from_x, low, one, near, far,
    vec_out, own, send1, send2, send3, top, side, down_own,
):
    rows, more = own.shape[0], vec.shape[0]
    first = 4 * rows
    for k, dst in enumerate((own, send1, send2, send3)):
        at = slice(k * rows, (k + 1) * rows)
        value = g00[at, :].astype(F32) + from_y[at, :].astype(F32) + from_x[at, :].astype(F32)
        dst[0:rows, :] = value.astype(dst.dtype)
    sums = vec[...]
    sums += from_y[first : first + more, :].astype(F32) + from_y[first + more :, :].astype(F32)
    vec_out[...] = sums
    high = sums.astype(BF16)
    rest = (sums - high.astype(F32)).astype(BF16)
    for dst in (send1, send2, send3):
        dst[rows : rows + more, :] = high
        dst[rows + more : rows + 2 * more, :] = rest
    down = near[...] + far[...].astype(F32)
    down_own[...] = down[0:rows]
    send1[rows + 2 * more :, :] = down[rows:].astype(BF16)
    total = low[...].astype(F32) + one[...].astype(F32)
    top[...] = total[0 : 2 * rows]
    side[...] = total[2 * rows :].astype(BF16)


def corner_kernel(top, got, own, out):
    rows = own.shape[0]
    own[...] = top[0:rows, :] + got[0:rows, :].astype(F32)
    out[...] = (top[rows:, :] + got[rows:, :].astype(F32)).astype(BF16)


def finish_kernel(*refs):
    vec, (parts, (q, k, v, o, vec_out)) = refs[0], (refs[1:-5], refs[-5:])
    rows, more = parts[0].shape[0], vec.shape[0]
    total = parts[0][...]
    sums = vec[...]
    for part in parts[1:]:
        total += part[0:rows, :].astype(F32)
        sums += part[rows : rows + more, :].astype(F32) + part[rows + more : rows + 2 * more, :].astype(F32)
    vec_out[...] = sums
    q[...] = jnp.concatenate([total[:, 0:128], total[:, 384:448]], axis=1)
    k[...] = jnp.concatenate([total[:, 128:256], total[:, 512:576]], axis=1)
    v[...] = jnp.concatenate([total[:, 256:384], total[:, 448:512]], axis=1)
    out = jnp.concatenate([total[:, 640:768], total[:, 576:640]], axis=1)
    high = out.astype(BF16)
    low = (out - high.astype(F32)).astype(BF16)
    unit = eye(out.shape[1])
    o[...] = nt(unit, high) + nt(unit, low)


def place_of(depth, r, z, y, count):
    rel = lax.broadcasted_iota(jnp.int32, (count, 1), 0)
    half = count // 2
    ry = (rel >= half).astype(jnp.int32)
    rest = rel - ry * half
    rz = jnp.zeros_like(rel)
    for k in range(1, depth):
        rz += (rest >= k * r).astype(jnp.int32)
    az = z - rz
    az += depth * (az < 0).astype(jnp.int32)
    ay = y + ry - 2 * y * ry
    return az * (2 * r) + ay * r + rest - rz * r


def prep_kernel(
    depth, where, tok_o, tok_p, mem_o, mem_p, cot_o, cot_p, vec, patch,
    x_ref, xt_ref, tok_r, cot_r, cot_t, mem_r, vec_r, hot_ref, ok_ref, unscaled,
):
    features = tok_o.shape[1]
    lane = lax.broadcasted_iota(jnp.int32, (features, features), 1)
    place = place_of(depth, features // (2 * depth), where[0], where[1], features)
    hot_ref[...] = (lane == place).astype(F32).astype(BF16)
    gain = vec[0:1, :].astype(F32)
    shift = vec[1:2, :].astype(F32)
    vec_r[...] = nt(vec[...], hot_ref[...])
    rows = lax.broadcasted_iota(jnp.int32, (SLOTS, PATCHES), 0)
    cols = lax.broadcasted_iota(jnp.int32, (SLOTS, PATCHES), 1)
    columns = nt((rows == cols).astype(F32), (patch[...] > 0).astype(F32))
    which = lax.broadcasted_iota(jnp.int32, columns.shape, 1)
    for at in range(2):
        one = jnp.sum(jnp.where(which == where[2 + at], columns, 0.0), axis=1, keepdims=True)
        ok_ref[at] = jnp.broadcast_to(one, (SLOTS, 128))

    for at, (mem, tok) in enumerate(((mem_o, tok_o), (mem_p, tok_p))):
        normed, _ = standard(tok[...].astype(F32))
        low = (normed * gain + shift).astype(BF16)
        x_ref[at, SLOTS:KEYS, :] = nt(low, hot_ref[...]).astype(BF16)
        unscaled[at, SLOTS:KEYS, :] = nt(normed.astype(BF16), hot_ref[...]).astype(BF16)
        xt_ref[:, at * KEYS + SLOTS : (at + 1) * KEYS] = nt(hot_ref[...], low).astype(BF16)
        normed, _ = standard(mem[...].astype(F32))
        normed = jnp.concatenate([normed, jnp.zeros((SLOTS - PATCHES, features), F32)], axis=0)
        unscaled[at, 0:SLOTS, :] = nt(normed.astype(BF16), hot_ref[...]).astype(BF16)
        low = (normed * gain + shift).astype(BF16)
        x_ref[at, 0:SLOTS, :] = nt(low, hot_ref[...]).astype(BF16)
        xt_ref[:, at * KEYS : at * KEYS + SLOTS] = nt(hot_ref[...], low).astype(BF16)
    raw = jnp.concatenate([mem_o[...].astype(F32), jnp.zeros((SLOTS - PATCHES, features), F32)], axis=0)
    mem_r[...] = nt(raw.astype(BF16), hot_ref[...]).astype(BF16)
    for at, (tok, cot) in enumerate(((tok_o, cot_o), (tok_p, cot_p))):
        rows = slice(at * TEXT, (at + 1) * TEXT)
        tok_r[rows, :] = nt(tok[...], hot_ref[...]).astype(BF16)
        cot_r[rows, :] = nt(cot[...], hot_ref[...]).astype(BF16)
        cot_t[:, rows] = nt(hot_ref[...], cot[...]).astype(BF16)


def assemble(parts, w_ref):
    own, own_y, peer, far_top, far_bottom = parts
    half, cut = w_ref.shape[1] // 2, far_top.shape[0]
    w_ref[0, 0:half, :] = own[0:half, :]
    w_ref[0, half : 2 * half, :] = own_y[0:half, :]
    w_ref[1, 0:half, :] = peer[0:half, :]
    w_ref[1, half : half + cut, :] = far_top[...]
    w_ref[1, half + cut : 2 * half, :] = far_bottom[...]


def assemble_quads(pieces, w_ref):
    block = pieces[0].shape[0] // 4
    for k, piece in enumerate(pieces):
        for quarter in range(4):
            first = (quarter % 2) * 4 * block + k * block
            w_ref[quarter // 2, first : first + block, :] = piece[quarter * block : (quarter + 1) * block, :]


def head_lanes(m, head):
    first = m * 640
    if head < 2:
        return first, first + 128, first + 256
    return first + 384, first + 512, first + 384


def attend_kernel(
    where, split, length,
    own, own_y, peer, far_top, far_bottom, x_ref, ok_ref,
    wq_ref, wo_ref, y_ref, p_ref, ctx_ref, part_ref, up_ref, bias, factor,
):
    half, cut = wq_ref.shape[0] // 2, far_top.shape[0]
    for m, first, src, size in (
        (0, 0, own, half), (0, half, own_y, half), (1, 0, peer, half),
        (1, half, far_top, cut), (1, half + cut, far_bottom, cut),
    ):
        rows = slice(first, first + size)
        wq_ref[rows, m * 640 : (m + 1) * 640] = src[0:size, 0:640]
        wo_ref[rows, m * 128 : (m + 1) * 128] = src[0:size, 640:768]
        wo_ref[rows, 256 + m * 128 : 384 + m * 128] = src[0:size, 512:640]
    lane = lax.broadcasted_iota(jnp.int32, (1, 128), 1)
    one = jnp.ones((1, 128), F32)
    for m, src in enumerate((own, peer)):
        tail = src[half : half + 16, :].astype(F32)
        bias[0:1, m * 640 : (m + 1) * 640] = tail[0:1, 0:640]
        up_ref[m] = tail[1:2, :]
        for group, value in enumerate(
            (one * SCALE, one, one, jnp.where(lane < HEAD, SCALE, 1.0), jnp.where(lane < HEAD, 1.0, 0.0))
        ):
            first = m * 640 + group * 128
            factor[0:1, first : first + 128] = value
    for e in range(2):
        for first in range(0, 1280, 256):
            at = slice(first, first + 256)
            y = (nn(x_ref[e], wq_ref[:, at]) + bias[0:1, at]) * factor[0:1, at]
            y_ref[e, :, at] = y.astype(BF16)

    lane = lax.broadcasted_iota(jnp.int32, (TEXT, 128), 1)
    zero = jnp.zeros((TEXT, 128), BF16)
    unit = eye(128)
    unit_t = eye(TEXT)
    key_place = lax.broadcasted_iota(jnp.int32, (TEXT, TEXT), 0)
    query_place = lax.broadcasted_iota(jnp.int32, (TEXT, TEXT), 1)

    def step(e, carry):
        patch_ok = jnp.concatenate([ok_ref[e], ok_ref[e]], axis=1) > 0.0
        prefix, valid = split[where[2 + e]], length[where[2 + e]]
        text_ok = ((key_place < prefix) | (key_place <= query_place)) & (key_place < valid)
        for m in range(2):
            parts = []
            for head in range(3):
                qa, ka, va = head_lanes(m, head)
                low = head != 1
                q = jnp.where((lane < HEAD) if low else (lane >= HEAD), y_ref[e, SLOTS:KEYS, qa : qa + 128], zero)
                if head != 1:
                    vt_all = nt(unit, y_ref[e, :, va : va + 128]).astype(BF16)
                vt = vt_all[0:HEAD] if head == 0 else vt_all[HEAD:128]
                s_mem = jnp.where(patch_ok, nt(y_ref[e, 0:SLOTS, ka : ka + 128], q), NEG)
                s_text = jnp.where(text_ok, nt(y_ref[e, SLOTS:KEYS, ka : ka + 128], q), NEG)
                largest = jnp.maximum(
                    jnp.max(s_mem, axis=0, keepdims=True), jnp.max(s_text, axis=0, keepdims=True)
                )
                e_mem = jnp.exp(s_mem - largest)
                e_text = jnp.exp(s_text - largest)
                total = jnp.sum(e_mem, axis=0, keepdims=True) + jnp.sum(e_text, axis=0, keepdims=True)
                inverse = 1.0 / total
                p_mem = (e_mem * inverse).astype(BF16)
                p_text = (e_text * inverse).astype(BF16)
                p_ref[e, m * 3 + head, 0:SLOTS, :] = p_mem
                p_ref[e, m * 3 + head, SLOTS:KEYS, :] = p_text
                parts.append(nn(vt[:, 0:SLOTS], p_mem) + nn(vt[:, SLOTS:KEYS], p_text))
            c01t = jnp.concatenate([parts[0], parts[1]], axis=0).astype(BF16)
            c2t = jnp.concatenate([jnp.zeros((HEAD, TEXT), F32), parts[2]], axis=0).astype(BF16)
            ctx_ref[e, :, m * 128 : (m + 1) * 128] = nt(unit_t, c01t).astype(BF16)
            ctx_ref[e, :, 256 + m * 128 : 384 + m * 128] = nt(unit_t, c2t).astype(BF16)
        return carry

    lax.fori_loop(0, 2, step, 0, unroll=True)
    features = wo_ref.shape[0]
    ctx = ctx_ref[...].reshape(2 * TEXT, 512)
    for first in range(0, features, 256):
        at = slice(first, first + 256)
        part_ref[:, :, at] = nt(ctx, wo_ref[at, :]).astype(BF16).reshape(2, TEXT, 256)


def gelu_pair(v):
    c = 0.7978845608028654
    square = v * v
    t = jnp.tanh(c * v * (1.0 + 0.044715 * square))
    gelu = 0.5 * v * (1.0 + t)
    slope = 0.5 * (1.0 + t) + 0.5 * v * (1.0 - t * t) * (c * (1.0 + 3 * 0.044715 * square))
    return gelu, slope


def up_kernel(
    part, part_in, tok_r, vec_r, cot_t, bias, u0, u1, u2, u3, u4,
    res_ref, mid_t, hid_ref, slope_ref, g00, g01, g10, g11_top, g11_bottom, mid_ref, u_ref,
):
    half = g00.shape[0]
    assemble((u0, u1, u2, u3, u4), u_ref)
    for e in range(2):
        rows = slice(e * TEXT, (e + 1) * TEXT)
        res = (
            tok_r[rows, :].astype(F32)
            + (part[e].astype(F32) + part_in[1 - e].astype(F32))
            + vec_r[4:5, :]
        )
        res_ref[rows, :] = res
        normed, _ = standard(res)
        mid_ref[rows, :] = (normed * vec_r[2:3, :] + vec_r[3:4, :]).astype(BF16)
    mid_t[...] = nt(eye(mid_ref.shape[1]), mid_ref[...]).astype(BF16)
    wide = u_ref.shape[2]
    for m in range(2):
        for first in range(0, wide, 256):
            at = slice(first, first + 256)
            gelu, slope = gelu_pair(nn(mid_ref[...], u_ref[m, :, at]) + bias[m, :, at])
            hid_ref[m, :, at] = gelu.astype(BF16)
            slope_ref[m, :, at] = slope.astype(BF16)
    for dst, m, first in (
        (g11_top, 1, half), (g11_bottom, 1, half + half // 2), (g01, 0, half), (g10, 1, 0), (g00, 0, 0)
    ):
        for lanes in range(0, wide, 256):
            at = slice(lanes, lanes + 256)
            dst[:, at] = nn(cot_t[first : first + dst.shape[0], :], hid_ref[m, :, at]).astype(BF16)


def down_kernel(
    u0, u1, u2, u3, u4, hid_ref, slope_ref, mid_t, cot_r, w0, w1, w2, w3,
    out_o, grad_ref, bias_ref, g0, g1, g2, g3, d_ref, pre_ref, u_ref,
):
    half = g0.shape[0]
    block = half // 4
    assemble((u0, u1, u2, u3, u4), u_ref)
    assemble_quads((w0, w1, w2, w3), d_ref)
    wide = d_ref.shape[2]
    for m in range(2):
        for first in range(0, wide, 256):
            at = slice(first, first + 256)
            pre = (nn(cot_r[...], d_ref[m, :, at]) * slope_ref[m, :, at].astype(F32)).astype(BF16)
            pre_ref[m, :, at] = pre
            bias_ref[m : m + 1, at] = jnp.sum(pre.astype(F32), axis=0, keepdims=True)
    for first in range(0, cot_r.shape[1], 256):
        at = slice(first, first + 256)
        grad = (nt(pre_ref[0], u_ref[0, at, :]) + nt(pre_ref[1], u_ref[1, at, :])).astype(BF16)
        grad_ref[0, :, at] = grad[0:TEXT]
        grad_ref[1, :, at] = grad[TEXT:]
        out = (nt(hid_ref[0], d_ref[0, at, :]) + nt(hid_ref[1], d_ref[1, at, :])).astype(BF16)
        out_o[:, at] = out[0:TEXT]
        grad_ref[2, :, at] = out[TEXT:]
    for m in range(2):
        for ry in range(2):
            rows = slice((m * 2 + ry) * block, (m * 2 + ry + 1) * block)
            for first in range(0, wide, 256):
                at = slice(first, first + 256)
                grad = nn(mid_t[ry * half : (ry + 1) * half, :], pre_ref[m, :, at]).astype(BF16)
                for k, dst in enumerate((g0, g1, g2, g3)):
                    dst[rows, at] = grad[k * block : (k + 1) * block, :]


def attend_back_kernel(
    where, grad, grad_in, res_ref, cot_r, vec_r, wq_ref, wo_ref, y_ref, p_ref, unscaled, up_bias,
    rg_ref, agt_ref, dy_ref, back_o, back_p, sums, ag_ref, back_ref, dc_ref,
):
    lane = lax.broadcasted_iota(jnp.int32, (TEXT, 128), 1)
    row = lax.broadcasted_iota(jnp.int32, (128, TEXT), 0)
    zero = jnp.zeros((TEXT, 128), BF16)
    unit = eye(128)
    unit_t = eye(TEXT)
    for e in range(2):
        rows = slice(e * TEXT, (e + 1) * TEXT)
        mid_grad = grad[e].astype(F32) + grad_in[1 - e].astype(F32)
        normed, inverse = standard(res_ref[rows, :])
        cot = cot_r[rows, :].astype(F32)
        resid = cot + standard_back(normed, inverse, mid_grad, vec_r[2:3, :])
        low = resid.astype(BF16)
        ag_ref[rows, :] = low
        if e == 0:
            rg_ref[...] = resid
            sums[0:1, :] = jnp.sum(mid_grad * normed, axis=0, keepdims=True)
            sums[1:2, :] = jnp.sum(mid_grad, axis=0, keepdims=True)
            sums[2:3, :] = jnp.sum(low.astype(F32), axis=0, keepdims=True)
            sums[3:4, :] = jnp.sum(cot, axis=0, keepdims=True)
            sums[4:8, :] = jnp.zeros_like(sums[4:8, :])
    features = ag_ref.shape[1]
    agt_ref[...] = nt(eye(features), ag_ref[...]).astype(BF16)
    for first in range(0, 512, 256):
        at = slice(first, first + 256)
        dc_ref[:, at] = nn(ag_ref[...], wo_ref[:, at]).astype(BF16)

    def step(e, carry):
        rows = pl.ds(pl.multiple_of(e * TEXT, TEXT), TEXT)
        for m in range(2):
            dk, dv, dqt = [], [], []
            for head in range(3):
                qa, ka, va = head_lanes(m, head)
                low = lane < HEAD
                keep = low if head == 0 else ~low
                first = m * 128 if head < 2 else 256 + m * 128
                dc = jnp.where(keep, dc_ref[rows, first : first + 128], zero)
                q = jnp.where(~low if head == 1 else low, y_ref[e, SLOTS:KEYS, qa : qa + 128], zero)
                if head != 1:
                    kt_all = nt(unit, y_ref[e, :, ka : ka + 128]).astype(BF16)
                kt = kt_all[HEAD:128] if head == 1 else kt_all[0:HEAD]
                prob = p_ref[e, m * 3 + head]
                probs = prob.astype(F32)
                grad_p = nt(y_ref[e, :, va : va + 128], dc)
                dot = jnp.sum(probs * grad_p, axis=0, keepdims=True)
                score = (probs * (grad_p - dot)).astype(BF16)
                dk.append(nn(score, q))
                dv.append(nn(prob, dc))
                dqt.append(nn(kt, score))
            first = m * 640
            dv2 = dv[2].astype(BF16)
            dq01 = nt(unit_t, (jnp.concatenate([dqt[0], dqt[1]], axis=0) * SCALE).astype(BF16))
            dq2 = nt(
                unit_t,
                (jnp.concatenate([dqt[2], jnp.zeros((HEAD, TEXT), F32)], axis=0) * SCALE).astype(BF16),
            )
            dy_ref[e, 0:SLOTS, first : first + 128] = zero
            dy_ref[e, SLOTS:KEYS, first : first + 128] = dq01.astype(BF16)
            dy_ref[e, :, first + 128 : first + 256] = (dk[0] + dk[1]).astype(BF16)
            dy_ref[e, :, first + 256 : first + 384] = (dv[0] + dv[1]).astype(BF16)
            dy_ref[e, 0:SLOTS, first + 384 : first + 512] = dv2[0:SLOTS]
            dy_ref[e, SLOTS:KEYS, first + 384 : first + 512] = (dq2 + dv2[SLOTS:KEYS].astype(F32)).astype(BF16)
            dy_ref[e, :, first + 512 : first + 640] = dk[2].astype(BF16)
        return carry

    lax.fori_loop(0, 2, step, 0, unroll=True)
    for e in range(2):
        for first in range(0, features, 256):
            at = slice(first, first + 256)
            back_ref[e, :, at] = nt(dy_ref[e], wq_ref[at, :])
    bias = jnp.sum(dy_ref[0].astype(F32), axis=0, keepdims=True) + jnp.sum(
        dy_ref[1].astype(F32), axis=0, keepdims=True
    )
    back_o[...] = back_ref[0]
    back_p[0:KEYS, :] = back_ref[1].astype(BF16)
    for e in range(2):
        sums[4:5, :] += jnp.sum(back_ref[e] * unscaled[e].astype(F32), axis=0, keepdims=True)
        sums[5:6, :] += jnp.sum(back_ref[e], axis=0, keepdims=True)
    index = lax.broadcasted_iota(jnp.int32, (4, 1), 0)
    own, peer = index == where[4], index == where[5]
    sums[8:12, 0:640] = jnp.where(own, bias[:, 0:640], 0.0) + jnp.where(peer, bias[:, 640:1280], 0.0)
    sums[8:12, 640:768] = jnp.zeros((4, 128), F32)
    sums[12:16, :] = jnp.where(own, up_bias[0:1, :], 0.0) + jnp.where(peer, up_bias[1:2, :], 0.0)
    high = sums[...].astype(BF16)
    back_p[KEYS : KEYS + 16, :] = high
    back_p[KEYS + 16 : KEYS + 32, :] = (sums[...] - high.astype(F32)).astype(BF16)


def weight_kernel(
    xt_ref, agt_ref, dy_ref, ctx_ref, sums, back_in, hot_ref, g00, g01, g10, g11_top, g11_bottom, vec_ref,
):
    half = g00.shape[0]
    more = vec_ref.shape[0]
    vec = sums[...] + back_in[KEYS : KEYS + more, :].astype(F32) + back_in[KEYS + more :, :].astype(F32)
    vec_ref[...] = vec
    vec_ref[0:8, :] = restore(vec[0:8, :], hot_ref[...])
    high = vec_ref[...].astype(BF16)
    low = (vec_ref[...] - high.astype(F32)).astype(BF16)
    cut = g11_bottom.shape[0]
    g11_top[cut : cut + more, :] = high
    g11_top[cut + more :, :] = low
    dy = dy_ref[...].reshape(2 * KEYS, 1280)
    ctx = ctx_ref[...].reshape(2 * TEXT, 512)
    for ry in range(2):
        rows = slice(ry * half, (ry + 1) * half)
        out = [nn(agt_ref[rows, :], ctx[:, k * 256 : (k + 1) * 256]) for k in range(2)]

        def put(m, lanes, value):
            value = value.astype(BF16)
            if m == 0:
                (g00, g01)[ry][0:half, lanes] = value
            elif ry == 0:
                g10[0:half, lanes] = value
            else:
                g11_top[0:cut, lanes] = value[0:cut]
                g11_bottom[0:cut, lanes] = value[cut:]

        for chunk in range(5):
            grad = nn(xt_ref[rows, :], dy[:, chunk * 256 : (chunk + 1) * 256])
            for side in range(2):
                m, group = divmod(chunk * 2 + side, 5)
                value = grad[:, side * 128 : (side + 1) * 128]
                if group == 4:
                    value += out[1][:, m * 128 : (m + 1) * 128]
                put(m, slice(group * 128, (group + 1) * 128), value)
        for m in range(2):
            put(m, slice(640, 768), out[0][:, m * 128 : (m + 1) * 128])


def restore(v, hot):
    high = v.astype(BF16)
    low = (v - high.astype(F32)).astype(BF16)
    return nn(high, hot) + nn(low, hot)


def last_kernel(
    back_o, back_in, tok_r, mem_r, rg_ref, res_ref, out_o, out_in, vec_r, hot_ref,
    layer_ref, in_ref, mem_ref,
):
    hot = hot_ref[...]
    gain = vec_r[0:1, :]
    layer = (
        res_ref[0:TEXT, :] + (out_o[...].astype(F32) + out_in[2].astype(F32)) + vec_r[5:6, :]
    ).astype(BF16)
    layer_ref[...] = nn(layer, hot).astype(BF16)
    mem_back = back_o[0:SLOTS, :] + back_in[0:SLOTS, :].astype(F32)
    text_back = back_o[SLOTS:KEYS, :] + back_in[SLOTS:KEYS, :].astype(F32)
    normed, inverse = standard(tok_r[0:TEXT, :].astype(F32))
    in_ref[...] = restore(rg_ref[...] + standard_back(normed, inverse, text_back, gain), hot)
    normed, inverse = standard(mem_r[...].astype(F32))
    mem_ref[...] = restore(standard_back(normed, inverse, mem_back, gain), hot)[0:PATCHES, :]


def attend_call(where, split, length, parts, x, ok, after=()):
    features = x.shape[-1]
    return call(
        attend_kernel,
        [
            ((features, 1280), BF16), ((features, 512), BF16), ((2, KEYS, 1280), BF16), ((2, 6, KEYS, TEXT), BF16),
            ((2, TEXT, 512), BF16), ((2, TEXT, features), BF16), ((2, 1, features), F32),
        ],
        where, split, length, *parts, x, ok,
        smem=3, scratch=[pltpu.VMEM((8, 1280), F32), pltpu.VMEM((8, 1280), F32)], after=after,
    )


def back_call(where, grad, grad_in, res, cot_r, vec_r, wq, wo, y, p, unscaled, up_bias, after=()):
    features = res.shape[-1]
    return call(
        attend_back_kernel,
        [
            ((TEXT, features), F32), ((features, 2 * TEXT), BF16), ((2, KEYS, 1280), BF16),
            ((KEYS, features), F32), ((KEYS + 32, features), BF16), ((16, features), F32),
        ],
        where, grad, grad_in, res, cot_r, vec_r, wq, wo, y, p, unscaled, up_bias, smem=1, after=after,
        scratch=[
            pltpu.VMEM((2 * TEXT, features), BF16), pltpu.VMEM((2, KEYS, features), F32),
            pltpu.VMEM((2 * TEXT, 512), BF16),
        ],
    )


class Links:
    def __init__(self, dp, mp):
        self.dp, self.mp, self.depth = dp, mp, dp // 2
        self.x = self.pairs(lambda d, m: (d, m ^ 2))
        self.c = self.pairs(lambda d, m: (d, m ^ 1))
        self.y = self.pairs(lambda d, m: (d ^ 1, m))

    def pairs(self, to):
        out = []
        for d in range(self.dp):
            for m in range(self.mp):
                d2, m2 = to(d, m)
                out.append((d * self.mp + m, d2 * self.mp + m2))
        return out

    def z(self, k):
        return self.pairs(lambda d, m: ((((d // 2 + k) % self.depth) * 2 + d % 2), m))

    def send(self, a, pairs):
        return lax.ppermute(a, AXES, pairs)

    def line(self, shard, *others, tail=None, ring=False, after=()):
        more = [] if tail is None else [tail]
        if self.depth == 4:
            pieces = [shard]
            for k in range(1, 4):
                pieces.append(self.send(pieces[-1], self.z(1)) if ring else self.send(shard, self.z(k)))
            pieces += more
            return call(
                functools.partial(join_kernel, len(pieces)),
                [((sum(p.shape[0] for p in pieces), shard.shape[1]), BF16)] + [(o.shape, o.dtype) for o in others],
                *pieces, *others, after=after,
            )
        held = shard[None]
        step = 1
        while step < self.depth:
            held = jnp.concatenate([held, self.send(held, self.z(step))], axis=0)
            step *= 2
        return (jnp.concatenate([held.reshape(-1, shard.shape[1])] + more, axis=0),) + tuple(others)

    def square(self, rows, half, after=()):
        own_y, peer = self.send(rows, self.y), self.send(rows, self.x)
        top, bottom = call(cut_kernel, [((half // 2, rows.shape[1]), BF16)] * 2, own_y, peer, after=after)
        return [rows, own_y, peer, self.send(top, self.x), self.send(bottom, self.y)], bottom

    def low(self, shard, after=()):
        own_y, peer = self.send(shard, self.y), self.send(shard, self.x)
        return call(
            functools.partial(join_kernel, 4), [((4 * shard.shape[0], shard.shape[1]), shard.dtype)],
            shard, own_y, peer, self.send(own_y, self.x), after=after,
        )[0]

    def quads(self, low):
        pieces = [low]
        if self.depth == 4:
            for _ in range(3):
                pieces.append(self.send(pieces[-1], self.z(1)))
            return pieces
        held = low[None]
        step = 1
        while step < self.depth:
            held = jnp.concatenate([held, self.send(held, self.z(step))], axis=0)
            step *= 2
        r, lanes = low.shape[0] // 4, low.shape[1]
        whole = held.reshape(self.depth, 4, r, lanes).transpose(1, 0, 2, 3).reshape(4, 4, -1, lanes)
        return [whole[:, k].reshape(-1, lanes) for k in range(4)]

    def halve(self, pieces):
        lanes = pieces[0].shape[1]
        whole = jnp.stack([p.reshape(4, -1, lanes) for p in pieces], axis=1)
        whole = whole.reshape(4, self.depth, -1, lanes).transpose(1, 0, 2, 3).astype(F32)
        step = self.depth // 2
        while step >= 1:
            whole = whole[:step] + self.send(whole[step:].astype(BF16), self.z(-step)).astype(F32)
            step //= 2
        return whole.reshape(-1, lanes)

    def home(self, after, *parts):
        rows, lanes = parts[0].shape
        held = sum(p.astype(F32) for p in parts).reshape(self.depth, -1, lanes)
        step = self.depth // 2
        while step >= 1:
            held = held[:step] + self.send(held[step:].astype(BF16), self.z(-step)).astype(F32)
            step //= 2
        return [held[0]]

    def meet(self, after, g01, g10, far_top, far_bottom):
        to_y, to_x = call(
            add_kernel, [(g01.shape, BF16), (g10.shape, BF16)], g01, far_top, g10, far_bottom, after=after
        )
        return self.send(to_y, self.y), self.send(to_x, self.x), to_x

    def meet_with(self, after, vec, g01, g10, far_top, far_bottom):
        (to_x,) = call(add_bottom_kernel, [(g10.shape, BF16)], g10, far_bottom, after=after)
        to_y, vec = call(
            add_top_kernel, [((g01.shape[0] + 2 * vec.shape[0], g01.shape[1]), BF16), (vec.shape, F32)],
            vec, g01, far_top, after=(to_x,),
        )
        return self.send(to_y, self.y), self.send(to_x, self.x), vec

    def wind_up(self, vec, attn, up, down):
        (g00, from_y, from_x), (low, one), (near, far) = attn, up, down
        more, lanes = vec.shape
        r = low.shape[0] // 4
        if self.depth == 4:
            after = call(gate_kernel, [((8, 128), F32)], after=(one, far))
            vec, own, s1, s2, s3, top, side, down_own = call(
                final_kernel,
                [(vec.shape, F32), ((r, lanes), F32), ((2 * r + 2 * more, lanes), BF16)]
                + [((r + 2 * more, lanes), BF16)] * 2
                + [((2 * r, lanes), F32), ((2 * r, lanes), BF16), ((r, lanes), F32)],
                vec, g00, from_y, from_x, low, one, near, far, after=after,
            )
            got = [self.send(s, self.z(-k - 1)) for k, s in enumerate((s1, s2, s3))]
            attn_parts = [vec, own] + got
            down_parts = [down_own, got[0][r + 2 * more :]]
        else:
            rows = g00.shape[0]
            vec = vec + from_y[rows : rows + more].astype(F32) + from_y[rows + more :].astype(F32)
            step = 1
            while step < self.depth:
                vec = vec + self.send(vec, self.z(step))
                step *= 2
            attn_parts = [vec] + self.home((), g00, from_y[:rows], from_x)
            down_parts = [near]
            total = low.astype(F32)
            top, side = total[: 2 * r], total[2 * r :].astype(BF16)
        up_own, out = call(
            corner_kernel, [((r, lanes), F32), ((r, lanes), BF16)], top, self.send(side, self.x)
        )
        return attn_parts, [up_own, self.send(out, self.y)], down_parts


def add_up(parts):
    total = parts[0]
    for part in parts[1:]:
        total = total + part.astype(F32)
    return total


def per_device(
    tokens, memory, split_point, text_length, patch_mask,
    query_weight, query_bias, key_weight, value_weight, value_bias,
    out_weight, out_bias, attn_gain, attn_shift, mlp_gain, mlp_shift,
    up_weight, up_bias, down_weight, down_bias, cotangent,
):
    features = tokens.shape[1]
    width = query_weight.shape[1]
    hidden = up_weight.shape[1]
    dp, mp = lax.axis_size("dp"), lax.axis_size("mp")
    links = Links(dp, mp)
    dp_at, mp_at = lax.axis_index("dp"), lax.axis_index("mp")
    r = features // dp
    half = features // 2

    tok_p = links.send(tokens, links.c)
    mem_p = links.send(memory, links.c)
    cot_p = links.send(cotangent, links.c)
    (attn_own,) = call(
        pack_kernel, [((r, features), BF16)], query_weight, key_weight, value_weight, out_weight
    )
    (biases,) = call(
        bias_kernel, [((16, features), BF16)],
        query_bias.reshape(1, -1), value_bias.reshape(1, -1), up_bias.reshape(1, -1),
        after=(attn_own, tok_p, mem_p, cot_p),
    )

    low_d = links.low(down_weight.T, after=(biases,))
    quads_d = links.quads(low_d)
    rows_a, up_own = links.line(attn_own, up_weight, tail=biases, after=(low_d,))

    where = jnp.stack([dp_at // 2, dp_at % 2, mp_at, mp_at ^ 1, mp_at, mp_at ^ 2]).astype(jnp.int32)
    blank = jnp.zeros_like(attn_gain)
    vec = jnp.stack(
        [attn_gain, attn_shift, mlp_gain, mlp_shift, out_bias, down_bias] + [blank] * 10
    )
    x, xt, tok_r, cot_r, cot_t, mem_r, vec_r, hot, ok, unscaled = call(
        functools.partial(prep_kernel, dp // 2),
        [
            ((2, KEYS, features), BF16), ((features, 2 * KEYS), BF16),
            ((2 * TEXT, features), BF16), ((2 * TEXT, features), BF16), ((features, 2 * TEXT), BF16),
            ((SLOTS, features), BF16), ((16, features), F32), ((features, features), BF16),
            ((2, SLOTS, 128), F32), ((2, KEYS, features), BF16),
        ],
        where, tokens, tok_p, memory, mem_p, cotangent, cot_p, vec, patch_mask,
        smem=1, after=(rows_a,),
    )
    parts_a, token = links.square(rows_a, half, after=(ok,))
    (rows_u,) = links.line(up_own, ring=True, after=(token,))

    wq, wo, y, p, ctx, part, ub = attend_call(where, split_point, text_length, parts_a, x, ok, after=(rows_u,))
    part_in = links.send(part, links.c)
    parts_u, token = links.square(rows_u, half, after=(part,))
    (token,) = call(gate_kernel, [((8, 128), F32)], after=(token, *parts_u[3:]))

    quarter = ((half, hidden), BF16)
    eighth = ((half // 2, hidden), BF16)
    res, mid_t, hid, slope, d00, d01, d10, d11t, d11b = call(
        up_kernel,
        [
            ((2 * TEXT, features), F32), ((features, 2 * TEXT), BF16),
            ((2, 2 * TEXT, hidden), BF16), ((2, 2 * TEXT, hidden), BF16),
        ]
        + [quarter] * 3 + [eighth] * 2,
        part, part_in, tok_r, vec_r, cot_t, ub, *parts_u, after=(token,),
        scratch=[pltpu.VMEM((2 * TEXT, features), BF16), pltpu.VMEM((2, features, hidden), BF16)],
    )
    d_far = links.send(d11t, links.x), links.send(d11b, links.y)

    layer_o, mid_grad, up_bias_part, *u = call(
        down_kernel,
        [((TEXT, features), BF16), ((3, TEXT, features), BF16), ((2, hidden), F32)]
        + [quarter] * 4,
        *parts_u, hid, slope, mid_t, cot_r, *quads_d,
        scratch=[
            pltpu.VMEM((2, features, hidden), BF16), pltpu.VMEM((2, 2 * TEXT, hidden), BF16),
            pltpu.VMEM((2, features, hidden), BF16),
        ],
    )
    grad_in = links.send(mid_grad, links.c)
    d_y, d_x, token = links.meet((mid_grad,), d01, d10, *d_far)
    ring = links.depth == 4
    if ring:
        u_got = links.send(u[2], links.z(-1)), links.send(u[3], links.z(1))

    rg, ag_t, dy, back_o, back_p, sums = back_call(
        where, mid_grad, grad_in, res, cot_r, vec_r, wq, wo, y, p, unscaled, up_bias_part, after=(token,)
    )
    back_in = links.send(back_p, links.c)
    if ring:
        near, far = call(
            fold_kernel, [((half // 2, hidden), F32), ((half // 2, hidden), BF16)], d00, d_y, d_x, after=(dy,)
        )
        down = near, links.send(far, links.z(-2))
    else:
        near = links.home((), d00, d_y, d_x)[0]
        down = near, None
    a00, a01, a10, a11t, a11b, stack = call(
        weight_kernel,
        [((half, features), BF16)] * 3
        + [((half // 2 + 32, features), BF16), ((half // 2, features), BF16), ((16, features), F32)],
        xt, ag_t, dy, ctx, sums, back_in, hot, after=(near,),
    )
    a_far = links.send(a11t, links.x), links.send(a11b, links.y)
    layer_out, input_grad, memory_grad = call(
        last_kernel,
        [((TEXT, features), BF16), ((TEXT, features), F32), ((PATCHES, features), F32)],
        back_o, back_in, tok_r, mem_r, rg, res, layer_o, grad_in, vec_r, hot, after=(a00,),
    )
    token = input_grad
    if ring:
        token, low = call(
            pass_kernel, [(u[1].shape, BF16)] * 2, u[1], u_got[0], u[0], u_got[1], after=(input_grad,)
        )
        up = low, links.send(token, links.z(-1))
    else:
        up = links.halve(u), None
    a_y, a_x, stack = links.meet_with((token,), stack, a01, a10, *a_far)
    attn_parts, up_parts, down_parts = links.wind_up(stack, (a00, a_y, a_x), up, down)
    query_sum, key_sum, value_sum, out_sum, stack = call(
        finish_kernel,
        [((r, width), F32)] * 3 + [((width, r), F32), (stack.shape, F32)], *attn_parts,
    )

    at = dp_at * mp + mp_at
    few = features // (dp * mp)
    q_bias = jnp.concatenate([stack[8:12, 0:128], stack[8:12, 384:448]], axis=1).reshape(1, features)
    v_bias = jnp.concatenate([stack[8:12, 256:384], stack[8:12, 448:512]], axis=1).reshape(1, features)
    vectors = lax.dynamic_slice(jnp.concatenate([stack[0:6], q_bias, v_bias]), (0, at * few), (8, few))
    many = up_bias.shape[0] // dp
    up_bias_sum = lax.dynamic_slice(stack[12:16].reshape(-1), (at * many,), (many,))

    return (
        layer_out, input_grad, memory_grad,
        query_sum, key_sum, value_sum, out_sum, add_up(up_parts), add_up(down_parts).T,
        vectors[6], vectors[7], up_bias_sum,
        vectors[2], vectors[3], vectors[4], vectors[5], vectors[0], vectors[1],
    )


def solution(mesh):
    rows = P(AXES, None)
    flat = P(AXES)
    in_specs = (
        rows, rows, P("dp"), P("dp"), P("dp", None),
        P("dp", "mp"), P("mp"), P("dp", "mp"), P("dp", "mp"), P("mp"),
        P("mp", "dp"), P(), P(), P(), P(), P(),
        P("dp", "mp"), P("mp"), P("mp", "dp"), P(), rows,
    )
    out_specs = (
        rows, rows, rows,
        P("dp", "mp"), P("dp", "mp"), P("dp", "mp"), P("mp", "dp"), P("dp", "mp"), P("mp", "dp"),
    ) + (flat,) * 9
    return jax.shard_map(
        per_device, mesh=mesh, in_specs=in_specs, out_specs=out_specs, check_vma=False
    )
```

```python
import functools

import jax
import jax.numpy as jnp
from jax import lax
from jax.experimental import pallas as pl
from jax.experimental.pallas import tpu as pltpu
from jax.sharding import PartitionSpec as P

HEAD = 64
TEXT = 256
PATCHES = 196
SLOTS = 256
KEYS = SLOTS + TEXT
EPS = 1e-06
NEG = -1000000000.0
SCALE = HEAD ** (-0.5)
F32 = jnp.float32
BF16 = jnp.bfloat16
AXES = ("dp", "mp")

CUT = 384


def nn(a, b):
    return lax.dot_general(a, b, (((1,), (0,)), ((), ())), preferred_element_type=F32)


def nt(a, b):
    return lax.dot_general(a, b, (((1,), (1,)), ((), ())), preferred_element_type=F32)


def eye(n):
    rows = lax.broadcasted_iota(jnp.int32, (n, n), 0)
    cols = lax.broadcasted_iota(jnp.int32, (n, n), 1)
    return (rows == cols).astype(F32).astype(BF16)


def standard(matrix):
    average = jnp.mean(matrix, axis=-1, keepdims=True)
    centered = matrix - average
    inverse = lax.rsqrt(jnp.mean(centered * centered, axis=-1, keepdims=True) + EPS)
    return centered * inverse, inverse


def standard_back(normed, inverse, grad_out, gain):
    scaled = grad_out * gain
    return inverse * (
        scaled
        - jnp.mean(scaled, axis=-1, keepdims=True)
        - normed * jnp.mean(scaled * normed, axis=-1, keepdims=True)
    )


UNIT = 1e9
COST = {
    "prep_kernel": 8.0, "attend_kernel": 17.0, "up_kernel": 9.0, "down_kernel": 9.0,
    "gate_kernel": 30.0, "add_kernel": 30.0, "pass_kernel": 30.0, "add_bottom_kernel": 30.0, "fold_kernel": 30.0, "corner_kernel": 30.0, "cut_kernel": 30.0, "attend_back_kernel": 19.0, "weight_kernel": 6.0, "last_kernel": 6.0,
}


ROOM = {
    "pack_kernel": 56,    "prep_kernel": 24, "attend_kernel": 26, "up_kernel": 26, "down_kernel": 26,
    "attend_back_kernel": 26, "weight_kernel": 20, "last_kernel": 16,
}


def call(kernel, out_shapes, *args, scratch=(), smem=0, after=(), anywhere=False):
    name = getattr(kernel, "func", kernel).__name__
    waits = len(after)

    def body(*refs):
        return kernel(*refs[waits:])

    place = pl.BlockSpec(memory_space=pl.ANY if anywhere else pltpu.VMEM)
    return pl.pallas_call(
        body,
        out_shape=[jax.ShapeDtypeStruct(s, d) for s, d in out_shapes],
        in_specs=[pl.BlockSpec(memory_space=pl.ANY)] * waits
        + [pl.BlockSpec(memory_space=pltpu.SMEM)] * smem
        + [place] * (len(args) - smem),
        out_specs=[place] * len(out_shapes),
        scratch_shapes=list(scratch),
        compiler_params=pltpu.CompilerParams(vmem_limit_bytes=ROOM.get(name, 8) * 1024 * 1024),
        cost_estimate=pl.CostEstimate(
            flops=int(COST.get(name, 2.0) * UNIT), bytes_accessed=0, transcendentals=0
        ),
        name=name,
    )(*after, *args)


def pack_kernel(q, k, v, o, a_ref):
    ot = nt(eye(q.shape[0]), o[...]).astype(BF16)
    a_ref[:, 0:128] = q[:, 0:128]
    a_ref[:, 128:256] = k[:, 0:128]
    a_ref[:, 256:384] = v[:, 0:128]
    a_ref[:, 384:512] = jnp.concatenate([q[:, 128:192], v[:, 128:192]], axis=1)
    a_ref[:, 512:640] = jnp.concatenate([k[:, 128:192], ot[:, 128:192]], axis=1)
    a_ref[:, 640:768] = ot[:, 0:128]


def bias_kernel(qb, vb, ub, bias_ref):
    blank = jnp.zeros((1, 128), F32)
    qf, vf = qb[...].astype(F32), vb[...].astype(F32)
    row = jnp.concatenate(
        [qf[:, 0:128], blank, vf[:, 0:128], qf[:, 128:192], vf[:, 128:192], blank, blank], axis=1
    )
    rest = jnp.zeros((14, row.shape[1]), F32)
    bias_ref[...] = jnp.concatenate([row, ub[...].astype(F32), rest], axis=0).astype(BF16)


def join_kernel(count, *refs):
    extra = (len(refs) - count - 1) // 2
    out, first = refs[count + extra], 0
    for piece in refs[:count]:
        out[first : first + piece.shape[0], :] = piece[...]
        first += piece.shape[0]
    for src, dst in zip(refs[count : count + extra], refs[count + extra + 1 :]):
        dst[...] = src[...]


def cut_kernel(a, b, out_a, out_b):
    cut = out_a.shape[0]
    out_a[...] = a[0:cut, :]
    out_b[...] = b[cut : 2 * cut, :]


def gate_kernel(token):
    token[...] = jnp.zeros_like(token)


def add_kernel(top, far_top, bottom, far_bottom, out_top, out_bottom):
    cut = far_top.shape[0]
    out_top[0:cut, :] = (top[0:cut, :].astype(F32) + far_top[...].astype(F32)).astype(BF16)
    out_top[cut:, :] = top[cut:, :]
    out_bottom[0:cut, :] = bottom[0:cut, :]
    out_bottom[cut:, :] = (bottom[cut:, :].astype(F32) + far_bottom[...].astype(F32)).astype(BF16)


def add_bottom_kernel(bottom, far_bottom, out):
    cut = far_bottom.shape[0]
    out[0:cut, :] = bottom[0:cut, :]
    out[cut:, :] = (bottom[cut:, :].astype(F32) + far_bottom[...].astype(F32)).astype(BF16)


def add_top_kernel(vec, top, far_top, out, vec_out):
    half, more = top.shape[0], vec.shape[0]
    cut = half // 2
    out[0:cut, :] = (top[0:cut, :].astype(F32) + far_top[0:cut, :].astype(F32)).astype(BF16)
    out[cut:half, :] = top[cut:, :]
    sums = vec[...] + far_top[cut : cut + more, :].astype(F32)
    vec_out[...] = sums
    out[half : half + more, :] = sums.astype(BF16)


def pass_kernel(one, got_one, low, got_low, out, low_out):
    out[...] = (one[...].astype(F32) + got_one[...].astype(F32)).astype(BF16)
    low_out[...] = (low[...].astype(F32) + got_low[...].astype(F32)).astype(BF16)


def fold_kernel(*refs):
    total_kernel(3, *refs)


def total_kernel(count, *refs):
    rows = refs[count].shape[0]
    for k, dst in enumerate(refs[count:]):
        at = slice(k * rows, (k + 1) * rows)
        value = refs[0][at, :].astype(F32)
        for other in refs[1:count]:
            value += other[at, :].astype(F32)
        dst[...] = value.astype(dst.dtype)


def final_kernel(
    vec, g00, from_y, from_x, low, one, near, far,
    vec_out, own, send1, send2, send3, top, side, down_own,
):
    rows, more = own.shape[0], vec.shape[0]
    first = 4 * rows
    for k, dst in enumerate((own, send1, send2, send3)):
        at = slice(k * rows, (k + 1) * rows)
        value = g00[at, :].astype(F32) + from_y[at, :].astype(F32) + from_x[at, :].astype(F32)
        dst[0:rows, :] = value.astype(dst.dtype)
    sums = vec[...]
    sums += from_y[first : first + more, :].astype(F32)
    vec_out[...] = sums
    for dst in (send1, send2, send3):
        dst[rows : rows + more, :] = sums.astype(BF16)
    down = near[...] + far[...].astype(F32)
    down_own[...] = down[0:rows]
    send1[rows + more :, :] = down[rows:].astype(BF16)
    total = low[...].astype(F32) + one[...].astype(F32)
    top[...] = total[0 : 2 * rows]
    side[...] = total[2 * rows :].astype(BF16)


def corner_kernel(top, got, own, out):
    rows = own.shape[0]
    own[...] = top[0:rows, :] + got[0:rows, :].astype(F32)
    out[...] = (top[rows:, :] + got[rows:, :].astype(F32)).astype(BF16)


def finish_kernel(count, *refs):
    vec, parts, others = refs[0], refs[1:count], refs[count:-7]
    q, k, v, o, vec_out, up_out, down_out = refs[-7:]
    rows, more = parts[0].shape[0], vec.shape[0]
    total = parts[0][...]
    sums = vec[...]
    for part in parts[1:]:
        total += part[0:rows, :].astype(F32)
        sums += part[rows : rows + more, :].astype(F32)
    vec_out[...] = sums
    up_out[...] = others[0][...] + others[1][...].astype(F32)
    down = others[2][...]
    if len(parts) > 1:
        down += parts[1][rows + more :, :].astype(F32)
    down_out[...] = down
    q[...] = jnp.concatenate([total[:, 0:128], total[:, 384:448]], axis=1)
    k[...] = jnp.concatenate([total[:, 128:256], total[:, 512:576]], axis=1)
    v[...] = jnp.concatenate([total[:, 256:384], total[:, 448:512]], axis=1)
    out = jnp.concatenate([total[:, 640:768], total[:, 576:640]], axis=1)
    high = out.astype(BF16)
    low = (out - high.astype(F32)).astype(BF16)
    unit = eye(out.shape[1])
    o[...] = nt(unit, high) + nt(unit, low)


def place_of(depth, r, z, y, count):
    rel = lax.broadcasted_iota(jnp.int32, (count, 1), 0)
    half = count // 2
    ry = (rel >= half).astype(jnp.int32)
    rest = rel - ry * half
    rz = jnp.zeros_like(rel)
    for k in range(1, depth):
        rz += (rest >= k * r).astype(jnp.int32)
    az = z - rz
    az += depth * (az < 0).astype(jnp.int32)
    ay = y + ry - 2 * y * ry
    return az * (2 * r) + ay * r + rest - rz * r


def prep_kernel(
    depth, where, tok_o, tok_p, mem_o, mem_p, cot_o, cot_p, vec, patch,
    x_ref, xt_ref, tok_r, cot_r, cot_t, mem_r, vec_r, hot_ref, ok_ref, unscaled,
):
    features = tok_o.shape[1]
    lane = lax.broadcasted_iota(jnp.int32, (features, features), 1)
    place = place_of(depth, features // (2 * depth), where[0], where[1], features)
    hot_ref[...] = (lane == place).astype(F32).astype(BF16)
    gain = vec[0:1, :].astype(F32)
    shift = vec[1:2, :].astype(F32)
    vec_r[...] = nt(vec[...], hot_ref[...])
    rows = lax.broadcasted_iota(jnp.int32, (SLOTS, PATCHES), 0)
    cols = lax.broadcasted_iota(jnp.int32, (SLOTS, PATCHES), 1)
    columns = nt((rows == cols).astype(F32), (patch[...] > 0).astype(F32))
    which = lax.broadcasted_iota(jnp.int32, columns.shape, 1)
    for at in range(2):
        one = jnp.sum(jnp.where(which == where[2 + at], columns, 0.0), axis=1, keepdims=True)
        ok_ref[at] = jnp.broadcast_to(one, (SLOTS, 128))

    for at, (mem, tok) in enumerate(((mem_o, tok_o), (mem_p, tok_p))):
        normed, _ = standard(tok[...].astype(F32))
        low = (normed * gain + shift).astype(BF16)
        x_ref[at, SLOTS:KEYS, :] = nt(low, hot_ref[...]).astype(BF16)
        unscaled[at, SLOTS:KEYS, :] = nt(normed.astype(BF16), hot_ref[...]).astype(BF16)
        xt_ref[:, at * KEYS + SLOTS : (at + 1) * KEYS] = nt(hot_ref[...], low).astype(BF16)
        normed, _ = standard(mem[...].astype(F32))
        normed = jnp.concatenate([normed, jnp.zeros((SLOTS - PATCHES, features), F32)], axis=0)
        unscaled[at, 0:SLOTS, :] = nt(normed.astype(BF16), hot_ref[...]).astype(BF16)
        low = (normed * gain + shift).astype(BF16)
        x_ref[at, 0:SLOTS, :] = nt(low, hot_ref[...]).astype(BF16)
        xt_ref[:, at * KEYS : at * KEYS + SLOTS] = nt(hot_ref[...], low).astype(BF16)
    raw = jnp.concatenate([mem_o[...].astype(F32), jnp.zeros((SLOTS - PATCHES, features), F32)], axis=0)
    mem_r[...] = nt(raw.astype(BF16), hot_ref[...]).astype(BF16)
    for at, (tok, cot) in enumerate(((tok_o, cot_o), (tok_p, cot_p))):
        rows = slice(at * TEXT, (at + 1) * TEXT)
        tok_r[rows, :] = nt(tok[...], hot_ref[...]).astype(BF16)
        cot_r[rows, :] = nt(cot[...], hot_ref[...]).astype(BF16)
        cot_t[:, rows] = nt(hot_ref[...], cot[...]).astype(BF16)


def assemble(parts, w_ref):
    own, own_y, peer, far_top, far_bottom = parts
    half, cut = w_ref.shape[1] // 2, far_top.shape[0]
    w_ref[0, 0:half, :] = own[0:half, :]
    w_ref[0, half : 2 * half, :] = own_y[0:half, :]
    w_ref[1, 0:half, :] = peer[0:half, :]
    w_ref[1, half : half + cut, :] = far_top[...]
    w_ref[1, half + cut : 2 * half, :] = far_bottom[...]


def assemble_quads(pieces, w_ref):
    block = pieces[0].shape[0] // 4
    for k, piece in enumerate(pieces):
        for quarter in range(4):
            first = (quarter % 2) * 4 * block + k * block
            w_ref[quarter // 2, first : first + block, :] = piece[quarter * block : (quarter + 1) * block, :]


def head_lanes(m, head):
    first = m * 640
    if head < 2:
        return first, first + 128, first + 256
    return first + 384, first + 512, first + 384


def attend_kernel(
    where, split, length,
    own, own_y, peer, far_top, far_bottom, x_ref, ok_ref,
    wq_ref, wo_ref, y_ref, p_ref, ctx_ref, part_ref, up_ref, bias, factor,
):
    half, cut = wq_ref.shape[0] // 2, far_top.shape[0]
    for m, first, src, size in (
        (0, 0, own, half), (0, half, own_y, half), (1, 0, peer, half),
        (1, half, far_top, cut), (1, half + cut, far_bottom, cut),
    ):
        rows = slice(first, first + size)
        wq_ref[rows, m * 640 : (m + 1) * 640] = src[0:size, 0:640]
        wo_ref[rows, m * 128 : (m + 1) * 128] = src[0:size, 640:768]
        wo_ref[rows, 256 + m * 128 : 384 + m * 128] = src[0:size, 512:640]
    lane = lax.broadcasted_iota(jnp.int32, (1, 128), 1)
    one = jnp.ones((1, 128), F32)
    for m, src in enumerate((own, peer)):
        tail = src[half : half + 16, :].astype(F32)
        bias[0:1, m * 640 : (m + 1) * 640] = tail[0:1, 0:640]
        up_ref[m] = tail[1:2, :]
        for group, value in enumerate(
            (one * SCALE, one, one, jnp.where(lane < HEAD, SCALE, 1.0), jnp.where(lane < HEAD, 1.0, 0.0))
        ):
            first = m * 640 + group * 128
            factor[0:1, first : first + 128] = value
    for e in range(2):
        for first in range(0, 1280, 256):
            at = slice(first, first + 256)
            y = (nn(x_ref[e], wq_ref[:, at]) + bias[0:1, at]) * factor[0:1, at]
            y_ref[e, :, at] = y.astype(BF16)

    lane = lax.broadcasted_iota(jnp.int32, (TEXT, 128), 1)
    zero = jnp.zeros((TEXT, 128), BF16)
    unit = eye(128)
    unit_t = eye(TEXT)
    key_place = lax.broadcasted_iota(jnp.int32, (TEXT, TEXT), 0)
    query_place = lax.broadcasted_iota(jnp.int32, (TEXT, TEXT), 1)

    def step(e, carry):
        patch_ok = jnp.concatenate([ok_ref[e], ok_ref[e]], axis=1) > 0.0
        prefix, valid = split[where[2 + e]], length[where[2 + e]]
        text_ok = ((key_place < prefix) | (key_place <= query_place)) & (key_place < valid)
        for m in range(2):
            parts = []
            for head in range(3):
                qa, ka, va = head_lanes(m, head)
                low = head != 1
                q = jnp.where((lane < HEAD) if low else (lane >= HEAD), y_ref[e, SLOTS:KEYS, qa : qa + 128], zero)
                if head != 1:
                    vt_all = nt(unit, y_ref[e, :, va : va + 128]).astype(BF16)
                vt = vt_all[0:HEAD] if head == 0 else vt_all[HEAD:128]
                s_mem = jnp.where(patch_ok, nt(y_ref[e, 0:SLOTS, ka : ka + 128], q), NEG)
                s_text = jnp.where(text_ok, nt(y_ref[e, SLOTS:KEYS, ka : ka + 128], q), NEG)
                largest = jnp.maximum(
                    jnp.max(s_mem, axis=0, keepdims=True), jnp.max(s_text, axis=0, keepdims=True)
                )
                e_mem = jnp.exp(s_mem - largest)
                e_text = jnp.exp(s_text - largest)
                total = jnp.sum(e_mem, axis=0, keepdims=True) + jnp.sum(e_text, axis=0, keepdims=True)
                inverse = 1.0 / total
                p_mem = (e_mem * inverse).astype(BF16)
                p_text = (e_text * inverse).astype(BF16)
                p_ref[e, m * 3 + head, 0:SLOTS, :] = p_mem
                p_ref[e, m * 3 + head, SLOTS:KEYS, :] = p_text
                parts.append(nn(vt[:, 0:SLOTS], p_mem) + nn(vt[:, SLOTS:KEYS], p_text))
            c01t = jnp.concatenate([parts[0], parts[1]], axis=0).astype(BF16)
            c2t = jnp.concatenate([jnp.zeros((HEAD, TEXT), F32), parts[2]], axis=0).astype(BF16)
            ctx_ref[e, :, m * 128 : (m + 1) * 128] = nt(unit_t, c01t).astype(BF16)
            ctx_ref[e, :, 256 + m * 128 : 384 + m * 128] = nt(unit_t, c2t).astype(BF16)
        return carry

    lax.fori_loop(0, 2, step, 0, unroll=True)
    features = wo_ref.shape[0]
    ctx = ctx_ref[...].reshape(2 * TEXT, 512)
    for first in range(0, features, 256):
        at = slice(first, first + 256)
        part_ref[:, :, at] = nt(ctx, wo_ref[at, :]).astype(BF16).reshape(2, TEXT, 256)


def gelu_pair(v):
    c = 0.7978845608028654
    square = v * v
    t = jnp.tanh(c * v * (1.0 + 0.044715 * square))
    gelu = 0.5 * v * (1.0 + t)
    slope = 0.5 * (1.0 + t) + 0.5 * v * (1.0 - t * t) * (c * (1.0 + 3 * 0.044715 * square))
    return gelu, slope


def up_kernel(
    part, part_in, tok_r, vec_r, cot_t, bias, u0, u1, u2, u3, u4,
    res_ref, mid_t, hid_ref, slope_ref, g00, g01, g10, g11_top, g11_bottom, mid_ref, u_ref,
):
    half = g00.shape[0]
    assemble((u0, u1, u2, u3, u4), u_ref)
    for e in range(2):
        rows = slice(e * TEXT, (e + 1) * TEXT)
        res = (
            tok_r[rows, :].astype(F32)
            + (part[e].astype(F32) + part_in[1 - e].astype(F32))
            + vec_r[4:5, :]
        )
        res_ref[rows, :] = res
        normed, _ = standard(res)
        mid_ref[rows, :] = (normed * vec_r[2:3, :] + vec_r[3:4, :]).astype(BF16)
    mid_t[...] = nt(eye(mid_ref.shape[1]), mid_ref[...]).astype(BF16)
    wide = u_ref.shape[2]
    for m in range(2):
        for first in range(0, wide, 256):
            at = slice(first, first + 256)
            gelu, slope = gelu_pair(nn(mid_ref[...], u_ref[m, :, at]) + bias[m, :, at])
            hid_ref[m, :, at] = gelu.astype(BF16)
            slope_ref[m, :, at] = slope.astype(BF16)
    for dst, m, first in (
        (g11_top, 1, half), (g11_bottom, 1, half + half // 2), (g01, 0, half), (g10, 1, 0), (g00, 0, 0)
    ):
        for lanes in range(0, wide, 256):
            at = slice(lanes, lanes + 256)
            dst[:, at] = nn(cot_t[first : first + dst.shape[0], :], hid_ref[m, :, at]).astype(BF16)


def down_kernel(
    u0, u1, u2, u3, u4, hid_ref, slope_ref, mid_t, cot_r, w0, w1, w2, w3,
    out_o, grad_ref, bias_ref, g0, g1, g2, g3, d_ref, pre_ref, u_ref,
):
    half = g0.shape[0]
    block = half // 4
    assemble((u0, u1, u2, u3, u4), u_ref)
    assemble_quads((w0, w1, w2, w3), d_ref)
    wide = d_ref.shape[2]
    for m in range(2):
        for first in range(0, wide, 256):
            at = slice(first, first + 256)
            pre = (nn(cot_r[...], d_ref[m, :, at]) * slope_ref[m, :, at].astype(F32)).astype(BF16)
            pre_ref[m, :, at] = pre
            bias_ref[m : m + 1, at] = jnp.sum(pre.astype(F32), axis=0, keepdims=True)
    for first in range(0, cot_r.shape[1], 256):
        at = slice(first, first + 256)
        grad = (nt(pre_ref[0], u_ref[0, at, :]) + nt(pre_ref[1], u_ref[1, at, :])).astype(BF16)
        grad_ref[0, :, at] = grad[0:TEXT]
        grad_ref[1, :, at] = grad[TEXT:]
        out = (nt(hid_ref[0], d_ref[0, at, :]) + nt(hid_ref[1], d_ref[1, at, :])).astype(BF16)
        out_o[:, at] = out[0:TEXT]
        grad_ref[2, :, at] = out[TEXT:]
    for m in range(2):
        for ry in range(2):
            rows = slice((m * 2 + ry) * block, (m * 2 + ry + 1) * block)
            for first in range(0, wide, 256):
                at = slice(first, first + 256)
                grad = nn(mid_t[ry * half : (ry + 1) * half, :], pre_ref[m, :, at]).astype(BF16)
                for k, dst in enumerate((g0, g1, g2, g3)):
                    dst[rows, at] = grad[k * block : (k + 1) * block, :]


def attend_back_kernel(
    where, grad, grad_in, res_ref, cot_r, vec_r, wq_ref, wo_ref, y_ref, p_ref, unscaled, up_bias,
    rg_ref, agt_ref, dy_ref, back_o, back_p, sums, ag_ref, back_ref, dc_ref,
):
    lane = lax.broadcasted_iota(jnp.int32, (TEXT, 128), 1)
    row = lax.broadcasted_iota(jnp.int32, (128, TEXT), 0)
    zero = jnp.zeros((TEXT, 128), BF16)
    unit = eye(128)
    unit_t = eye(TEXT)
    for e in range(2):
        rows = slice(e * TEXT, (e + 1) * TEXT)
        mid_grad = grad[e].astype(F32) + grad_in[1 - e].astype(F32)
        normed, inverse = standard(res_ref[rows, :])
        cot = cot_r[rows, :].astype(F32)
        resid = cot + standard_back(normed, inverse, mid_grad, vec_r[2:3, :])
        low = resid.astype(BF16)
        ag_ref[rows, :] = low
        if e == 0:
            rg_ref[...] = resid
            sums[0:1, :] = jnp.sum(mid_grad * normed, axis=0, keepdims=True)
            sums[1:2, :] = jnp.sum(mid_grad, axis=0, keepdims=True)
            sums[2:3, :] = jnp.sum(low.astype(F32), axis=0, keepdims=True)
            sums[3:4, :] = jnp.sum(cot, axis=0, keepdims=True)
            sums[4:8, :] = jnp.zeros_like(sums[4:8, :])
    features = ag_ref.shape[1]
    agt_ref[...] = nt(eye(features), ag_ref[...]).astype(BF16)
    for first in range(0, 512, 256):
        at = slice(first, first + 256)
        dc_ref[:, at] = nn(ag_ref[...], wo_ref[:, at]).astype(BF16)

    def step(e, carry):
        rows = pl.ds(pl.multiple_of(e * TEXT, TEXT), TEXT)
        for m in range(2):
            dk, dv, dqt = [], [], []
            for head in range(3):
                qa, ka, va = head_lanes(m, head)
                low = lane < HEAD
                keep = low if head == 0 else ~low
                first = m * 128 if head < 2 else 256 + m * 128
                dc = jnp.where(keep, dc_ref[rows, first : first + 128], zero)
                q = jnp.where(~low if head == 1 else low, y_ref[e, SLOTS:KEYS, qa : qa + 128], zero)
                if head != 1:
                    kt_all = nt(unit, y_ref[e, :, ka : ka + 128]).astype(BF16)
                kt = kt_all[HEAD:128] if head == 1 else kt_all[0:HEAD]
                prob = p_ref[e, m * 3 + head]
                probs = prob.astype(F32)
                grad_p = nt(y_ref[e, :, va : va + 128], dc)
                dot = jnp.sum(probs * grad_p, axis=0, keepdims=True)
                score = (probs * (grad_p - dot)).astype(BF16)
                dk.append(nn(score, q))
                dv.append(nn(prob, dc))
                dqt.append(nn(kt, score))
            first = m * 640
            dv2 = dv[2].astype(BF16)
            dq01 = nt(unit_t, (jnp.concatenate([dqt[0], dqt[1]], axis=0) * SCALE).astype(BF16))
            dq2 = nt(
                unit_t,
                (jnp.concatenate([dqt[2], jnp.zeros((HEAD, TEXT), F32)], axis=0) * SCALE).astype(BF16),
            )
            dy_ref[e, 0:SLOTS, first : first + 128] = zero
            dy_ref[e, SLOTS:KEYS, first : first + 128] = dq01.astype(BF16)
            dy_ref[e, :, first + 128 : first + 256] = (dk[0] + dk[1]).astype(BF16)
            dy_ref[e, :, first + 256 : first + 384] = (dv[0] + dv[1]).astype(BF16)
            dy_ref[e, 0:SLOTS, first + 384 : first + 512] = dv2[0:SLOTS]
            dy_ref[e, SLOTS:KEYS, first + 384 : first + 512] = (dq2 + dv2[SLOTS:KEYS].astype(F32)).astype(BF16)
            dy_ref[e, :, first + 512 : first + 640] = dk[2].astype(BF16)
        return carry

    lax.fori_loop(0, 2, step, 0, unroll=True)
    for e in range(2):
        for first in range(0, features, 256):
            at = slice(first, first + 256)
            back_ref[e, :, at] = nt(dy_ref[e], wq_ref[at, :])
    bias = jnp.sum(dy_ref[0].astype(F32), axis=0, keepdims=True) + jnp.sum(
        dy_ref[1].astype(F32), axis=0, keepdims=True
    )
    back_o[...] = back_ref[0]
    back_p[0:KEYS, :] = back_ref[1].astype(BF16)
    for e in range(2):
        sums[4:5, :] += jnp.sum(back_ref[e] * unscaled[e].astype(F32), axis=0, keepdims=True)
        sums[5:6, :] += jnp.sum(back_ref[e], axis=0, keepdims=True)
    index = lax.broadcasted_iota(jnp.int32, (4, 1), 0)
    own, peer = index == where[4], index == where[5]
    sums[8:12, 0:640] = jnp.where(own, bias[:, 0:640], 0.0) + jnp.where(peer, bias[:, 640:1280], 0.0)
    sums[8:12, 640:768] = jnp.zeros((4, 128), F32)
    sums[12:16, :] = jnp.where(own, up_bias[0:1, :], 0.0) + jnp.where(peer, up_bias[1:2, :], 0.0)
    high = sums[...].astype(BF16)
    back_p[KEYS : KEYS + 16, :] = high
    back_p[KEYS + 16 : KEYS + 32, :] = (sums[...] - high.astype(F32)).astype(BF16)


def weight_kernel(
    xt_ref, agt_ref, dy_ref, ctx_ref, sums, back_in, hot_ref, g00, g01, g10, g11_top, g11_bottom, vec_ref,
):
    half = g00.shape[0]
    more = vec_ref.shape[0]
    vec = sums[...] + back_in[KEYS : KEYS + more, :].astype(F32) + back_in[KEYS + more :, :].astype(F32)
    vec_ref[...] = vec
    vec_ref[0:8, :] = restore(vec[0:8, :], hot_ref[...])
    cut = g11_bottom.shape[0]
    g11_top[cut : cut + more, :] = vec_ref[...].astype(BF16)
    dy = dy_ref[...].reshape(2 * KEYS, 1280)
    ctx = ctx_ref[...].reshape(2 * TEXT, 512)
    for ry in range(2):
        rows = slice(ry * half, (ry + 1) * half)
        out = [nn(agt_ref[rows, :], ctx[:, k * 256 : (k + 1) * 256]) for k in range(2)]

        def put(m, lanes, value):
            value = value.astype(BF16)
            if m == 0:
                (g00, g01)[ry][0:half, lanes] = value
            elif ry == 0:
                g10[0:half, lanes] = value
            else:
                g11_top[0:cut, lanes] = value[0:cut]
                g11_bottom[0:cut, lanes] = value[cut:]

        for chunk in range(5):
            grad = nn(xt_ref[rows, :], dy[:, chunk * 256 : (chunk + 1) * 256])
            for side in range(2):
                m, group = divmod(chunk * 2 + side, 5)
                value = grad[:, side * 128 : (side + 1) * 128]
                if group == 4:
                    value += out[1][:, m * 128 : (m + 1) * 128]
                put(m, slice(group * 128, (group + 1) * 128), value)
        for m in range(2):
            put(m, slice(640, 768), out[0][:, m * 128 : (m + 1) * 128])


def restore(v, hot):
    high = v.astype(BF16)
    low = (v - high.astype(F32)).astype(BF16)
    return nn(high, hot) + nn(low, hot)


def last_kernel(
    back_o, back_in, tok_r, mem_r, rg_ref, res_ref, out_o, out_in, vec_r, hot_ref,
    layer_ref, in_ref, mem_ref,
):
    hot = hot_ref[...]
    gain = vec_r[0:1, :]
    layer = (
        res_ref[0:TEXT, :] + (out_o[...].astype(F32) + out_in[2].astype(F32)) + vec_r[5:6, :]
    ).astype(BF16)
    layer_ref[...] = nn(layer, hot).astype(BF16)
    mem_back = back_o[0:SLOTS, :] + back_in[0:SLOTS, :].astype(F32)
    text_back = back_o[SLOTS:KEYS, :] + back_in[SLOTS:KEYS, :].astype(F32)
    normed, inverse = standard(tok_r[0:TEXT, :].astype(F32))
    in_ref[...] = restore(rg_ref[...] + standard_back(normed, inverse, text_back, gain), hot)
    normed, inverse = standard(mem_r[...].astype(F32))
    mem_ref[...] = restore(standard_back(normed, inverse, mem_back, gain), hot)[0:PATCHES, :]


def attend_call(where, split, length, parts, x, ok, after=()):
    features = x.shape[-1]
    return call(
        attend_kernel,
        [
            ((features, 1280), BF16), ((features, 512), BF16), ((2, KEYS, 1280), BF16), ((2, 6, KEYS, TEXT), BF16),
            ((2, TEXT, 512), BF16), ((2, TEXT, features), BF16), ((2, 1, features), F32),
        ],
        where, split, length, *parts, x, ok,
        smem=3, scratch=[pltpu.VMEM((8, 1280), F32), pltpu.VMEM((8, 1280), F32)], after=after,
    )


def back_call(where, grad, grad_in, res, cot_r, vec_r, wq, wo, y, p, unscaled, up_bias, after=()):
    features = res.shape[-1]
    return call(
        attend_back_kernel,
        [
            ((TEXT, features), F32), ((features, 2 * TEXT), BF16), ((2, KEYS, 1280), BF16),
            ((KEYS, features), F32), ((KEYS + 32, features), BF16), ((16, features), F32),
        ],
        where, grad, grad_in, res, cot_r, vec_r, wq, wo, y, p, unscaled, up_bias, smem=1, after=after,
        scratch=[
            pltpu.VMEM((2 * TEXT, features), BF16), pltpu.VMEM((2, KEYS, features), F32),
            pltpu.VMEM((2 * TEXT, 512), BF16),
        ],
    )


class Links:
    def __init__(self, dp, mp):
        self.dp, self.mp, self.depth = dp, mp, dp // 2
        self.x = self.pairs(lambda d, m: (d, m ^ 2))
        self.c = self.pairs(lambda d, m: (d, m ^ 1))
        self.y = self.pairs(lambda d, m: (d ^ 1, m))

    def pairs(self, to):
        out = []
        for d in range(self.dp):
            for m in range(self.mp):
                d2, m2 = to(d, m)
                out.append((d * self.mp + m, d2 * self.mp + m2))
        return out

    def z(self, k):
        return self.pairs(lambda d, m: ((((d // 2 + k) % self.depth) * 2 + d % 2), m))

    def send(self, a, pairs):
        return lax.ppermute(a, AXES, pairs)

    def line(self, shard, *others, tail=None, ring=False, after=()):
        more = [] if tail is None else [tail]
        if self.depth == 4:
            pieces = [shard]
            for k in range(1, 4):
                pieces.append(self.send(pieces[-1], self.z(1)) if ring else self.send(shard, self.z(k)))
            pieces += more
            return call(
                functools.partial(join_kernel, len(pieces)),
                [((sum(p.shape[0] for p in pieces), shard.shape[1]), BF16)] + [(o.shape, o.dtype) for o in others],
                *pieces, *others, after=after,
            )
        held = shard[None]
        step = 1
        while step < self.depth:
            held = jnp.concatenate([held, self.send(held, self.z(step))], axis=0)
            step *= 2
        return (jnp.concatenate([held.reshape(-1, shard.shape[1])] + more, axis=0),) + tuple(others)

    def square(self, rows, half, after=()):
        own_y, peer = self.send(rows, self.y), self.send(rows, self.x)
        top, bottom = call(cut_kernel, [((half // 2, rows.shape[1]), BF16)] * 2, own_y, peer, after=after)
        return [rows, own_y, peer, self.send(top, self.x), self.send(bottom, self.y)], bottom

    def low(self, shard, after=()):
        own_y, peer = self.send(shard, self.y), self.send(shard, self.x)
        return call(
            functools.partial(join_kernel, 4), [((4 * shard.shape[0], shard.shape[1]), shard.dtype)],
            shard, own_y, peer, self.send(own_y, self.x), after=after,
        )[0]

    def quads(self, low):
        pieces = [low]
        if self.depth == 4:
            for _ in range(3):
                pieces.append(self.send(pieces[-1], self.z(1)))
            return pieces
        held = low[None]
        step = 1
        while step < self.depth:
            held = jnp.concatenate([held, self.send(held, self.z(step))], axis=0)
            step *= 2
        r, lanes = low.shape[0] // 4, low.shape[1]
        whole = held.reshape(self.depth, 4, r, lanes).transpose(1, 0, 2, 3).reshape(4, 4, -1, lanes)
        return [whole[:, k].reshape(-1, lanes) for k in range(4)]

    def halve(self, pieces):
        lanes = pieces[0].shape[1]
        whole = jnp.stack([p.reshape(4, -1, lanes) for p in pieces], axis=1)
        whole = whole.reshape(4, self.depth, -1, lanes).transpose(1, 0, 2, 3).astype(F32)
        step = self.depth // 2
        while step >= 1:
            whole = whole[:step] + self.send(whole[step:].astype(BF16), self.z(-step)).astype(F32)
            step //= 2
        return whole.reshape(-1, lanes)

    def home(self, after, *parts):
        rows, lanes = parts[0].shape
        held = sum(p.astype(F32) for p in parts).reshape(self.depth, -1, lanes)
        step = self.depth // 2
        while step >= 1:
            held = held[:step] + self.send(held[step:].astype(BF16), self.z(-step)).astype(F32)
            step //= 2
        return [held[0]]

    def meet(self, after, g01, g10, far_top, far_bottom):
        to_y, to_x = call(
            add_kernel, [(g01.shape, BF16), (g10.shape, BF16)], g01, far_top, g10, far_bottom, after=after
        )
        return self.send(to_y, self.y), self.send(to_x, self.x), to_x

    def meet_with(self, after, vec, g01, g10, far_top, far_bottom):
        (to_x,) = call(add_bottom_kernel, [(g10.shape, BF16)], g10, far_bottom, after=after)
        to_y, vec = call(
            add_top_kernel, [((g01.shape[0] + vec.shape[0], g01.shape[1]), BF16), (vec.shape, F32)],
            vec, g01, far_top, after=(to_x,),
        )
        return self.send(to_y, self.y), self.send(to_x, self.x), vec

    def wind_up(self, vec, attn, up, down):
        (g00, from_y, from_x), (low, one), (near, far) = attn, up, down
        more, lanes = vec.shape
        r = low.shape[0] // 4
        if self.depth == 4:
            after = call(gate_kernel, [((8, 128), F32)], after=(one, far))
            vec, own, s1, s2, s3, top, side, down_own = call(
                final_kernel,
                [(vec.shape, F32), ((r, lanes), F32), ((2 * r + more, lanes), BF16)]
                + [((r + more, lanes), BF16)] * 2
                + [((2 * r, lanes), F32), ((2 * r, lanes), BF16), ((r, lanes), F32)],
                vec, g00, from_y, from_x, low, one, near, far, after=after,
            )
            got = [self.send(s, self.z(-k - 1)) for k, s in enumerate((s1, s2, s3))]
            attn_parts = [vec, own] + got
            down_parts = [down_own]
        else:
            rows = g00.shape[0]
            vec = vec + from_y[rows : rows + more].astype(F32)
            step = 1
            while step < self.depth:
                vec = vec + self.send(vec, self.z(step))
                step *= 2
            attn_parts = [vec] + self.home((), g00, from_y[:rows], from_x)
            down_parts = [near]
            total = low.astype(F32)
            top, side = total[: 2 * r], total[2 * r :].astype(BF16)
        up_own, out = call(
            corner_kernel, [((r, lanes), F32), ((r, lanes), BF16)], top, self.send(side, self.x)
        )
        return attn_parts, [up_own, self.send(out, self.y)], down_parts


def per_device(
    tokens, memory, split_point, text_length, patch_mask,
    query_weight, query_bias, key_weight, value_weight, value_bias,
    out_weight, out_bias, attn_gain, attn_shift, mlp_gain, mlp_shift,
    up_weight, up_bias, down_weight, down_bias, cotangent,
):
    features = tokens.shape[1]
    width = query_weight.shape[1]
    hidden = up_weight.shape[1]
    dp, mp = lax.axis_size("dp"), lax.axis_size("mp")
    links = Links(dp, mp)
    dp_at, mp_at = lax.axis_index("dp"), lax.axis_index("mp")
    r = features // dp
    half = features // 2

    tok_p = links.send(tokens, links.c)
    mem_p = links.send(memory, links.c)
    cot_p = links.send(cotangent, links.c)
    (attn_own,) = call(
        pack_kernel, [((r, features), BF16)], query_weight, key_weight, value_weight, out_weight
    )
    (biases,) = call(
        bias_kernel, [((16, features), BF16)],
        query_bias.reshape(1, -1), value_bias.reshape(1, -1), up_bias.reshape(1, -1),
        after=(attn_own, tok_p, mem_p, cot_p),
    )

    low_d = links.low(down_weight.T, after=(biases,))
    quads_d = links.quads(low_d)
    rows_a, up_own = links.line(attn_own, up_weight, tail=biases, after=(low_d,))

    where = jnp.stack([dp_at // 2, dp_at % 2, mp_at, mp_at ^ 1, mp_at, mp_at ^ 2]).astype(jnp.int32)
    blank = jnp.zeros_like(attn_gain)
    vec = jnp.stack(
        [attn_gain, attn_shift, mlp_gain, mlp_shift, out_bias, down_bias] + [blank] * 10
    )
    x, xt, tok_r, cot_r, cot_t, mem_r, vec_r, hot, ok, unscaled = call(
        functools.partial(prep_kernel, dp // 2),
        [
            ((2, KEYS, features), BF16), ((features, 2 * KEYS), BF16),
            ((2 * TEXT, features), BF16), ((2 * TEXT, features), BF16), ((features, 2 * TEXT), BF16),
            ((SLOTS, features), BF16), ((16, features), F32), ((features, features), BF16),
            ((2, SLOTS, 128), F32), ((2, KEYS, features), BF16),
        ],
        where, tokens, tok_p, memory, mem_p, cotangent, cot_p, vec, patch_mask,
        smem=1, after=(rows_a,),
    )
    parts_a, token = links.square(rows_a, half, after=(ok,))
    (rows_u,) = links.line(up_own, ring=True, after=(token,))

    wq, wo, y, p, ctx, part, ub = attend_call(where, split_point, text_length, parts_a, x, ok, after=(rows_u,))
    part_in = links.send(part, links.c)
    parts_u, token = links.square(rows_u, half, after=(part,))
    (token,) = call(gate_kernel, [((8, 128), F32)], after=(token, *parts_u[3:]))

    quarter = ((half, hidden), BF16)
    eighth = ((half // 2, hidden), BF16)
    res, mid_t, hid, slope, d00, d01, d10, d11t, d11b = call(
        up_kernel,
        [
            ((2 * TEXT, features), F32), ((features, 2 * TEXT), BF16),
            ((2, 2 * TEXT, hidden), BF16), ((2, 2 * TEXT, hidden), BF16),
        ]
        + [quarter] * 3 + [eighth] * 2,
        part, part_in, tok_r, vec_r, cot_t, ub, *parts_u, after=(token,),
        scratch=[pltpu.VMEM((2 * TEXT, features), BF16), pltpu.VMEM((2, features, hidden), BF16)],
    )
    d_far = links.send(d11t, links.x), links.send(d11b, links.y)

    layer_o, mid_grad, up_bias_part, *u = call(
        down_kernel,
        [((TEXT, features), BF16), ((3, TEXT, features), BF16), ((2, hidden), F32)]
        + [quarter] * 4,
        *parts_u, hid, slope, mid_t, cot_r, *quads_d,
        scratch=[
            pltpu.VMEM((2, features, hidden), BF16), pltpu.VMEM((2, 2 * TEXT, hidden), BF16),
            pltpu.VMEM((2, features, hidden), BF16),
        ],
    )
    grad_in = links.send(mid_grad, links.c)
    d_y, d_x, token = links.meet((mid_grad,), d01, d10, *d_far)
    ring = links.depth == 4
    if ring:
        u_got = links.send(u[2], links.z(-1)), links.send(u[3], links.z(1))

    rg, ag_t, dy, back_o, back_p, sums = back_call(
        where, mid_grad, grad_in, res, cot_r, vec_r, wq, wo, y, p, unscaled, up_bias_part, after=(token,)
    )
    back_in = links.send(back_p, links.c)
    if ring:
        near, far = call(
            fold_kernel, [((half // 2, hidden), F32), ((half // 2, hidden), BF16)], d00, d_y, d_x, after=(dy,)
        )
        down = near, links.send(far, links.z(-2))
    else:
        near = links.home((), d00, d_y, d_x)[0]
        down = near, None
    a00, a01, a10, a11t, a11b, stack = call(
        weight_kernel,
        [((half, features), BF16)] * 3
        + [((half // 2 + 16, features), BF16), ((half // 2, features), BF16), ((16, features), F32)],
        xt, ag_t, dy, ctx, sums, back_in, hot, after=(near,),
    )
    a_far = links.send(a11t, links.x), links.send(a11b, links.y)
    layer_out, input_grad, memory_grad = call(
        last_kernel,
        [((TEXT, features), BF16), ((TEXT, features), F32), ((PATCHES, features), F32)],
        back_o, back_in, tok_r, mem_r, rg, res, layer_o, grad_in, vec_r, hot, after=(a00,),
    )
    token = input_grad
    if ring:
        token, low = call(
            pass_kernel, [(u[1].shape, BF16)] * 2, u[1], u_got[0], u[0], u_got[1], after=(input_grad,)
        )
        up = low, links.send(token, links.z(-1))
    else:
        up = links.halve(u), None
    a_y, a_x, stack = links.meet_with((token,), stack, a01, a10, *a_far)
    attn_parts, up_parts, down_parts = links.wind_up(stack, (a00, a_y, a_x), up, down)
    query_sum, key_sum, value_sum, out_sum, stack, up_sum, down_sum = call(
        functools.partial(finish_kernel, len(attn_parts)),
        [((r, width), F32)] * 3 + [((width, r), F32), (stack.shape, F32)] + [((r, hidden), F32)] * 2,
        *attn_parts, *up_parts, *down_parts,
    )

    at = dp_at * mp + mp_at
    few = features // (dp * mp)
    q_bias = jnp.concatenate([stack[8:12, 0:128], stack[8:12, 384:448]], axis=1).reshape(1, features)
    v_bias = jnp.concatenate([stack[8:12, 256:384], stack[8:12, 448:512]], axis=1).reshape(1, features)
    vectors = lax.dynamic_slice(jnp.concatenate([stack[0:6], q_bias, v_bias]), (0, at * few), (8, few))
    many = up_bias.shape[0] // dp
    up_bias_sum = lax.dynamic_slice(stack[12:16].reshape(-1), (at * many,), (many,))

    return (
        layer_out, input_grad, memory_grad,
        query_sum, key_sum, value_sum, out_sum, up_sum, down_sum.T,
        vectors[6], vectors[7], up_bias_sum,
        vectors[2], vectors[3], vectors[4], vectors[5], vectors[0], vectors[1],
    )


def solution(mesh):
    rows = P(AXES, None)
    flat = P(AXES)
    in_specs = (
        rows, rows, P("dp"), P("dp"), P("dp", None),
        P("dp", "mp"), P("mp"), P("dp", "mp"), P("dp", "mp"), P("mp"),
        P("mp", "dp"), P(), P(), P(), P(), P(),
        P("dp", "mp"), P("mp"), P("mp", "dp"), P(), rows,
    )
    out_specs = (
        rows, rows, rows,
        P("dp", "mp"), P("dp", "mp"), P("dp", "mp"), P("mp", "dp"), P("dp", "mp"), P("mp", "dp"),
    ) + (flat,) * 9
    return jax.shard_map(
        per_device, mesh=mesh, in_specs=in_specs, out_specs=out_specs, check_vma=False
    )
```

```python
import functools

import jax
import jax.numpy as jnp
from jax import lax
from jax.experimental import pallas as pl
from jax.experimental.pallas import tpu as pltpu
from jax.sharding import PartitionSpec as P

HEAD = 64
TEXT = 256
PATCHES = 196
SLOTS = 256
KEYS = SLOTS + TEXT
EPS = 1e-06
NEG = -1000000000.0
SCALE = HEAD ** (-0.5)
F32 = jnp.float32
BF16 = jnp.bfloat16
AXES = ("dp", "mp")

CUT = 384


def nn(a, b):
    return lax.dot_general(a, b, (((1,), (0,)), ((), ())), preferred_element_type=F32)


def nt(a, b):
    return lax.dot_general(a, b, (((1,), (1,)), ((), ())), preferred_element_type=F32)


def eye(n):
    rows = lax.broadcasted_iota(jnp.int32, (n, n), 0)
    cols = lax.broadcasted_iota(jnp.int32, (n, n), 1)
    return (rows == cols).astype(F32).astype(BF16)


def standard(matrix):
    average = jnp.mean(matrix, axis=-1, keepdims=True)
    centered = matrix - average
    inverse = lax.rsqrt(jnp.mean(centered * centered, axis=-1, keepdims=True) + EPS)
    return centered * inverse, inverse


def standard_back(normed, inverse, grad_out, gain):
    scaled = grad_out * gain
    return inverse * (
        scaled
        - jnp.mean(scaled, axis=-1, keepdims=True)
        - normed * jnp.mean(scaled * normed, axis=-1, keepdims=True)
    )


UNIT = 1e9
COST = {
    "prep_kernel": 30.0, "attend_kernel": 17.0, "up_kernel": 9.0, "down_kernel": 9.0,
    "gate_kernel": 30.0, "add_kernel": 30.0, "pass_kernel": 30.0, "add_bottom_kernel": 30.0, "fold_kernel": 30.0, "corner_kernel": 30.0, "cut_kernel": 30.0, "attend_back_kernel": 19.0, "weight_kernel": 6.0, "last_kernel": 6.0,
}


ROOM = {
    "pack_kernel": 56,    "prep_kernel": 24, "attend_kernel": 26, "up_kernel": 26, "down_kernel": 26,
    "attend_back_kernel": 26, "weight_kernel": 20, "last_kernel": 16,
}


def call(kernel, out_shapes, *args, scratch=(), smem=0, after=(), anywhere=False):
    name = getattr(kernel, "func", kernel).__name__
    waits = len(after)

    def body(*refs):
        return kernel(*refs[waits:])

    place = pl.BlockSpec(memory_space=pl.ANY if anywhere else pltpu.VMEM)
    return pl.pallas_call(
        body,
        out_shape=[jax.ShapeDtypeStruct(s, d) for s, d in out_shapes],
        in_specs=[pl.BlockSpec(memory_space=pl.ANY)] * waits
        + [pl.BlockSpec(memory_space=pltpu.SMEM)] * smem
        + [place] * (len(args) - smem),
        out_specs=[place] * len(out_shapes),
        scratch_shapes=list(scratch),
        compiler_params=pltpu.CompilerParams(vmem_limit_bytes=ROOM.get(name, 8) * 1024 * 1024),
        cost_estimate=pl.CostEstimate(
            flops=int(COST.get(name, 2.0) * UNIT), bytes_accessed=0, transcendentals=0
        ),
        name=name,
    )(*after, *args)


def pack_kernel(q, k, v, o, a_ref):
    ot = nt(eye(q.shape[0]), o[...]).astype(BF16)
    a_ref[:, 0:128] = q[:, 0:128]
    a_ref[:, 128:256] = k[:, 0:128]
    a_ref[:, 256:384] = v[:, 0:128]
    a_ref[:, 384:512] = jnp.concatenate([q[:, 128:192], v[:, 128:192]], axis=1)
    a_ref[:, 512:640] = jnp.concatenate([k[:, 128:192], ot[:, 128:192]], axis=1)
    a_ref[:, 640:768] = ot[:, 0:128]


def bias_kernel(qb, vb, ub, bias_ref):
    blank = jnp.zeros((1, 128), F32)
    qf, vf = qb[...].astype(F32), vb[...].astype(F32)
    row = jnp.concatenate(
        [qf[:, 0:128], blank, vf[:, 0:128], qf[:, 128:192], vf[:, 128:192], blank, blank], axis=1
    )
    rest = jnp.zeros((14, row.shape[1]), F32)
    bias_ref[...] = jnp.concatenate([row, ub[...].astype(F32), rest], axis=0).astype(BF16)


def join_kernel(count, *refs):
    extra = (len(refs) - count - 1) // 2
    out, first = refs[count + extra], 0
    for piece in refs[:count]:
        out[first : first + piece.shape[0], :] = piece[...]
        first += piece.shape[0]
    for src, dst in zip(refs[count : count + extra], refs[count + extra + 1 :]):
        dst[...] = src[...]


def cut_kernel(a, b, out_a, out_b):
    cut = out_a.shape[0]
    out_a[...] = a[0:cut, :]
    out_b[...] = b[cut : 2 * cut, :]


def gate_kernel(token):
    token[...] = jnp.zeros_like(token)


def add_kernel(top, far_top, bottom, far_bottom, out_top, out_bottom):
    cut = far_top.shape[0]
    out_top[0:cut, :] = (top[0:cut, :].astype(F32) + far_top[...].astype(F32)).astype(BF16)
    out_top[cut:, :] = top[cut:, :]
    out_bottom[0:cut, :] = bottom[0:cut, :]
    out_bottom[cut:, :] = (bottom[cut:, :].astype(F32) + far_bottom[...].astype(F32)).astype(BF16)


def add_bottom_kernel(bottom, far_bottom, out):
    cut = far_bottom.shape[0]
    out[0:cut, :] = bottom[0:cut, :]
    out[cut:, :] = (bottom[cut:, :].astype(F32) + far_bottom[...].astype(F32)).astype(BF16)


def add_top_kernel(vec, top, far_top, out, vec_out):
    half, more = top.shape[0], vec.shape[0]
    cut = half // 2
    out[0:cut, :] = (top[0:cut, :].astype(F32) + far_top[0:cut, :].astype(F32)).astype(BF16)
    out[cut:half, :] = top[cut:, :]
    sums = vec[...] + far_top[cut : cut + more, :].astype(F32)
    vec_out[...] = sums
    out[half : half + more, :] = sums.astype(BF16)


def pass_kernel(one, got_one, low, got_low, out, low_out):
    out[...] = (one[...].astype(F32) + got_one[...].astype(F32)).astype(BF16)
    low_out[...] = (low[...].astype(F32) + got_low[...].astype(F32)).astype(BF16)


def fold_kernel(*refs):
    total_kernel(3, *refs)


def total_kernel(count, *refs):
    rows = refs[count].shape[0]
    for k, dst in enumerate(refs[count:]):
        at = slice(k * rows, (k + 1) * rows)
        value = refs[0][at, :].astype(F32)
        for other in refs[1:count]:
            value += other[at, :].astype(F32)
        dst[...] = value.astype(dst.dtype)


def final_kernel(
    vec, g00, from_y, from_x, low, one, near, far,
    vec_out, own, send1, send2, send3, top, side, down_own,
):
    rows, more = own.shape[0], vec.shape[0]
    first = 4 * rows
    for k, dst in enumerate((own, send1, send2, send3)):
        at = slice(k * rows, (k + 1) * rows)
        value = g00[at, :].astype(F32) + from_y[at, :].astype(F32) + from_x[at, :].astype(F32)
        dst[0:rows, :] = value.astype(dst.dtype)
    sums = vec[...]
    sums += from_y[first : first + more, :].astype(F32)
    vec_out[...] = sums
    for dst in (send1, send2, send3):
        dst[rows : rows + more, :] = sums.astype(BF16)
    down = near[...] + far[...].astype(F32)
    down_own[...] = down[0:rows]
    send1[rows + more :, :] = down[rows:].astype(BF16)
    total = low[...].astype(F32) + one[...].astype(F32)
    top[...] = total[0 : 2 * rows]
    side[...] = total[2 * rows :].astype(BF16)


def corner_kernel(top, got, own, out):
    rows = own.shape[0]
    own[...] = top[0:rows, :] + got[0:rows, :].astype(F32)
    out[...] = (top[rows:, :] + got[rows:, :].astype(F32)).astype(BF16)


def finish_kernel(count, *refs):
    vec, parts, others = refs[0], refs[1:count], refs[count:-7]
    q, k, v, o, vec_out, up_out, down_out = refs[-7:]
    rows, more = parts[0].shape[0], vec.shape[0]
    total = parts[0][...]
    sums = vec[...]
    for part in parts[1:]:
        total += part[0:rows, :].astype(F32)
        sums += part[rows : rows + more, :].astype(F32)
    vec_out[...] = sums
    up_out[...] = others[0][...] + others[1][...].astype(F32)
    down = others[2][...]
    if len(parts) > 1:
        down += parts[1][rows + more :, :].astype(F32)
    down_out[...] = down
    q[...] = jnp.concatenate([total[:, 0:128], total[:, 384:448]], axis=1)
    k[...] = jnp.concatenate([total[:, 128:256], total[:, 512:576]], axis=1)
    v[...] = jnp.concatenate([total[:, 256:384], total[:, 448:512]], axis=1)
    out = jnp.concatenate([total[:, 640:768], total[:, 576:640]], axis=1)
    high = out.astype(BF16)
    low = (out - high.astype(F32)).astype(BF16)
    unit = eye(out.shape[1])
    o[...] = nt(unit, high) + nt(unit, low)


def place_of(depth, r, z, y, count):
    rel = lax.broadcasted_iota(jnp.int32, (count, 1), 0)
    half = count // 2
    ry = (rel >= half).astype(jnp.int32)
    rest = rel - ry * half
    rz = jnp.zeros_like(rel)
    for k in range(1, depth):
        rz += (rest >= k * r).astype(jnp.int32)
    az = z - rz
    az += depth * (az < 0).astype(jnp.int32)
    ay = y + ry - 2 * y * ry
    return az * (2 * r) + ay * r + rest - rz * r


def prep_kernel(
    depth, where, tok_o, tok_p, mem_o, mem_p, cot_o, cot_p, vec, patch,
    x_ref, xt_ref, tok_r, cot_r, cot_t, mem_r, vec_r, hot_ref, ok_ref, unscaled,
):
    features = tok_o.shape[1]
    lane = lax.broadcasted_iota(jnp.int32, (features, features), 1)
    place = place_of(depth, features // (2 * depth), where[0], where[1], features)
    hot_ref[...] = (lane == place).astype(F32).astype(BF16)
    gain = vec[0:1, :].astype(F32)
    shift = vec[1:2, :].astype(F32)
    vec_r[...] = nt(vec[...], hot_ref[...])
    rows = lax.broadcasted_iota(jnp.int32, (SLOTS, PATCHES), 0)
    cols = lax.broadcasted_iota(jnp.int32, (SLOTS, PATCHES), 1)
    columns = nt((rows == cols).astype(F32), (patch[...] > 0).astype(F32))
    which = lax.broadcasted_iota(jnp.int32, columns.shape, 1)
    for at in range(2):
        one = jnp.sum(jnp.where(which == where[2 + at], columns, 0.0), axis=1, keepdims=True)
        ok_ref[at] = jnp.broadcast_to(one, (SLOTS, 128))

    for at, (mem, tok) in enumerate(((mem_o, tok_o), (mem_p, tok_p))):
        normed, _ = standard(tok[...].astype(F32))
        low = (normed * gain + shift).astype(BF16)
        x_ref[at, SLOTS:KEYS, :] = nt(low, hot_ref[...]).astype(BF16)
        unscaled[at, SLOTS:KEYS, :] = nt(normed.astype(BF16), hot_ref[...]).astype(BF16)
        xt_ref[:, at * KEYS + SLOTS : (at + 1) * KEYS] = nt(hot_ref[...], low).astype(BF16)
        normed, _ = standard(mem[...].astype(F32))
        normed = jnp.concatenate([normed, jnp.zeros((SLOTS - PATCHES, features), F32)], axis=0)
        unscaled[at, 0:SLOTS, :] = nt(normed.astype(BF16), hot_ref[...]).astype(BF16)
        low = (normed * gain + shift).astype(BF16)
        x_ref[at, 0:SLOTS, :] = nt(low, hot_ref[...]).astype(BF16)
        xt_ref[:, at * KEYS : at * KEYS + SLOTS] = nt(hot_ref[...], low).astype(BF16)
    raw = jnp.concatenate([mem_o[...].astype(F32), jnp.zeros((SLOTS - PATCHES, features), F32)], axis=0)
    mem_r[...] = nt(raw.astype(BF16), hot_ref[...]).astype(BF16)
    for at, (tok, cot) in enumerate(((tok_o, cot_o), (tok_p, cot_p))):
        rows = slice(at * TEXT, (at + 1) * TEXT)
        tok_r[rows, :] = nt(tok[...], hot_ref[...]).astype(BF16)
        cot_r[rows, :] = nt(cot[...], hot_ref[...]).astype(BF16)
        cot_t[:, rows] = nt(hot_ref[...], cot[...]).astype(BF16)


def assemble(parts, w_ref):
    own, own_y, peer, far_top, far_bottom = parts
    half, cut = w_ref.shape[1] // 2, far_top.shape[0]
    w_ref[0, 0:half, :] = own[0:half, :]
    w_ref[0, half : 2 * half, :] = own_y[0:half, :]
    w_ref[1, 0:half, :] = peer[0:half, :]
    w_ref[1, half : half + cut, :] = far_top[...]
    w_ref[1, half + cut : 2 * half, :] = far_bottom[...]


def assemble_quads(pieces, w_ref):
    block = pieces[0].shape[0] // 4
    for k, piece in enumerate(pieces):
        for quarter in range(4):
            first = (quarter % 2) * 4 * block + k * block
            w_ref[quarter // 2, first : first + block, :] = piece[quarter * block : (quarter + 1) * block, :]


def head_lanes(m, head):
    first = m * 640
    if head < 2:
        return first, first + 128, first + 256
    return first + 384, first + 512, first + 384


def attend_kernel(
    where, split, length,
    own, own_y, peer, far_top, far_bottom, x_ref, ok_ref,
    wq_ref, wo_ref, y_ref, p_ref, ctx_ref, part_ref, up_ref, bias, factor,
):
    half, cut = wq_ref.shape[0] // 2, far_top.shape[0]
    for m, first, src, size in (
        (0, 0, own, half), (0, half, own_y, half), (1, 0, peer, half),
        (1, half, far_top, cut), (1, half + cut, far_bottom, cut),
    ):
        rows = slice(first, first + size)
        wq_ref[rows, m * 640 : (m + 1) * 640] = src[0:size, 0:640]
        wo_ref[rows, m * 128 : (m + 1) * 128] = src[0:size, 640:768]
        wo_ref[rows, 256 + m * 128 : 384 + m * 128] = src[0:size, 512:640]
    lane = lax.broadcasted_iota(jnp.int32, (1, 128), 1)
    one = jnp.ones((1, 128), F32)
    for m, src in enumerate((own, peer)):
        tail = src[half : half + 16, :].astype(F32)
        bias[0:1, m * 640 : (m + 1) * 640] = tail[0:1, 0:640]
        up_ref[m] = tail[1:2, :]
        for group, value in enumerate(
            (one * SCALE, one, one, jnp.where(lane < HEAD, SCALE, 1.0), jnp.where(lane < HEAD, 1.0, 0.0))
        ):
            first = m * 640 + group * 128
            factor[0:1, first : first + 128] = value
    for e in range(2):
        for first in range(0, 1280, 256):
            at = slice(first, first + 256)
            y = (nn(x_ref[e], wq_ref[:, at]) + bias[0:1, at]) * factor[0:1, at]
            y_ref[e, :, at] = y.astype(BF16)

    lane = lax.broadcasted_iota(jnp.int32, (TEXT, 128), 1)
    zero = jnp.zeros((TEXT, 128), BF16)
    unit = eye(128)
    unit_t = eye(TEXT)
    key_place = lax.broadcasted_iota(jnp.int32, (TEXT, TEXT), 0)
    query_place = lax.broadcasted_iota(jnp.int32, (TEXT, TEXT), 1)

    def step(e, carry):
        patch_ok = jnp.concatenate([ok_ref[e], ok_ref[e]], axis=1) > 0.0
        prefix, valid = split[where[2 + e]], length[where[2 + e]]
        text_ok = ((key_place < prefix) | (key_place <= query_place)) & (key_place < valid)
        for m in range(2):
            parts = []
            for head in range(3):
                qa, ka, va = head_lanes(m, head)
                low = head != 1
                q = jnp.where((lane < HEAD) if low else (lane >= HEAD), y_ref[e, SLOTS:KEYS, qa : qa + 128], zero)
                if head != 1:
                    vt_all = nt(unit, y_ref[e, :, va : va + 128]).astype(BF16)
                vt = vt_all[0:HEAD] if head == 0 else vt_all[HEAD:128]
                s_mem = jnp.where(patch_ok, nt(y_ref[e, 0:SLOTS, ka : ka + 128], q), NEG)
                s_text = jnp.where(text_ok, nt(y_ref[e, SLOTS:KEYS, ka : ka + 128], q), NEG)
                largest = jnp.maximum(
                    jnp.max(s_mem, axis=0, keepdims=True), jnp.max(s_text, axis=0, keepdims=True)
                )
                e_mem = jnp.exp(s_mem - largest)
                e_text = jnp.exp(s_text - largest)
                total = jnp.sum(e_mem, axis=0, keepdims=True) + jnp.sum(e_text, axis=0, keepdims=True)
                inverse = 1.0 / total
                p_mem = (e_mem * inverse).astype(BF16)
                p_text = (e_text * inverse).astype(BF16)
                p_ref[e, m * 3 + head, 0:SLOTS, :] = p_mem
                p_ref[e, m * 3 + head, SLOTS:KEYS, :] = p_text
                parts.append(nn(vt[:, 0:SLOTS], p_mem) + nn(vt[:, SLOTS:KEYS], p_text))
            c01t = jnp.concatenate([parts[0], parts[1]], axis=0).astype(BF16)
            c2t = jnp.concatenate([jnp.zeros((HEAD, TEXT), F32), parts[2]], axis=0).astype(BF16)
            ctx_ref[e, :, m * 128 : (m + 1) * 128] = nt(unit_t, c01t).astype(BF16)
            ctx_ref[e, :, 256 + m * 128 : 384 + m * 128] = nt(unit_t, c2t).astype(BF16)
        return carry

    lax.fori_loop(0, 2, step, 0, unroll=True)
    features = wo_ref.shape[0]
    ctx = ctx_ref[...].reshape(2 * TEXT, 512)
    for first in range(0, features, 256):
        at = slice(first, first + 256)
        part_ref[:, :, at] = nt(ctx, wo_ref[at, :]).astype(BF16).reshape(2, TEXT, 256)


def gelu_pair(v):
    c = 0.7978845608028654
    square = v * v
    t = jnp.tanh(c * v * (1.0 + 0.044715 * square))
    gelu = 0.5 * v * (1.0 + t)
    slope = 0.5 * (1.0 + t) + 0.5 * v * (1.0 - t * t) * (c * (1.0 + 3 * 0.044715 * square))
    return gelu, slope


def up_kernel(
    part, part_in, tok_r, vec_r, cot_t, bias, u0, u1, u2, u3, u4,
    res_ref, mid_t, hid_ref, slope_ref, g00, g01, g10, g11_top, g11_bottom, mid_ref, u_ref,
):
    half = g00.shape[0]
    assemble((u0, u1, u2, u3, u4), u_ref)
    for e in range(2):
        rows = slice(e * TEXT, (e + 1) * TEXT)
        res = (
            tok_r[rows, :].astype(F32)
            + (part[e].astype(F32) + part_in[1 - e].astype(F32))
            + vec_r[4:5, :]
        )
        res_ref[rows, :] = res
        normed, _ = standard(res)
        mid_ref[rows, :] = (normed * vec_r[2:3, :] + vec_r[3:4, :]).astype(BF16)
    mid_t[...] = nt(eye(mid_ref.shape[1]), mid_ref[...]).astype(BF16)
    wide = u_ref.shape[2]
    for m in range(2):
        for first in range(0, wide, 256):
            at = slice(first, first + 256)
            gelu, slope = gelu_pair(nn(mid_ref[...], u_ref[m, :, at]) + bias[m, :, at])
            hid_ref[m, :, at] = gelu.astype(BF16)
            slope_ref[m, :, at] = slope.astype(BF16)
    for dst, m, first in (
        (g11_top, 1, half), (g11_bottom, 1, half + half // 2), (g01, 0, half), (g10, 1, 0), (g00, 0, 0)
    ):
        for lanes in range(0, wide, 256):
            at = slice(lanes, lanes + 256)
            dst[:, at] = nn(cot_t[first : first + dst.shape[0], :], hid_ref[m, :, at]).astype(BF16)


def down_kernel(
    u0, u1, u2, u3, u4, hid_ref, slope_ref, mid_t, cot_r, w0, w1, w2, w3,
    out_o, grad_ref, bias_ref, g0, g1, g2, g3, d_ref, pre_ref, u_ref,
):
    half = g0.shape[0]
    block = half // 4
    assemble((u0, u1, u2, u3, u4), u_ref)
    assemble_quads((w0, w1, w2, w3), d_ref)
    wide = d_ref.shape[2]
    for m in range(2):
        for first in range(0, wide, 256):
            at = slice(first, first + 256)
            pre = (nn(cot_r[...], d_ref[m, :, at]) * slope_ref[m, :, at].astype(F32)).astype(BF16)
            pre_ref[m, :, at] = pre
            bias_ref[m : m + 1, at] = jnp.sum(pre.astype(F32), axis=0, keepdims=True)
    for first in range(0, cot_r.shape[1], 256):
        at = slice(first, first + 256)
        grad = (nt(pre_ref[0], u_ref[0, at, :]) + nt(pre_ref[1], u_ref[1, at, :])).astype(BF16)
        grad_ref[0, :, at] = grad[0:TEXT]
        grad_ref[1, :, at] = grad[TEXT:]
        out = (nt(hid_ref[0], d_ref[0, at, :]) + nt(hid_ref[1], d_ref[1, at, :])).astype(BF16)
        out_o[:, at] = out[0:TEXT]
        grad_ref[2, :, at] = out[TEXT:]
    for m in range(2):
        for ry in range(2):
            rows = slice((m * 2 + ry) * block, (m * 2 + ry + 1) * block)
            for first in range(0, wide, 256):
                at = slice(first, first + 256)
                grad = nn(mid_t[ry * half : (ry + 1) * half, :], pre_ref[m, :, at]).astype(BF16)
                for k, dst in enumerate((g0, g1, g2, g3)):
                    dst[rows, at] = grad[k * block : (k + 1) * block, :]


def attend_back_kernel(
    where, grad, grad_in, res_ref, cot_r, vec_r, wq_ref, wo_ref, y_ref, p_ref, unscaled, up_bias,
    rg_ref, agt_ref, dy_ref, back_o, back_p, sums, ag_ref, back_ref, dc_ref,
):
    lane = lax.broadcasted_iota(jnp.int32, (TEXT, 128), 1)
    row = lax.broadcasted_iota(jnp.int32, (128, TEXT), 0)
    zero = jnp.zeros((TEXT, 128), BF16)
    unit = eye(128)
    unit_t = eye(TEXT)
    for e in range(2):
        rows = slice(e * TEXT, (e + 1) * TEXT)
        mid_grad = grad[e].astype(F32) + grad_in[1 - e].astype(F32)
        normed, inverse = standard(res_ref[rows, :])
        cot = cot_r[rows, :].astype(F32)
        resid = cot + standard_back(normed, inverse, mid_grad, vec_r[2:3, :])
        low = resid.astype(BF16)
        ag_ref[rows, :] = low
        if e == 0:
            rg_ref[...] = resid
            sums[0:1, :] = jnp.sum(mid_grad * normed, axis=0, keepdims=True)
            sums[1:2, :] = jnp.sum(mid_grad, axis=0, keepdims=True)
            sums[2:3, :] = jnp.sum(low.astype(F32), axis=0, keepdims=True)
            sums[3:4, :] = jnp.sum(cot, axis=0, keepdims=True)
            sums[4:8, :] = jnp.zeros_like(sums[4:8, :])
    features = ag_ref.shape[1]
    agt_ref[...] = nt(eye(features), ag_ref[...]).astype(BF16)
    for first in range(0, 512, 256):
        at = slice(first, first + 256)
        dc_ref[:, at] = nn(ag_ref[...], wo_ref[:, at]).astype(BF16)

    def step(e, carry):
        rows = pl.ds(pl.multiple_of(e * TEXT, TEXT), TEXT)
        for m in range(2):
            dk, dv, dqt = [], [], []
            for head in range(3):
                qa, ka, va = head_lanes(m, head)
                low = lane < HEAD
                keep = low if head == 0 else ~low
                first = m * 128 if head < 2 else 256 + m * 128
                dc = jnp.where(keep, dc_ref[rows, first : first + 128], zero)
                q = jnp.where(~low if head == 1 else low, y_ref[e, SLOTS:KEYS, qa : qa + 128], zero)
                if head != 1:
                    kt_all = nt(unit, y_ref[e, :, ka : ka + 128]).astype(BF16)
                kt = kt_all[HEAD:128] if head == 1 else kt_all[0:HEAD]
                prob = p_ref[e, m * 3 + head]
                probs = prob.astype(F32)
                grad_p = nt(y_ref[e, :, va : va + 128], dc)
                dot = jnp.sum(probs * grad_p, axis=0, keepdims=True)
                score = (probs * (grad_p - dot)).astype(BF16)
                dk.append(nn(score, q))
                dv.append(nn(prob, dc))
                dqt.append(nn(kt, score))
            first = m * 640
            dv2 = dv[2].astype(BF16)
            dq01 = nt(unit_t, (jnp.concatenate([dqt[0], dqt[1]], axis=0) * SCALE).astype(BF16))
            dq2 = nt(
                unit_t,
                (jnp.concatenate([dqt[2], jnp.zeros((HEAD, TEXT), F32)], axis=0) * SCALE).astype(BF16),
            )
            dy_ref[e, 0:SLOTS, first : first + 128] = zero
            dy_ref[e, SLOTS:KEYS, first : first + 128] = dq01.astype(BF16)
            dy_ref[e, :, first + 128 : first + 256] = (dk[0] + dk[1]).astype(BF16)
            dy_ref[e, :, first + 256 : first + 384] = (dv[0] + dv[1]).astype(BF16)
            dy_ref[e, 0:SLOTS, first + 384 : first + 512] = dv2[0:SLOTS]
            dy_ref[e, SLOTS:KEYS, first + 384 : first + 512] = (dq2 + dv2[SLOTS:KEYS].astype(F32)).astype(BF16)
            dy_ref[e, :, first + 512 : first + 640] = dk[2].astype(BF16)
        return carry

    lax.fori_loop(0, 2, step, 0, unroll=True)
    for e in range(2):
        for first in range(0, features, 256):
            at = slice(first, first + 256)
            back_ref[e, :, at] = nt(dy_ref[e], wq_ref[at, :])
    bias = jnp.sum(dy_ref[0].astype(F32), axis=0, keepdims=True) + jnp.sum(
        dy_ref[1].astype(F32), axis=0, keepdims=True
    )
    back_o[...] = back_ref[0]
    back_p[0:KEYS, :] = back_ref[1].astype(BF16)
    for e in range(2):
        sums[4:5, :] += jnp.sum(back_ref[e] * unscaled[e].astype(F32), axis=0, keepdims=True)
        sums[5:6, :] += jnp.sum(back_ref[e], axis=0, keepdims=True)
    index = lax.broadcasted_iota(jnp.int32, (4, 1), 0)
    own, peer = index == where[4], index == where[5]
    sums[8:12, 0:640] = jnp.where(own, bias[:, 0:640], 0.0) + jnp.where(peer, bias[:, 640:1280], 0.0)
    sums[8:12, 640:768] = jnp.zeros((4, 128), F32)
    sums[12:16, :] = jnp.where(own, up_bias[0:1, :], 0.0) + jnp.where(peer, up_bias[1:2, :], 0.0)
    high = sums[...].astype(BF16)
    back_p[KEYS : KEYS + 16, :] = high
    back_p[KEYS + 16 : KEYS + 32, :] = (sums[...] - high.astype(F32)).astype(BF16)


def weight_kernel(
    xt_ref, agt_ref, dy_ref, ctx_ref, sums, back_in, hot_ref, g00, g01, g10, g11_top, g11_bottom, vec_ref,
):
    half = g00.shape[0]
    more = vec_ref.shape[0]
    vec = sums[...] + back_in[KEYS : KEYS + more, :].astype(F32) + back_in[KEYS + more :, :].astype(F32)
    vec_ref[...] = vec
    vec_ref[0:8, :] = restore(vec[0:8, :], hot_ref[...])
    cut = g11_bottom.shape[0]
    g11_top[cut : cut + more, :] = vec_ref[...].astype(BF16)
    dy = dy_ref[...].reshape(2 * KEYS, 1280)
    ctx = ctx_ref[...].reshape(2 * TEXT, 512)
    for ry in range(2):
        rows = slice(ry * half, (ry + 1) * half)
        out = [nn(agt_ref[rows, :], ctx[:, k * 256 : (k + 1) * 256]) for k in range(2)]

        def put(m, lanes, value):
            value = value.astype(BF16)
            if m == 0:
                (g00, g01)[ry][0:half, lanes] = value
            elif ry == 0:
                g10[0:half, lanes] = value
            else:
                g11_top[0:cut, lanes] = value[0:cut]
                g11_bottom[0:cut, lanes] = value[cut:]

        for chunk in range(5):
            grad = nn(xt_ref[rows, :], dy[:, chunk * 256 : (chunk + 1) * 256])
            for side in range(2):
                m, group = divmod(chunk * 2 + side, 5)
                value = grad[:, side * 128 : (side + 1) * 128]
                if group == 4:
                    value += out[1][:, m * 128 : (m + 1) * 128]
                put(m, slice(group * 128, (group + 1) * 128), value)
        for m in range(2):
            put(m, slice(640, 768), out[0][:, m * 128 : (m + 1) * 128])


def restore(v, hot):
    high = v.astype(BF16)
    low = (v - high.astype(F32)).astype(BF16)
    return nn(high, hot) + nn(low, hot)


def last_kernel(
    back_o, back_in, tok_r, mem_r, rg_ref, res_ref, out_o, out_in, vec_r, hot_ref,
    layer_ref, in_ref, mem_ref,
):
    hot = hot_ref[...]
    gain = vec_r[0:1, :]
    layer = (
        res_ref[0:TEXT, :] + (out_o[...].astype(F32) + out_in[2].astype(F32)) + vec_r[5:6, :]
    ).astype(BF16)
    layer_ref[...] = nn(layer, hot).astype(BF16)
    mem_back = back_o[0:SLOTS, :] + back_in[0:SLOTS, :].astype(F32)
    text_back = back_o[SLOTS:KEYS, :] + back_in[SLOTS:KEYS, :].astype(F32)
    normed, inverse = standard(tok_r[0:TEXT, :].astype(F32))
    in_ref[...] = restore(rg_ref[...] + standard_back(normed, inverse, text_back, gain), hot)
    normed, inverse = standard(mem_r[...].astype(F32))
    mem_ref[...] = restore(standard_back(normed, inverse, mem_back, gain), hot)[0:PATCHES, :]


def attend_call(where, split, length, parts, x, ok, after=()):
    features = x.shape[-1]
    return call(
        attend_kernel,
        [
            ((features, 1280), BF16), ((features, 512), BF16), ((2, KEYS, 1280), BF16), ((2, 6, KEYS, TEXT), BF16),
            ((2, TEXT, 512), BF16), ((2, TEXT, features), BF16), ((2, 1, features), F32),
        ],
        where, split, length, *parts, x, ok,
        smem=3, scratch=[pltpu.VMEM((8, 1280), F32), pltpu.VMEM((8, 1280), F32)], after=after,
    )


def back_call(where, grad, grad_in, res, cot_r, vec_r, wq, wo, y, p, unscaled, up_bias, after=()):
    features = res.shape[-1]
    return call(
        attend_back_kernel,
        [
            ((TEXT, features), F32), ((features, 2 * TEXT), BF16), ((2, KEYS, 1280), BF16),
            ((KEYS, features), F32), ((KEYS + 32, features), BF16), ((16, features), F32),
        ],
        where, grad, grad_in, res, cot_r, vec_r, wq, wo, y, p, unscaled, up_bias, smem=1, after=after,
        scratch=[
            pltpu.VMEM((2 * TEXT, features), BF16), pltpu.VMEM((2, KEYS, features), F32),
            pltpu.VMEM((2 * TEXT, 512), BF16),
        ],
    )


class Links:
    def __init__(self, dp, mp):
        self.dp, self.mp, self.depth = dp, mp, dp // 2
        self.x = self.pairs(lambda d, m: (d, m ^ 2))
        self.c = self.pairs(lambda d, m: (d, m ^ 1))
        self.y = self.pairs(lambda d, m: (d ^ 1, m))

    def pairs(self, to):
        out = []
        for d in range(self.dp):
            for m in range(self.mp):
                d2, m2 = to(d, m)
                out.append((d * self.mp + m, d2 * self.mp + m2))
        return out

    def z(self, k):
        return self.pairs(lambda d, m: ((((d // 2 + k) % self.depth) * 2 + d % 2), m))

    def send(self, a, pairs):
        return lax.ppermute(a, AXES, pairs)

    def line(self, shard, *others, tail=None, ring=False, after=()):
        more = [] if tail is None else [tail]
        if self.depth == 4:
            pieces = [shard]
            for k in range(1, 4):
                pieces.append(self.send(pieces[-1], self.z(1)) if ring else self.send(shard, self.z(k)))
            pieces += more
            return call(
                functools.partial(join_kernel, len(pieces)),
                [((sum(p.shape[0] for p in pieces), shard.shape[1]), BF16)] + [(o.shape, o.dtype) for o in others],
                *pieces, *others, after=after,
            )
        held = shard[None]
        step = 1
        while step < self.depth:
            held = jnp.concatenate([held, self.send(held, self.z(step))], axis=0)
            step *= 2
        return (jnp.concatenate([held.reshape(-1, shard.shape[1])] + more, axis=0),) + tuple(others)

    def square(self, rows, half, after=()):
        own_y, peer = self.send(rows, self.y), self.send(rows, self.x)
        top, bottom = call(cut_kernel, [((half // 2, rows.shape[1]), BF16)] * 2, own_y, peer, after=after)
        return [rows, own_y, peer, self.send(top, self.x), self.send(bottom, self.y)], bottom

    def low(self, shard, after=()):
        own_y, peer = self.send(shard, self.y), self.send(shard, self.x)
        return call(
            functools.partial(join_kernel, 4), [((4 * shard.shape[0], shard.shape[1]), shard.dtype)],
            shard, own_y, peer, self.send(own_y, self.x), after=after,
        )[0]

    def quads(self, low):
        pieces = [low]
        if self.depth == 4:
            for _ in range(3):
                pieces.append(self.send(pieces[-1], self.z(1)))
            return pieces
        held = low[None]
        step = 1
        while step < self.depth:
            held = jnp.concatenate([held, self.send(held, self.z(step))], axis=0)
            step *= 2
        r, lanes = low.shape[0] // 4, low.shape[1]
        whole = held.reshape(self.depth, 4, r, lanes).transpose(1, 0, 2, 3).reshape(4, 4, -1, lanes)
        return [whole[:, k].reshape(-1, lanes) for k in range(4)]

    def halve(self, pieces):
        lanes = pieces[0].shape[1]
        whole = jnp.stack([p.reshape(4, -1, lanes) for p in pieces], axis=1)
        whole = whole.reshape(4, self.depth, -1, lanes).transpose(1, 0, 2, 3).astype(F32)
        step = self.depth // 2
        while step >= 1:
            whole = whole[:step] + self.send(whole[step:].astype(BF16), self.z(-step)).astype(F32)
            step //= 2
        return whole.reshape(-1, lanes)

    def home(self, after, *parts):
        rows, lanes = parts[0].shape
        held = sum(p.astype(F32) for p in parts).reshape(self.depth, -1, lanes)
        step = self.depth // 2
        while step >= 1:
            held = held[:step] + self.send(held[step:].astype(BF16), self.z(-step)).astype(F32)
            step //= 2
        return [held[0]]

    def meet(self, after, g01, g10, far_top, far_bottom):
        to_y, to_x = call(
            add_kernel, [(g01.shape, BF16), (g10.shape, BF16)], g01, far_top, g10, far_bottom, after=after
        )
        return self.send(to_y, self.y), self.send(to_x, self.x), to_x

    def meet_with(self, after, vec, g01, g10, far_top, far_bottom):
        (to_x,) = call(add_bottom_kernel, [(g10.shape, BF16)], g10, far_bottom, after=after)
        to_y, vec = call(
            add_top_kernel, [((g01.shape[0] + vec.shape[0], g01.shape[1]), BF16), (vec.shape, F32)],
            vec, g01, far_top, after=(to_x,),
        )
        return self.send(to_y, self.y), self.send(to_x, self.x), vec

    def wind_up(self, vec, attn, up, down):
        (g00, from_y, from_x), (low, one), (near, far) = attn, up, down
        more, lanes = vec.shape
        r = low.shape[0] // 4
        if self.depth == 4:
            after = call(gate_kernel, [((8, 128), F32)], after=(one, far))
            vec, own, s1, s2, s3, top, side, down_own = call(
                final_kernel,
                [(vec.shape, F32), ((r, lanes), F32), ((2 * r + more, lanes), BF16)]
                + [((r + more, lanes), BF16)] * 2
                + [((2 * r, lanes), F32), ((2 * r, lanes), BF16), ((r, lanes), F32)],
                vec, g00, from_y, from_x, low, one, near, far, after=after,
            )
            got = [self.send(s, self.z(-k - 1)) for k, s in enumerate((s1, s2, s3))]
            attn_parts = [vec, own] + got
            down_parts = [down_own]
        else:
            rows = g00.shape[0]
            vec = vec + from_y[rows : rows + more].astype(F32)
            step = 1
            while step < self.depth:
                vec = vec + self.send(vec, self.z(step))
                step *= 2
            attn_parts = [vec] + self.home((), g00, from_y[:rows], from_x)
            down_parts = [near]
            total = low.astype(F32)
            top, side = total[: 2 * r], total[2 * r :].astype(BF16)
        up_own, out = call(
            corner_kernel, [((r, lanes), F32), ((r, lanes), BF16)], top, self.send(side, self.x)
        )
        return attn_parts, [up_own, self.send(out, self.y)], down_parts


def per_device(
    tokens, memory, split_point, text_length, patch_mask,
    query_weight, query_bias, key_weight, value_weight, value_bias,
    out_weight, out_bias, attn_gain, attn_shift, mlp_gain, mlp_shift,
    up_weight, up_bias, down_weight, down_bias, cotangent,
):
    features = tokens.shape[1]
    width = query_weight.shape[1]
    hidden = up_weight.shape[1]
    dp, mp = lax.axis_size("dp"), lax.axis_size("mp")
    links = Links(dp, mp)
    dp_at, mp_at = lax.axis_index("dp"), lax.axis_index("mp")
    r = features // dp
    half = features // 2

    tok_p = links.send(tokens, links.c)
    mem_p = links.send(memory, links.c)
    cot_p = links.send(cotangent, links.c)
    (attn_own,) = call(
        pack_kernel, [((r, features), BF16)], query_weight, key_weight, value_weight, out_weight
    )
    (biases,) = call(
        bias_kernel, [((16, features), BF16)],
        query_bias.reshape(1, -1), value_bias.reshape(1, -1), up_bias.reshape(1, -1),
        after=(attn_own, tok_p, mem_p, cot_p),
    )

    low_d = links.low(down_weight.T, after=(biases,))
    quads_d = links.quads(low_d)
    rows_a, up_own = links.line(attn_own, up_weight, tail=biases, after=(low_d,))

    where = jnp.stack([dp_at // 2, dp_at % 2, mp_at, mp_at ^ 1, mp_at, mp_at ^ 2]).astype(jnp.int32)
    blank = jnp.zeros_like(attn_gain)
    vec = jnp.stack(
        [attn_gain, attn_shift, mlp_gain, mlp_shift, out_bias, down_bias] + [blank] * 10
    )
    x, xt, tok_r, cot_r, cot_t, mem_r, vec_r, hot, ok, unscaled = call(
        functools.partial(prep_kernel, dp // 2),
        [
            ((2, KEYS, features), BF16), ((features, 2 * KEYS), BF16),
            ((2 * TEXT, features), BF16), ((2 * TEXT, features), BF16), ((features, 2 * TEXT), BF16),
            ((SLOTS, features), BF16), ((16, features), F32), ((features, features), BF16),
            ((2, SLOTS, 128), F32), ((2, KEYS, features), BF16),
        ],
        where, tokens, tok_p, memory, mem_p, cotangent, cot_p, vec, patch_mask,
        smem=1, after=(rows_a,),
    )
    parts_a, token = links.square(rows_a, half, after=(ok,))
    (rows_u,) = links.line(up_own, ring=True, after=(token,))

    wq, wo, y, p, ctx, part, ub = attend_call(where, split_point, text_length, parts_a, x, ok, after=(rows_u,))
    part_in = links.send(part, links.c)
    parts_u, token = links.square(rows_u, half, after=(part,))
    (token,) = call(gate_kernel, [((8, 128), F32)], after=(token, *parts_u[3:]))

    quarter = ((half, hidden), BF16)
    eighth = ((half // 2, hidden), BF16)
    res, mid_t, hid, slope, d00, d01, d10, d11t, d11b = call(
        up_kernel,
        [
            ((2 * TEXT, features), F32), ((features, 2 * TEXT), BF16),
            ((2, 2 * TEXT, hidden), BF16), ((2, 2 * TEXT, hidden), BF16),
        ]
        + [quarter] * 3 + [eighth] * 2,
        part, part_in, tok_r, vec_r, cot_t, ub, *parts_u, after=(token,),
        scratch=[pltpu.VMEM((2 * TEXT, features), BF16), pltpu.VMEM((2, features, hidden), BF16)],
    )
    d_far = links.send(d11t, links.x), links.send(d11b, links.y)

    layer_o, mid_grad, up_bias_part, *u = call(
        down_kernel,
        [((TEXT, features), BF16), ((3, TEXT, features), BF16), ((2, hidden), F32)]
        + [quarter] * 4,
        *parts_u, hid, slope, mid_t, cot_r, *quads_d,
        scratch=[
            pltpu.VMEM((2, features, hidden), BF16), pltpu.VMEM((2, 2 * TEXT, hidden), BF16),
            pltpu.VMEM((2, features, hidden), BF16),
        ],
    )
    grad_in = links.send(mid_grad, links.c)
    d_y, d_x, token = links.meet((mid_grad,), d01, d10, *d_far)
    ring = links.depth == 4
    if ring:
        u_got = links.send(u[2], links.z(-1)), links.send(u[3], links.z(1))

    rg, ag_t, dy, back_o, back_p, sums = back_call(
        where, mid_grad, grad_in, res, cot_r, vec_r, wq, wo, y, p, unscaled, up_bias_part, after=(token,)
    )
    back_in = links.send(back_p, links.c)
    if ring:
        near, far = call(
            fold_kernel, [((half // 2, hidden), F32), ((half // 2, hidden), BF16)], d00, d_y, d_x, after=(dy,)
        )
        down = near, links.send(far, links.z(-2))
    else:
        near = links.home((), d00, d_y, d_x)[0]
        down = near, None
    a00, a01, a10, a11t, a11b, stack = call(
        weight_kernel,
        [((half, features), BF16)] * 3
        + [((half // 2 + 16, features), BF16), ((half // 2, features), BF16), ((16, features), F32)],
        xt, ag_t, dy, ctx, sums, back_in, hot, after=(near,),
    )
    a_far = links.send(a11t, links.x), links.send(a11b, links.y)
    layer_out, input_grad, memory_grad = call(
        last_kernel,
        [((TEXT, features), BF16), ((TEXT, features), F32), ((PATCHES, features), F32)],
        back_o, back_in, tok_r, mem_r, rg, res, layer_o, grad_in, vec_r, hot, after=(a00,),
    )
    token = input_grad
    if ring:
        token, low = call(
            pass_kernel, [(u[1].shape, BF16)] * 2, u[1], u_got[0], u[0], u_got[1], after=(input_grad,)
        )
        up = low, links.send(token, links.z(-1))
    else:
        up = links.halve(u), None
    a_y, a_x, stack = links.meet_with((token,), stack, a01, a10, *a_far)
    attn_parts, up_parts, down_parts = links.wind_up(stack, (a00, a_y, a_x), up, down)
    query_sum, key_sum, value_sum, out_sum, stack, up_sum, down_sum = call(
        functools.partial(finish_kernel, len(attn_parts)),
        [((r, width), F32)] * 3 + [((width, r), F32), (stack.shape, F32)] + [((r, hidden), F32)] * 2,
        *attn_parts, *up_parts, *down_parts,
    )

    at = dp_at * mp + mp_at
    few = features // (dp * mp)
    q_bias = jnp.concatenate([stack[8:12, 0:128], stack[8:12, 384:448]], axis=1).reshape(1, features)
    v_bias = jnp.concatenate([stack[8:12, 256:384], stack[8:12, 448:512]], axis=1).reshape(1, features)
    vectors = lax.dynamic_slice(jnp.concatenate([stack[0:6], q_bias, v_bias]), (0, at * few), (8, few))
    many = up_bias.shape[0] // dp
    up_bias_sum = lax.dynamic_slice(stack[12:16].reshape(-1), (at * many,), (many,))

    return (
        layer_out, input_grad, memory_grad,
        query_sum, key_sum, value_sum, out_sum, up_sum, down_sum.T,
        vectors[6], vectors[7], up_bias_sum,
        vectors[2], vectors[3], vectors[4], vectors[5], vectors[0], vectors[1],
    )


def solution(mesh):
    rows = P(AXES, None)
    flat = P(AXES)
    in_specs = (
        rows, rows, P("dp"), P("dp"), P("dp", None),
        P("dp", "mp"), P("mp"), P("dp", "mp"), P("dp", "mp"), P("mp"),
        P("mp", "dp"), P(), P(), P(), P(), P(),
        P("dp", "mp"), P("mp"), P("mp", "dp"), P(), rows,
    )
    out_specs = (
        rows, rows, rows,
        P("dp", "mp"), P("dp", "mp"), P("dp", "mp"), P("mp", "dp"), P("dp", "mp"), P("mp", "dp"),
    ) + (flat,) * 9
    return jax.shard_map(
        per_device, mesh=mesh, in_specs=in_specs, out_specs=out_specs, check_vma=False
    )
```
